32 devices in a mesh: lat: 4 (over y, core), lon: 8 (over z, x).
Axes of the slice: x: 2, y: 2, z: 4, core: 2. Of those that a mesh axis runs over, the one named last changes fastest.
Arguments:
- obs_feat: bfloat16 [64, 393216], P(None, ('lat', 'lon')), may hold values from -6 to 6
- obs_offset: bfloat16 [2, 393216], P(None, ('lat', 'lon')), may hold values from 0 to 8
- block_tile: int32 [3072, 1], P(('lat', 'lon')), may hold values from 0 to 31; in each aligned block of 96 rows (0 to 95, 96 to 191, ...) at most 6 rows name the same one
- block_patch: int32 [3072], P(('lat', 'lon')), may hold values from 0 to 23
- embed_weight: bfloat16 [64, 256], replicated, may hold values from -3 to 3
- grid_base: bfloat16 [128, 384, 256], P('lat', 'lon'), may hold values from -3 to 3
- norm_gain: float32 [256], replicated, may hold values from 0.5 to 1.5
- qkv_weight: bfloat16 [256, 768], replicated, may hold values from -1 to 1
- out_weight: bfloat16 [256, 256], replicated, may hold values from -0.375 to 0.375
- mlp_gain: float32 [256], replicated, may hold values from 0.5 to 1.5
- up_weight: bfloat16 [256, 1024], replicated, may hold values from -0.375 to 0.375
- down_weight: bfloat16 [1024, 256], replicated, may hold values from -0.1875 to 0.1875
- decode_weight: bfloat16 [256, 64], replicated, may hold values from -0.75 to 0.75
Outputs:
- grid_latent: bfloat16 [128, 384, 256], P('lat', 'lon')
- obs_out: bfloat16 [64, 393216], P(None, ('lat', 'lon'))
The draws below stay inside these ranges and needn't reach their ends.
Inputs may be any that keep to these rules, and one draw needn't show every extreme that they name: `block_tile`: among the 96 blocks of one device, at most 6 name the same tile, a bound that some block reaches.
All inputs are finite; a program needn't handle non-finite values.
Results may differ from the reference program's by a relative error of at most 0.015.
Values may be sent and summed in bfloat16 or wider, within the bound.
No kernel may reach another device: no remote copies, remote signals or barrier semaphores. Data moves between devices by JAX's collectives and lax.ppermute only.
A program may use at most 192 MiB of HBM per device.

```python
import math
import jax
import jax.numpy as jnp
import numpy as np
from jax import lax

C = 256
HEAD_DIM = 32
FF = 1024
FEAT = 64
WIN = 8
PATCH = 8
BLK = 128
TH = 32
TW = 48
BPD = 96
CAP = 6
PPT = 24
NBLK = 3072
OBS = 393216
NLAT = 128
NLON = 384
N_LAT = 4
N_LON = 8
DEVICES = 32


def draw_qkv_weight(key, part):
    sub_keys = jax.random.split(key, 1)
    base_draw = jax.random.truncated_normal(sub_keys[0], -3.0, 3.0, (C, 3 * C), jnp.float32) * C ** (-0.5)
    return jnp.clip(base_draw, -1.0, 1.0).astype(jnp.bfloat16)


def set_ends(values, stream_key, low, high):
    longest = values.shape.index(max(values.shape))
    spots = []
    for shift in (0, 1):
        where = [jax.random.randint(jax.random.fold_in(stream_key, axis), (), 0, length) for axis, length in enumerate(values.shape)]
        where[longest] = (where[longest] + shift) % values.shape[longest]
        spots.append(tuple(where))
    return values.at[spots[0]].set(low).at[spots[1]].set(high)


def level_of(rng, dims, cuts, smallest, high):
    level, own = 1.0, jax.random.fold_in(rng, 6)
    for dim, blocks in cuts:
        heights = jnp.exp(jax.random.uniform(jax.random.fold_in(own, dim), (blocks,), jnp.float32, smallest / len(cuts), high / len(cuts)))
        level = level * jnp.repeat(heights, dims[dim] // blocks).reshape([-1 if axis == dim else 1 for axis in range(len(dims))])
    return level


def assign_block(key, own, number, rows, number_of, top, most, skew):
    order = jax.random.permutation(key, number_of)
    crowded, usual = load_shares(number_of, rows * top, most, skew, True), load_shares(number_of, rows * top, most, skew, False)
    places = jnp.arange(number_of)

    def named(lengths, rotation):
        used = int((lengths > 0).sum())
        fixed = max(1, used // 4)
        passed = fixed + (places - fixed + rotation * (used - fixed)) % max(1, number_of - fixed)
        return jnp.zeros((number_of,), jnp.int32).at[order[jnp.where(places < fixed, places, passed)]].set(jnp.asarray(lengths, jnp.int32))

    lengths = jnp.where(number % 4 == 0, named(crowded, number // 4), named(usual, number - number // 4 - 1))
    mixed = jax.random.permutation(jax.random.fold_in(own, 3), number_of)
    donor, taker = mixed[0:number_of // 2 * 2:2], mixed[1:number_of // 2 * 2:2]
    slack = jnp.minimum(lengths[donor] - 1, most - lengths[taker]) // 2
    slack = jnp.where((donor == order[0]) | (taker == order[0]) | (lengths[taker] == 0), 0, jnp.maximum(slack, 0))
    passed = jax.random.randint(jax.random.fold_in(own, 4), (number_of // 2,), 0, 1 << 20) % (slack + 1)
    lengths = lengths.at[donor].add(-passed).at[taker].add(passed)
    items = jnp.searchsorted(jnp.cumsum(lengths), jnp.arange(rows * top), side="right").astype(jnp.int32)
    grid = items.reshape(top, rows).T
    grid = grid[jax.random.permutation(jax.random.fold_in(own, 1), rows)]
    rotation = jax.random.randint(jax.random.fold_in(own, 2), (rows, 1), 0, top)
    return jnp.take_along_axis(grid, (jnp.arange(top)[None, :] + rotation) % top, axis=1)


def load_shares(number_of, total, most, lean, full):
    weights = [(1 << 20) // math.isqrt(standing ** lean) + 1 for standing in range(1, number_of + 1)]
    largest = most if full else min(most, max(-(-total // number_of), total * weights[0] // sum(weights)))
    least = 1 if total - largest >= number_of - 1 else 0
    holding, surplus = [largest] + [least] * (number_of - 1), total - largest - least * (number_of - 1)
    while surplus > 0:
        free = [i for i in range(1, number_of) if holding[i] < largest] or [i for i in range(1, number_of) if holding[i] < most]
        mass, remaining = sum([weights[i] for i in free]), surplus
        for i in free:
            extra = min(most - holding[i], max(1, remaining * weights[i] // mass), surplus)
            holding[i] = holding[i] + extra
            surplus = surplus - extra
    return np.array(holding)


def centred(key, shape, deviation, most, cuts=(), kind=jnp.bfloat16):
    result = jax.random.normal(key, shape, jnp.float32) * deviation
    if len(cuts) > 0:
        result = level_of(key, shape, cuts, -0.22, 0.18) * result
    return jnp.clip(result, min=-most, max=most).astype(kind)


def setup_inputs(seed: int = 0) -> dict:
    streams_of = jax.random.split(jax.random.key(seed), 14)
    obs_feat = centred(streams_of[0], (FEAT, OBS), 1.0, 6.0, ((1, 32),))
    obs_offset = jnp.clip(8.0 * jax.random.uniform(streams_of[1], (2, OBS), jnp.float32) ** level_of(streams_of[1], (2, OBS), ((1, 32),), -0.2, 0.2), 0.0, 8.0).astype(jnp.bfloat16)
    block_tile_keys = jax.random.split(jax.random.fold_in(streams_of[2], 1), NBLK // BPD)
    block_tile_turns = jax.random.permutation(jax.random.fold_in(streams_of[2], 3), NBLK // BPD)
    block_tile = jax.vmap(lambda own, number: assign_block(jax.random.fold_in(streams_of[2], 2), own, number, BPD, DEVICES, 1, CAP, 2))(block_tile_keys, block_tile_turns).reshape((NBLK, 1))
    block_patch = set_ends(jax.random.randint(streams_of[3], (NBLK,), 0, PPT), jax.random.fold_in(streams_of[3], 1), 0, PPT - 1).astype(jnp.int32)
    embed_weight = centred(streams_of[4], (FEAT, C), 0.5, 3.0)
    grid_base = centred(streams_of[5], (NLAT, NLON, C), 0.5, 3.0, ((0, 4), (1, 8)))
    norm_gain = jnp.clip(1.0 + 0.1 * jax.random.normal(streams_of[6], (C,), jnp.float32), 0.5, 1.5)
    qkv_weight = draw_qkv_weight(jax.random.fold_in(streams_of[13], 71), 0)
    out_weight = centred(streams_of[8], (C, C), C ** -0.5, 0.375)
    mlp_gain = jnp.clip(1.0 + 0.1 * jax.random.normal(streams_of[9], (C,), jnp.float32), 0.5, 1.5)
    up_weight = centred(streams_of[10], (C, FF), C ** -0.5, 0.375)
    down_weight = centred(streams_of[11], (FF, C), FF ** -0.5, 0.1875)
    decode_weight = centred(streams_of[12], (C, FEAT), (C // 4) ** -0.5, 0.75)
    return {"obs_feat": obs_feat, "obs_offset": obs_offset, "block_tile": block_tile, "block_patch": block_patch, "embed_weight": embed_weight, "grid_base": grid_base, "norm_gain": norm_gain, "qkv_weight": qkv_weight, "out_weight": out_weight, "mlp_gain": mlp_gain, "up_weight": up_weight, "down_weight": down_weight, "decode_weight": decode_weight}


epsilon = 1e-05
spread_coef = 0.5

def normalize(values, gain_row):
    center = lax.optimization_barrier(jnp.mean(values, axis=-1, keepdims=True))
    centered = values - center
    variance = lax.optimization_barrier(jnp.mean(centered * centered, axis=-1, keepdims=True))
    return centered * lax.rsqrt(variance + epsilon) * gain_row

def patch_weights(offsets):
    cell_ids = jnp.arange(PATCH * PATCH, dtype=jnp.int32)
    row_center = (cell_ids // PATCH).astype(jnp.float32) + 0.5
    col_center = (cell_ids % PATCH).astype(jnp.float32) + 0.5
    row_gap = row_center[:, None] - offsets[..., 0:1, :]
    col_gap = col_center[:, None] - offsets[..., 1:2, :]
    return jnp.exp(-spread_coef * (row_gap * row_gap + col_gap * col_gap)).astype(jnp.bfloat16)

def reference(obs_feat, obs_offset, block_tile, block_patch, embed_weight, grid_base, norm_gain, qkv_weight, out_weight, mlp_gain, up_weight, down_weight, decode_weight):
    lat_cells = TH * N_LAT
    lon_cells = TW * N_LON
    device_count = N_LAT * N_LON
    patch_cols = TW // PATCH
    grid_patch_rows = lat_cells // PATCH
    grid_patch_cols = lon_cells // PATCH
    patch_total = grid_patch_rows * grid_patch_cols
    tile_ids = block_tile[:, 0]
    patch_row = tile_ids // N_LON * (TH // PATCH) + block_patch // patch_cols
    patch_col = tile_ids % N_LON * patch_cols + block_patch % patch_cols
    patch_index = (patch_row * grid_patch_cols + patch_col).astype(jnp.int32)
    feat_groups = obs_feat.reshape(FEAT, device_count, BPD, BLK).transpose(1, 2, 0, 3)
    offset_groups = obs_offset.astype(jnp.float32).reshape(2, device_count, BPD, BLK).transpose(1, 2, 0, 3)

    def encode_group(args):
        feat_part, offset_part = args
        weights_f = patch_weights(offset_part).astype(jnp.float32)
        sums = jnp.einsum('bco,bfo->bcf', weights_f, feat_part.astype(jnp.float32))
        return (sums, lax.optimization_barrier(jnp.sum(weights_f, axis=2)))
    block_sums, block_mass = lax.map(encode_group, (feat_groups, offset_groups))
    block_sums = block_sums.reshape(device_count * BPD, PATCH * PATCH, FEAT)
    block_mass = block_mass.reshape(device_count * BPD, PATCH * PATCH)
    patch_sums = jax.ops.segment_sum(block_sums, patch_index, num_segments=patch_total)
    patch_mass = jax.ops.segment_sum(block_mass, patch_index, num_segments=patch_total)
    encoded = (patch_sums / (1.0 + patch_mass[:, :, None])).astype(jnp.bfloat16)
    encoded = encoded.reshape(grid_patch_rows, grid_patch_cols, PATCH, PATCH, FEAT).transpose(0, 2, 1, 3, 4).reshape(lat_cells * lon_cells, FEAT)
    lifted = jnp.dot(encoded, embed_weight, preferred_element_type=jnp.float32)
    grid_start = (grid_base.reshape(-1, C).astype(jnp.float32) + lifted).astype(jnp.bfloat16).reshape(lat_cells, lon_cells, C)
    margin = WIN // 2
    rolled = jnp.roll(grid_start, (-margin, -margin), axis=(0, 1))
    head_count = C // HEAD_DIM
    win_cols = lon_cells // WIN
    token_row = jnp.arange(WIN * WIN, dtype=jnp.int32) // WIN

    def attend(args):
        row_block, block_number = args
        normed = normalize(row_block.astype(jnp.float32), norm_gain).astype(jnp.bfloat16)
        packed = jnp.dot(normed.reshape(-1, C), qkv_weight, preferred_element_type=jnp.float32).astype(jnp.bfloat16)
        windows = packed.reshape(WIN, win_cols, WIN, 3, head_count, HEAD_DIM).transpose(1, 0, 2, 3, 4, 5)
        windows = windows.reshape(win_cols, WIN * WIN, 3, head_count, HEAD_DIM).astype(jnp.float32)
        global_row = block_number * WIN + token_row
        wrapped = (global_row >= lat_cells - margin).astype(jnp.int32)
        same_side = wrapped[:, None] == wrapped[None, :]
        scores = jnp.einsum('wqhd,wkhd->whqk', windows[:, :, 0], windows[:, :, 1]) * HEAD_DIM ** (-0.5)
        scores = jnp.where(same_side[None, None, :, :], scores, -1e+30)
        row_top = lax.optimization_barrier(jnp.max(scores, axis=-1, keepdims=True))
        raised = jnp.exp(scores - row_top)
        attn_probs = (raised / lax.optimization_barrier(jnp.sum(raised, axis=-1, keepdims=True))).astype(jnp.bfloat16)
        attended = jnp.einsum('whqk,wkhd->wqhd', attn_probs.astype(jnp.float32), windows[:, :, 2]).astype(jnp.bfloat16)
        return attended.reshape(win_cols, WIN, WIN, C).transpose(1, 0, 2, 3).reshape(WIN, lon_cells, C)
    attended = lax.map(attend, (rolled.reshape(lat_cells // WIN, WIN, lon_cells, C), jnp.arange(lat_cells // WIN, dtype=jnp.int32)))
    attended = jnp.roll(attended.reshape(lat_cells, lon_cells, C), (margin, margin), axis=(0, 1))

    def finish(args):
        start_rows, attended_rows = args
        residual = start_rows.reshape(-1, C).astype(jnp.float32) + jnp.dot(attended_rows.reshape(-1, C), out_weight, preferred_element_type=jnp.float32)
        normed_mlp = normalize(residual, mlp_gain).astype(jnp.bfloat16)
        hidden = jax.nn.gelu(jnp.dot(normed_mlp, up_weight, preferred_element_type=jnp.float32)).astype(jnp.bfloat16)
        latent_rows = residual + jnp.dot(hidden, down_weight, preferred_element_type=jnp.float32)
        return latent_rows.astype(jnp.bfloat16).reshape(WIN, lon_cells, C)
    grid_latent = lax.map(finish, (grid_start.reshape(lat_cells // WIN, WIN, lon_cells, C), attended.reshape(lat_cells // WIN, WIN, lon_cells, C)))
    grid_latent = grid_latent.reshape(lat_cells, lon_cells, C)
    projected = jnp.dot(grid_latent.reshape(-1, C), decode_weight, preferred_element_type=jnp.float32).astype(jnp.bfloat16)
    patch_values = projected.reshape(grid_patch_rows, PATCH, grid_patch_cols, PATCH, FEAT).transpose(0, 2, 1, 3, 4).reshape(patch_total, PATCH * PATCH, FEAT)

    def decode_group(args):
        offset_part, index_part = args
        weights_f = patch_weights(offset_part).astype(jnp.float32)
        values_f = patch_values[index_part].astype(jnp.float32)
        numerator = jnp.einsum('bco,bcf->bfo', weights_f, values_f)
        denominator = lax.optimization_barrier(jnp.sum(weights_f, axis=1))
        return (numerator / denominator[:, None, :]).astype(jnp.bfloat16)
    decoded = lax.map(decode_group, (offset_groups, patch_index.reshape(device_count, BPD)))
    obs_out = decoded.transpose(2, 0, 1, 3).reshape(FEAT, device_count * BPD * BLK)
    return (grid_latent, obs_out)
```

```python
import jax
import jax.numpy as jnp
from jax import lax
from jax.experimental import pallas as pl
from jax.experimental.pallas import tpu as pltpu
from jax.sharding import PartitionSpec as P

HEAD_DIM = 32
WIN = 8
PATCH = 8
BLK = 128
CELLS = PATCH * PATCH
LANES = 2 * CELLS

epsilon = 1e-05
spread_coef = 0.5

NT = (((1,), (1,)), ((), ()))
TN = (((0,), (0,)), ((), ()))


def params(**extra):
    return pltpu.CompilerParams(vmem_limit_bytes=56 * 1024 * 1024, **extra)


def vmem():
    return pl.BlockSpec(memory_space=pltpu.VMEM)


def smem():
    return pl.BlockSpec(memory_space=pltpu.SMEM)


def normalize(values, gain_row):
    center = jnp.mean(values, axis=-1, keepdims=True)
    centered = values - center
    variance = jnp.mean(centered * centered, axis=-1, keepdims=True)
    return centered * lax.rsqrt(variance + epsilon) * gain_row


def block_weights(offsets):
    axis_id = lax.broadcasted_iota(jnp.int32, (PATCH, BLK), 0).astype(jnp.float32) + 0.5
    row_gap = axis_id - offsets[0:1]
    col_gap = axis_id - offsets[1:2]
    row_gap = row_gap * row_gap
    col_gap = col_gap * col_gap
    total = row_gap[:, None, :] + col_gap[None, :, :]
    return jnp.exp(-spread_coef * total).reshape(CELLS, BLK).astype(jnp.bfloat16)


def meta_rows(pairs):
    return -(-3 * pairs // 16) * 16


def encode_blocks(capacity, devices, tile_ref, patch_ref, feat_ref, offset_ref, send_ref, slot_ref, count_ref):
    blocks = feat_ref.shape[1] // BLK
    feat_width = feat_ref.shape[0]
    pairs = capacity // 2
    meta = meta_rows(pairs)
    chunk = pairs * feat_width + meta
    send_ref[...] = jnp.zeros_like(send_ref)

    def clear(t, _):
        count_ref[t] = 0
        return 0

    lax.fori_loop(0, devices, clear, 0)
    lane_half = lax.broadcasted_iota(jnp.int32, (feat_width, LANES), 1) // CELLS
    meta_half = lax.broadcasted_iota(jnp.int32, (meta, LANES), 1) // CELLS
    meta_row = lax.broadcasted_iota(jnp.int32, (meta, LANES), 0)
    ones = jnp.ones((16, BLK), jnp.bfloat16)

    def one(b):
        tile = tile_ref[b]
        rank = count_ref[tile]
        count_ref[tile] = rank + 1
        slot_ref[b] = tile * capacity + rank
        pair = rank // 2
        half = rank % 2
        col = pl.multiple_of(b * BLK, BLK)
        feat = jnp.concatenate([feat_ref[:, pl.ds(col, BLK)], ones], axis=0)
        weights = block_weights(offset_ref[:, pl.ds(col, BLK)].astype(jnp.float32))
        twice = jnp.concatenate([weights, weights], axis=0)
        sums = lax.dot_general(feat, twice, NT, preferred_element_type=jnp.float32)
        row = pl.multiple_of(tile * chunk + pair * feat_width, 16)
        old = send_ref[pl.ds(row, feat_width), :].astype(jnp.float32)
        send_ref[pl.ds(row, feat_width), :] = jnp.where(
            lane_half == half, sums[:feat_width], old
        ).astype(jnp.bfloat16)
        mass = sums[feat_width : feat_width + 1]
        high = mass.astype(jnp.bfloat16).astype(jnp.float32)
        low = mass - high
        tag = (patch_ref[b] + 1).astype(jnp.float32)
        row = pl.multiple_of(tile * chunk + pairs * feat_width, 16)
        old = send_ref[pl.ds(row, meta), :].astype(jnp.float32)
        new = jnp.where(
            meta_row == pair,
            high,
            jnp.where(
                meta_row == pairs + pair, low, jnp.where(meta_row == 2 * pairs + pair, tag, old)
            ),
        )
        send_ref[pl.ds(row, meta), :] = jnp.where(meta_half == half, new, old).astype(jnp.bfloat16)

    unroll = 4 if blocks % 4 == 0 else 1

    def body(i, _):
        for u in range(unroll):
            one(i * unroll + u)
        return 0

    lax.fori_loop(0, blocks // unroll, body, 0)


def start_tile(capacity, devices, id_ref, recv_ref, embed_ref, base_ref, start_ref, acc_ref):
    feat_width, channels = embed_ref.shape
    tile_rows, tile_cols, _ = base_ref.shape
    pairs = capacity // 2
    meta = meta_rows(pairs)
    chunk = pairs * feat_width + meta
    patch_rows, patch_cols = tile_rows // PATCH, tile_cols // PATCH
    acc_ref[...] = jnp.zeros_like(acc_ref)
    first = lax.broadcasted_iota(jnp.int32, (feat_width + 8, LANES), 1) < CELLS

    def gather(d, _):
        base = pl.multiple_of(d * chunk, 16)
        tags = recv_ref[pl.ds(base + pairs * feat_width, meta), :].astype(jnp.float32)
        for k in range(pairs):
            sums = recv_ref[pl.ds(base + k * feat_width, feat_width), :].astype(jnp.float32)
            mass = tags[k : k + 1] + tags[pairs + k : pairs + k + 1]
            both = jnp.concatenate([sums, jnp.broadcast_to(mass, (8, LANES))], axis=0)
            slot = d * capacity + 2 * k
            a = id_ref[slot]
            acc_ref[a] += jnp.where(first, both, 0.0)
            b = id_ref[slot + 1]
            acc_ref[b] += jnp.where(first, 0.0, both)
        return 0

    lax.fori_loop(0, devices, gather, 0)
    head = lax.broadcasted_iota(jnp.int32, (feat_width, LANES), 1) < CELLS
    embed = embed_ref[...]

    def encoded(p):
        total = acc_ref[p]
        total = total + pltpu.roll(total, CELLS, 1)
        return total[:feat_width] / (1.0 + total[feat_width : feat_width + 1])

    def lift(pr, _):
        parts = []
        for pc in range(0, patch_cols, 2):
            p = pr * patch_cols + pc
            pair = jnp.where(head, encoded(p), encoded(p + 1)).astype(jnp.bfloat16)
            parts.append(lax.dot_general(pair, embed, TN, preferred_element_type=jnp.float32))
        lifted = jnp.concatenate(parts, axis=0).reshape(patch_cols, PATCH, PATCH, channels)
        lifted = lifted.transpose(1, 0, 2, 3).reshape(PATCH, tile_cols, channels)
        rows = pl.ds(pr * PATCH, PATCH)
        start_ref[rows] = (base_ref[rows].astype(jnp.float32) + lifted).astype(jnp.bfloat16)
        return 0

    lax.fori_loop(0, patch_rows, lift, 0)


def grid_block(
    capacity, devices, lat_cells, place_ref, id_ref, ext_ref, norm_ref, qkv_ref, out_ref, mlp_ref,
    up_ref, down_ref, decode_ref, latent_ref, back_ref, packed_ref, att_ref, proj_ref,
):
    ext_rows, ext_cols, channels = ext_ref.shape
    tile_rows, tile_cols, _ = latent_ref.shape
    margin = WIN // 2
    win_rows, win_cols = ext_rows // WIN, ext_cols // WIN
    patch_rows, patch_cols = tile_rows // PATCH, tile_cols // PATCH
    tokens = WIN * WIN
    group = 128
    heads = group // HEAD_DIM
    feat_width = decode_ref.shape[0]
    pairs = capacity // 2
    scale = HEAD_DIM ** (-0.5)
    norm_gain = norm_ref[...]
    head_of = lax.broadcasted_iota(jnp.int32, (tokens, group), 1) // HEAD_DIM
    key_row = lax.broadcasted_iota(jnp.int32, (tokens, heads * tokens), 0) // WIN
    query_row = lax.broadcasted_iota(jnp.int32, (tokens, heads * tokens), 1) % tokens // WIN

    def attend(wr, _):
        rows = pl.ds(wr * WIN, WIN)
        cells = ext_ref[rows].reshape(WIN, win_cols, WIN, channels).transpose(1, 0, 2, 3)
        normed = normalize(cells.reshape(win_cols * tokens, channels), norm_gain)
        packed_ref[...] = jnp.dot(
            normed.astype(jnp.bfloat16), qkv_ref[...], preferred_element_type=jnp.float32
        ).astype(jnp.bfloat16)
        top = place_ref[0] * tile_rows - margin + wr * WIN
        side = lambda r: (r >= 0).astype(jnp.int32) + (r >= lat_cells).astype(jnp.int32)
        bias = jnp.where(side(top + key_row) == side(top + query_row), 0.0, -1e30)
        for w in range(win_cols):
            span = slice(w * tokens, (w + 1) * tokens)
            for g in range(channels // group):
                at = lambda i: slice(i * channels + g * group, i * channels + (g + 1) * group)
                query = packed_ref[span, at(0)]
                key = packed_ref[span, at(1)]
                value = packed_ref[span, at(2)]
                stack = jnp.concatenate(
                    [jnp.where(head_of == h, query, jnp.zeros_like(query)) for h in range(heads)],
                    axis=0,
                )
                scores = lax.dot_general(key, stack, NT, preferred_element_type=jnp.float32)
                scores = scores + bias
                peak = jnp.max(scores, axis=0, keepdims=True)
                raised = jnp.exp((scores - peak) * scale)
                total = jnp.sum(raised, axis=0, keepdims=True)
                probs = (raised * (1.0 / total)).astype(jnp.bfloat16)
                mixed = lax.dot_general(probs, value, TN, preferred_element_type=jnp.float32)
                picked = mixed[:tokens]
                for h in range(1, heads):
                    picked = jnp.where(head_of == h, mixed[h * tokens : (h + 1) * tokens], picked)
                att_ref[rows, w * WIN : (w + 1) * WIN, g * group : (g + 1) * group] = picked.reshape(
                    WIN, WIN, group
                )
        return 0

    lax.fori_loop(0, win_rows, attend, 0)
    mlp_gain = mlp_ref[...]

    def by_patch(values):
        values = values.reshape(PATCH, patch_cols, PATCH, channels).transpose(1, 0, 2, 3)
        return values.reshape(patch_cols * CELLS, channels)

    def finish(pr, _):
        rows = pl.ds(margin + pr * PATCH, PATCH)
        attended = by_patch(att_ref[rows, margin : margin + tile_cols, :]).astype(jnp.bfloat16)
        begun = by_patch(ext_ref[rows, margin : margin + tile_cols, :])
        residual = begun + jnp.dot(attended, out_ref[...], preferred_element_type=jnp.float32)
        normed = normalize(residual, mlp_gain).astype(jnp.bfloat16)
        hidden = jax.nn.gelu(
            jnp.dot(normed, up_ref[...], preferred_element_type=jnp.float32)
        ).astype(jnp.bfloat16)
        latent = residual + jnp.dot(hidden, down_ref[...], preferred_element_type=jnp.float32)
        placed = latent.reshape(patch_cols, PATCH, PATCH, channels).transpose(1, 0, 2, 3)
        latent_ref[pl.ds(pr * PATCH, PATCH)] = placed.reshape(PATCH, tile_cols, channels).astype(
            jnp.bfloat16
        )
        latent = latent.astype(jnp.bfloat16)
        for pc in range(patch_cols):
            cells = latent[pc * CELLS : (pc + 1) * CELLS]
            proj_ref[pr * patch_cols + pc] = lax.dot_general(
                decode_ref[...],
                jnp.concatenate([cells, cells], axis=0),
                NT,
                preferred_element_type=jnp.float32,
            )
        return 0

    lax.fori_loop(0, patch_rows, finish, 0)
    first = lax.broadcasted_iota(jnp.int32, (feat_width, LANES), 1) < CELLS

    def reply(d, _):
        for k in range(pairs):
            slot = d * capacity + 2 * k
            pair = jnp.where(first, proj_ref[id_ref[slot]], proj_ref[id_ref[slot + 1]])
            row = pl.multiple_of((d * pairs + k) * feat_width, 16)
            back_ref[pl.ds(row, feat_width), :] = pair.astype(jnp.bfloat16)
        return 0

    lax.fori_loop(0, devices, reply, 0)


def decode_blocks(slot_ref, back_ref, offset_ref, out_ref):
    feat_width, count = out_ref.shape
    blocks = count // BLK

    def one(b):
        slot = slot_ref[b]
        col = pl.multiple_of(b * BLK, BLK)
        weights = block_weights(offset_ref[:, pl.ds(col, BLK)].astype(jnp.float32))
        total = jnp.sum(weights.astype(jnp.float32), axis=0, keepdims=True)
        nothing = jnp.zeros_like(weights)
        low = slot % 2 == 0
        both = jnp.concatenate(
            [jnp.where(low, weights, nothing), jnp.where(low, nothing, weights)], axis=0
        )
        values = back_ref[pl.ds(pl.multiple_of(slot // 2 * feat_width, 16), feat_width), :]
        mean = jnp.dot(values, both, preferred_element_type=jnp.float32) / total
        out_ref[:, pl.ds(col, BLK)] = mean.astype(jnp.bfloat16)

    unroll = 4 if blocks % 4 == 0 else 1

    def body(i, _):
        for u in range(unroll):
            one(i * unroll + u)
        return 0

    lax.fori_loop(0, blocks // unroll, body, 0)


def with_halo(array, sides, width):
    for axis, dim in sides:
        size, length = (lax.axis_size(axis), array.shape[dim])
        up = [(i, (i + 1) % size) for i in range(size)]
        down = [(j, i) for i, j in up]
        last = lax.slice_in_dim(array, length - width, length, axis=dim)
        initial = lax.slice_in_dim(array, 0, width, axis=dim)
        before = lax.ppermute(last, axis, up)
        after = lax.ppermute(initial, axis, down)
        array = jnp.concatenate([before, array, after], axis=dim)
    return array


def local(
    obs_feat,
    obs_offset,
    block_tile,
    block_patch,
    embed_weight,
    grid_base,
    norm_gain,
    qkv_weight,
    out_weight,
    mlp_gain,
    up_weight,
    down_weight,
    decode_weight,
):
    lat_devices = lax.axis_size("lat")
    lon_devices = lax.axis_size("lon")
    devices = lat_devices * lon_devices
    feat_width, obs_count = obs_feat.shape
    blocks = obs_count // BLK
    capacity = max(2, 2 * blocks // devices)
    capacity += capacity % 2
    pairs = capacity // 2
    tile_rows, tile_cols, channels = grid_base.shape
    patch_total = (tile_rows // PATCH) * (tile_cols // PATCH)
    chunk = pairs * feat_width + meta_rows(pairs)

    send, slots = pl.pallas_call(
        lambda *refs: encode_blocks(capacity, devices, *refs),
        out_shape=(
            jax.ShapeDtypeStruct((devices * chunk, LANES), jnp.bfloat16),
            jax.ShapeDtypeStruct((blocks,), jnp.int32),
        ),
        in_specs=[smem(), smem(), vmem(), vmem()],
        out_specs=(vmem(), smem()),
        scratch_shapes=[pltpu.SMEM((devices,), jnp.int32)],
        compiler_params=params(),
        name="encode_blocks",
    )(block_tile.reshape(blocks), block_patch, obs_feat, obs_offset)

    recv = lax.all_to_all(
        send.reshape(devices, chunk, LANES), ("lat", "lon"), split_axis=0, concat_axis=0, tiled=True
    )
    tags = recv[:, pairs * feat_width + 2 * pairs : pairs * feat_width + 3 * pairs, 0 :: CELLS]
    ids = jnp.clip(tags.astype(jnp.float32).astype(jnp.int32) - 1, 0, patch_total - 1).reshape(-1)

    start = pl.pallas_call(
        lambda *refs: start_tile(capacity, devices, *refs),
        out_shape=jax.ShapeDtypeStruct(grid_base.shape, jnp.bfloat16),
        in_specs=[smem(), vmem(), vmem(), vmem()],
        out_specs=vmem(),
        scratch_shapes=[pltpu.VMEM((patch_total, feat_width + 8, LANES), jnp.float32)],
        compiler_params=params(),
        name="start_tile",
    )(ids, recv.reshape(devices * chunk, LANES), embed_weight, grid_base)

    margin = WIN // 2
    ext = with_halo(start, (("lat", 0), ("lon", 1)), margin).astype(jnp.float32)
    ext_rows, ext_cols, _ = ext.shape
    place = lax.axis_index("lat").astype(jnp.int32).reshape(1)

    latent, back = pl.pallas_call(
        lambda *refs: grid_block(capacity, devices, tile_rows * lat_devices, *refs),
        out_shape=(
            jax.ShapeDtypeStruct(grid_base.shape, jnp.bfloat16),
            jax.ShapeDtypeStruct((devices * pairs * feat_width, LANES), jnp.bfloat16),
        ),
        in_specs=[smem(), smem()] + [vmem()] * 8,
        out_specs=(vmem(), vmem()),
        scratch_shapes=[
            pltpu.VMEM((ext_cols // WIN * WIN * WIN, 3 * channels), jnp.bfloat16),
            pltpu.VMEM((ext_rows, ext_cols, channels), jnp.float32),
            pltpu.VMEM((patch_total, feat_width, LANES), jnp.float32),
        ],
        compiler_params=params(),
        name="grid_block",
    )(
        place,
        ids,
        ext,
        norm_gain.reshape(1, channels),
        qkv_weight,
        out_weight,
        mlp_gain.reshape(1, channels),
        up_weight,
        down_weight,
        decode_weight.T,
    )

    returned = lax.all_to_all(
        back.reshape(devices, pairs * feat_width, LANES),
        ("lat", "lon"),
        split_axis=0,
        concat_axis=0,
        tiled=True,
    )
    obs_out = pl.pallas_call(
        decode_blocks,
        out_shape=jax.ShapeDtypeStruct((feat_width, obs_count), jnp.bfloat16),
        in_specs=[smem(), vmem(), vmem()],
        out_specs=vmem(),
        compiler_params=params(),
        name="decode_blocks",
    )(slots, returned.reshape(devices * pairs * feat_width, LANES), obs_offset)
    return (latent, obs_out)


def solution(mesh):
    placed = (
        P(None, ("lat", "lon")),
        P(None, ("lat", "lon")),
        P(("lat", "lon"), None),
        P(("lat", "lon")),
        P(),
        P("lat", "lon", None),
        P(),
        P(),
        P(),
        P(),
        P(),
        P(),
        P(),
    )
    return jax.shard_map(
        local,
        mesh=mesh,
        in_specs=placed,
        out_specs=(P("lat", "lon", None), P(None, ("lat", "lon"))),
        check_vma=False,
    )
```

```python
import math

import jax
import jax.numpy as jnp
from jax import lax
from jax.experimental import pallas as pl
from jax.experimental.pallas import tpu as pltpu
from jax.sharding import PartitionSpec as P

HEAD_DIM = 32
WIN = 8
PATCH = 8
BLK = 128
CELLS = PATCH * PATCH
LANES = 2 * CELLS

epsilon = 1e-05
spread_coef = 0.5

NT = (((1,), (1,)), ((), ()))
TN = (((0,), (0,)), ((), ()))


def params(mib):
    return pltpu.CompilerParams(vmem_limit_bytes=mib * 1024 * 1024)


def vmem():
    return pl.BlockSpec(memory_space=pltpu.VMEM)


def smem():
    return pl.BlockSpec(memory_space=pltpu.SMEM)


def normalize(values, gain_row):
    center = jnp.mean(values, axis=-1, keepdims=True)
    centered = values - center
    variance = jnp.mean(centered * centered, axis=-1, keepdims=True)
    return centered * lax.rsqrt(variance + epsilon) * gain_row


def block_weights(offsets):
    axis_id = lax.broadcasted_iota(jnp.int32, (PATCH, BLK), 0).astype(jnp.float32) + 0.5
    row_gap = axis_id - offsets[0:1]
    col_gap = axis_id - offsets[1:2]
    row_gap = row_gap * row_gap
    col_gap = col_gap * col_gap
    total = row_gap[:, None, :] + col_gap[None, :, :]
    return jnp.exp(-spread_coef * total).reshape(CELLS, BLK).astype(jnp.bfloat16)


def meta_rows(pairs):
    return -(-3 * pairs // 16) * 16


def encode_blocks(capacity, devices, tile_ref, patch_ref, feat_ref, offset_ref, send_ref, slot_ref, count_ref):
    blocks = feat_ref.shape[1] // BLK
    feat_width = feat_ref.shape[0]
    pairs = capacity // 2
    meta = meta_rows(pairs)
    chunk = pairs * feat_width + meta
    send_ref[...] = jnp.zeros_like(send_ref)

    def clear(t, _):
        count_ref[t] = 0
        return 0

    lax.fori_loop(0, devices, clear, 0)
    lane_half = lax.broadcasted_iota(jnp.int32, (feat_width, LANES), 1) // CELLS
    meta_half = lax.broadcasted_iota(jnp.int32, (meta, LANES), 1) // CELLS
    meta_row = lax.broadcasted_iota(jnp.int32, (meta, LANES), 0)
    ones = jnp.ones((16, BLK), jnp.bfloat16)

    def one(b):
        tile = tile_ref[b]
        rank = count_ref[tile]
        count_ref[tile] = rank + 1
        slot_ref[b] = tile * capacity + rank
        pair = rank // 2
        half = rank % 2
        col = pl.multiple_of(b * BLK, BLK)
        feat = jnp.concatenate([feat_ref[:, pl.ds(col, BLK)], ones], axis=0)
        weights = block_weights(offset_ref[:, pl.ds(col, BLK)].astype(jnp.float32))
        twice = jnp.concatenate([weights, weights], axis=0)
        sums = lax.dot_general(feat, twice, NT, preferred_element_type=jnp.float32)
        row = pl.multiple_of(tile * chunk + pair * feat_width, 16)
        old = send_ref[pl.ds(row, feat_width), :].astype(jnp.float32)
        send_ref[pl.ds(row, feat_width), :] = jnp.where(
            lane_half == half, sums[:feat_width], old
        ).astype(jnp.bfloat16)
        mass = sums[feat_width : feat_width + 1]
        high = mass.astype(jnp.bfloat16).astype(jnp.float32)
        low = mass - high
        tag = (patch_ref[b] + 1).astype(jnp.float32)
        row = pl.multiple_of(tile * chunk + pairs * feat_width, 16)
        old = send_ref[pl.ds(row, meta), :].astype(jnp.float32)
        new = jnp.where(
            meta_row == pair,
            high,
            jnp.where(
                meta_row == pairs + pair, low, jnp.where(meta_row == 2 * pairs + pair, tag, old)
            ),
        )
        send_ref[pl.ds(row, meta), :] = jnp.where(meta_half == half, new, old).astype(jnp.bfloat16)

    unroll = 32 if blocks % 32 == 0 else 1

    def body(i, _):
        for u in range(unroll):
            one(i * unroll + u)
        return 0

    lax.fori_loop(0, blocks // unroll, body, 0)


def start_tile(capacity, devices, id_ref, recv_ref, embed_ref, base_ref, start_ref, acc_ref):
    feat_width, channels = embed_ref.shape
    tile_rows, tile_cols, _ = base_ref.shape
    pairs = capacity // 2
    meta = meta_rows(pairs)
    chunk = pairs * feat_width + meta
    patch_rows, patch_cols = tile_rows // PATCH, tile_cols // PATCH
    acc_ref[...] = jnp.zeros_like(acc_ref)
    first = lax.broadcasted_iota(jnp.int32, (feat_width + 8, LANES), 1) < CELLS

    def gather(d, _):
        base = pl.multiple_of(d * chunk, 16)
        tags = recv_ref[pl.ds(base + pairs * feat_width, meta), :].astype(jnp.float32)
        for k in range(pairs):
            sums = recv_ref[pl.ds(base + k * feat_width, feat_width), :].astype(jnp.float32)
            mass = tags[k : k + 1] + tags[pairs + k : pairs + k + 1]
            both = jnp.concatenate([sums, jnp.broadcast_to(mass, (8, LANES))], axis=0)
            slot = d * capacity + 2 * k
            a = id_ref[slot]
            acc_ref[a] += jnp.where(first, both, 0.0)
            b = id_ref[slot + 1]
            acc_ref[b] += jnp.where(first, 0.0, both)
        return 0

    lax.fori_loop(0, devices, gather, 0, unroll=4)
    head = lax.broadcasted_iota(jnp.int32, (feat_width, LANES), 1) < CELLS
    embed = embed_ref[...]

    def encoded(p):
        total = acc_ref[p]
        total = total + pltpu.roll(total, CELLS, 1)
        return total[:feat_width] / (1.0 + total[feat_width : feat_width + 1])

    def lift(pr, _):
        parts = []
        for pc in range(0, patch_cols, 2):
            p = pr * patch_cols + pc
            pair = jnp.where(head, encoded(p), encoded(p + 1)).astype(jnp.bfloat16)
            parts.append(lax.dot_general(pair, embed, TN, preferred_element_type=jnp.float32))
        lifted = jnp.concatenate(parts, axis=0).reshape(patch_cols, PATCH, PATCH, channels)
        lifted = lifted.transpose(1, 0, 2, 3).reshape(PATCH, tile_cols, channels)
        rows = pl.ds(pr * PATCH, PATCH)
        start_ref[rows] = (base_ref[rows].astype(jnp.float32) + lifted).astype(jnp.bfloat16)
        return 0

    lax.fori_loop(0, patch_rows, lift, 0, unroll=True)


def grid_block(
    capacity, devices, lat_cells, place_ref, id_ref, ext_ref, norm_ref, qkv_ref, out_ref, mlp_ref,
    up_ref, down_ref, decode_ref, latent_ref, back_ref, turned_ref, key_ref, pack_ref, att_ref,
    mixed_ref, proj_ref, score_ref, prob_ref,
):
    ext_rows, ext_cols, channels = ext_ref.shape
    tile_rows, tile_cols, _ = latent_ref.shape
    margin = WIN // 2
    win_rows, win_cols = ext_rows // WIN, ext_cols // WIN
    win_pairs = -(-win_cols // 2)
    patch_rows, patch_cols = tile_rows // PATCH, tile_cols // PATCH
    tokens = WIN * WIN
    group = 128
    heads = group // HEAD_DIM
    feat_width = decode_ref.shape[1]
    pairs = capacity // 2
    scale = HEAD_DIM ** (-0.5) / math.log(2.0)
    norm_gain = norm_ref[...]
    turned_ref[:channels] = qkv_ref[:, :channels].T
    turned_ref[channels:] = qkv_ref[:, 2 * channels :].T
    shape = (tokens, heads * LANES)
    own = lax.broadcasted_iota(jnp.int32, shape, 1) % LANES < tokens
    key_row = lax.broadcasted_iota(jnp.int32, (tokens, LANES), 0) // WIN
    query_row = lax.broadcasted_iota(jnp.int32, (tokens, LANES), 1) % tokens // WIN
    nothing = jnp.zeros(shape, jnp.bfloat16)
    empty = jnp.zeros((HEAD_DIM, LANES), jnp.bfloat16)

    def attend(wr):
        rows = pl.ds(wr * WIN, WIN)
        cells = ext_ref[rows].reshape(WIN, win_cols, WIN, channels).transpose(1, 0, 2, 3)
        normed = normalize(cells.reshape(win_cols * tokens, channels), norm_gain)
        normed = normed.astype(jnp.bfloat16)
        if win_cols % 2:
            normed = jnp.concatenate([normed, jnp.zeros((tokens, channels), jnp.bfloat16)], axis=0)
        key_ref[...] = jnp.dot(
            normed, qkv_ref[:, channels : 2 * channels], preferred_element_type=jnp.float32
        ).astype(jnp.bfloat16)
        pack_ref[...] = lax.dot_general(
            turned_ref[...], normed, NT, preferred_element_type=jnp.float32
        ).astype(jnp.bfloat16)
        edge = wr in (0, win_rows - 1)
        if edge:
            top = place_ref[0] * tile_rows - margin + wr * WIN
            side = lambda r: (r >= 0).astype(jnp.int32) + (r >= lat_cells).astype(jnp.int32)
            bias = jnp.where(side(top + key_row) == side(top + query_row), 0.0, -1e30)
            bias = jnp.concatenate([bias] * heads, axis=1)
        parts = [(p, g) for p in range(win_pairs) for g in range(channels // group)]
        for n, (p, g) in enumerate(parts):
            span = slice(p * LANES, (p + 1) * LANES)
            at = slice(g * group, (g + 1) * group)
            query = pack_ref[at, span]
            stack = jnp.concatenate(
                [
                    jnp.concatenate(
                        [
                            query[h * HEAD_DIM : (h + 1) * HEAD_DIM] if i == h else empty
                            for i in range(heads)
                        ],
                        axis=0,
                    )
                    for h in range(heads)
                ],
                axis=1,
            )
            scores = jnp.dot(key_ref[span, at], stack, preferred_element_type=jnp.float32)
            scores = jnp.where(own, scores[:tokens], scores[tokens:])
            score_ref[n] = scores + bias if edge else scores
        for n, (p, g) in enumerate(parts):
            scores = score_ref[n]
            peak = jnp.max(scores, axis=0, keepdims=True)
            raised = jnp.exp2((scores - peak) * scale)
            total = jnp.sum(raised, axis=0, keepdims=True)
            probs = (raised * (1.0 / total)).astype(jnp.bfloat16)
            prob_ref[n, :tokens] = jnp.where(own, probs, nothing)
            prob_ref[n, tokens:] = jnp.where(own, nothing, probs)
        for n, (p, g) in enumerate(parts):
            span = slice(p * LANES, (p + 1) * LANES)
            for h in range(0, heads, 2):
                at = g * group + h * HEAD_DIM
                both = jnp.dot(
                    pack_ref[channels + at : channels + at + 2 * HEAD_DIM, span],
                    prob_ref[n, :, h * LANES : (h + 2) * LANES],
                    preferred_element_type=jnp.float32,
                ).astype(jnp.bfloat16)
                att_ref[at : at + HEAD_DIM, span] = both[:HEAD_DIM, :LANES]
                att_ref[at + HEAD_DIM : at + 2 * HEAD_DIM, span] = both[HEAD_DIM:, LANES:]
        mixed = lax.dot_general(att_ref[...], out_ref[...], TN, preferred_element_type=jnp.float32)
        for w in range(win_cols):
            mixed_ref[rows, w * WIN : (w + 1) * WIN, :] = mixed[w * tokens : (w + 1) * tokens].reshape(
                WIN, WIN, channels
            )

    for wr in range(win_rows):
        attend(wr)
    mlp_gain = mlp_ref[...]
    first = lax.broadcasted_iota(jnp.int32, (feat_width, LANES), 1) < CELLS

    def by_patch(values):
        values = values.reshape(PATCH, patch_cols, PATCH, channels).transpose(1, 0, 2, 3)
        return values.reshape(patch_cols * CELLS, channels)

    def finish(pr, _):
        rows = pl.ds(margin + pr * PATCH, PATCH)
        inner = slice(margin, margin + tile_cols)
        residual = by_patch(ext_ref[rows, inner, :] + mixed_ref[rows, inner, :])
        normed = normalize(residual, mlp_gain).astype(jnp.bfloat16)
        hidden = jax.nn.gelu(
            jnp.dot(normed, up_ref[...], preferred_element_type=jnp.float32)
        ).astype(jnp.bfloat16)
        latent = residual + jnp.dot(hidden, down_ref[...], preferred_element_type=jnp.float32)
        placed = latent.reshape(patch_cols, PATCH, PATCH, channels).transpose(1, 0, 2, 3)
        latent_ref[pl.ds(pr * PATCH, PATCH)] = placed.reshape(PATCH, tile_cols, channels).astype(
            jnp.bfloat16
        )
        latent = latent.astype(jnp.bfloat16)
        projected = jnp.dot(latent, decode_ref[...], preferred_element_type=jnp.float32)
        for pc in range(0, patch_cols, 2):
            turned = projected[pc * CELLS : pc * CELLS + LANES].T
            swapped = pltpu.roll(turned, CELLS, 1)
            proj_ref[pr * patch_cols + pc] = jnp.where(first, turned, swapped)
            proj_ref[pr * patch_cols + pc + 1] = jnp.where(first, swapped, turned)
        return 0

    lax.fori_loop(0, patch_rows, finish, 0, unroll=True)

    def reply(d, _):
        for k in range(pairs):
            slot = d * capacity + 2 * k
            pair = jnp.where(first, proj_ref[id_ref[slot]], proj_ref[id_ref[slot + 1]])
            row = pl.multiple_of((d * pairs + k) * feat_width, 16)
            back_ref[pl.ds(row, feat_width), :] = pair.astype(jnp.bfloat16)
        return 0

    lax.fori_loop(0, devices, reply, 0)


def decode_blocks(slot_ref, back_ref, offset_ref, out_ref):
    feat_width, count = out_ref.shape
    blocks = count // BLK

    def one(b):
        slot = slot_ref[b]
        col = pl.multiple_of(b * BLK, BLK)
        weights = block_weights(offset_ref[:, pl.ds(col, BLK)].astype(jnp.float32))
        total = jnp.sum(weights.astype(jnp.float32), axis=0, keepdims=True)
        nothing = jnp.zeros_like(weights)
        low = slot % 2 == 0
        both = jnp.concatenate(
            [jnp.where(low, weights, nothing), jnp.where(low, nothing, weights)], axis=0
        )
        values = back_ref[pl.ds(pl.multiple_of(slot // 2 * feat_width, 16), feat_width), :]
        mean = jnp.dot(values, both, preferred_element_type=jnp.float32) * (1.0 / total)
        out_ref[:, pl.ds(col, BLK)] = mean.astype(jnp.bfloat16)

    unroll = 32 if blocks % 32 == 0 else 1

    def body(i, _):
        for u in range(unroll):
            one(i * unroll + u)
        return 0

    lax.fori_loop(0, blocks // unroll, body, 0)


def with_halo(array, sides, width):
    for axis, dim in sides:
        size, length = (lax.axis_size(axis), array.shape[dim])
        up = [(i, (i + 1) % size) for i in range(size)]
        down = [(j, i) for i, j in up]
        last = lax.slice_in_dim(array, length - width, length, axis=dim)
        initial = lax.slice_in_dim(array, 0, width, axis=dim)
        before = lax.ppermute(last, axis, up)
        after = lax.ppermute(initial, axis, down)
        array = jnp.concatenate([before, array, after], axis=dim)
    return array


def local(
    obs_feat,
    obs_offset,
    block_tile,
    block_patch,
    embed_weight,
    grid_base,
    norm_gain,
    qkv_weight,
    out_weight,
    mlp_gain,
    up_weight,
    down_weight,
    decode_weight,
):
    lat_devices = lax.axis_size("lat")
    lon_devices = lax.axis_size("lon")
    devices = lat_devices * lon_devices
    feat_width, obs_count = obs_feat.shape
    blocks = obs_count // BLK
    capacity = max(2, 2 * blocks // devices)
    capacity += capacity % 2
    pairs = capacity // 2
    tile_rows, tile_cols, channels = grid_base.shape
    patch_total = (tile_rows // PATCH) * (tile_cols // PATCH)
    chunk = pairs * feat_width + meta_rows(pairs)

    send, slots = pl.pallas_call(
        lambda *refs: encode_blocks(capacity, devices, *refs),
        out_shape=(
            jax.ShapeDtypeStruct((devices * chunk, LANES), jnp.bfloat16),
            jax.ShapeDtypeStruct((blocks,), jnp.int32),
        ),
        in_specs=[smem(), smem(), vmem(), vmem()],
        out_specs=(vmem(), smem()),
        scratch_shapes=[pltpu.SMEM((devices,), jnp.int32)],
        compiler_params=params(8),
        name="encode_blocks",
    )(block_tile.reshape(blocks), block_patch, obs_feat, obs_offset)

    recv = lax.all_to_all(
        send.reshape(devices, chunk, LANES), ("lat", "lon"), split_axis=0, concat_axis=0, tiled=True
    )
    tags = recv[:, pairs * feat_width + 2 * pairs : pairs * feat_width + 3 * pairs, 0 :: CELLS]
    ids = jnp.clip(tags.astype(jnp.float32).astype(jnp.int32) - 1, 0, patch_total - 1).reshape(-1)

    start = pl.pallas_call(
        lambda *refs: start_tile(capacity, devices, *refs),
        out_shape=jax.ShapeDtypeStruct(grid_base.shape, jnp.bfloat16),
        in_specs=[smem(), vmem(), vmem(), vmem()],
        out_specs=vmem(),
        scratch_shapes=[pltpu.VMEM((patch_total, feat_width + 8, LANES), jnp.float32)],
        compiler_params=params(8),
        name="start_tile",
    )(ids, recv.reshape(devices * chunk, LANES), embed_weight, grid_base)

    margin = WIN // 2
    ext = with_halo(start, (("lat", 0), ("lon", 1)), margin).astype(jnp.float32)
    ext_rows, ext_cols, _ = ext.shape
    padded = -(-ext_cols // (2 * WIN)) * LANES
    place = lax.axis_index("lat").astype(jnp.int32).reshape(1)

    latent, back = pl.pallas_call(
        lambda *refs: grid_block(capacity, devices, tile_rows * lat_devices, *refs),
        out_shape=(
            jax.ShapeDtypeStruct(grid_base.shape, jnp.bfloat16),
            jax.ShapeDtypeStruct((devices * pairs * feat_width, LANES), jnp.bfloat16),
        ),
        in_specs=[smem(), smem()] + [vmem()] * 8,
        out_specs=(vmem(), vmem()),
        scratch_shapes=[
            pltpu.VMEM((2 * channels, channels), jnp.bfloat16),
            pltpu.VMEM((padded, channels), jnp.bfloat16),
            pltpu.VMEM((2 * channels, padded), jnp.bfloat16),
            pltpu.VMEM((channels, padded), jnp.bfloat16),
            pltpu.VMEM((ext_rows, ext_cols, channels), jnp.float32),
            pltpu.VMEM((patch_total, feat_width, LANES), jnp.float32),
            pltpu.VMEM((padded * channels // LANES // 128, WIN * WIN, 4 * LANES), jnp.float32),
            pltpu.VMEM((padded * channels // LANES // 128, LANES, 4 * LANES), jnp.bfloat16),
        ],
        compiler_params=params(20),
        name="grid_block",
    )(
        place,
        ids,
        ext,
        norm_gain.reshape(1, channels),
        qkv_weight,
        out_weight,
        mlp_gain.reshape(1, channels),
        up_weight,
        down_weight,
        decode_weight,
    )

    returned = lax.all_to_all(
        back.reshape(devices, pairs * feat_width, LANES),
        ("lat", "lon"),
        split_axis=0,
        concat_axis=0,
        tiled=True,
    )
    obs_out = pl.pallas_call(
        decode_blocks,
        out_shape=jax.ShapeDtypeStruct((feat_width, obs_count), jnp.bfloat16),
        in_specs=[smem(), vmem(), vmem()],
        out_specs=vmem(),
        compiler_params=params(8),
        name="decode_blocks",
    )(slots, returned.reshape(devices * pairs * feat_width, LANES), obs_offset)
    return (latent, obs_out)


def solution(mesh):
    placed = (
        P(None, ("lat", "lon")),
        P(None, ("lat", "lon")),
        P(("lat", "lon"), None),
        P(("lat", "lon")),
        P(),
        P("lat", "lon", None),
        P(),
        P(),
        P(),
        P(),
        P(),
        P(),
        P(),
    )
    return jax.shard_map(
        local,
        mesh=mesh,
        in_specs=placed,
        out_specs=(P("lat", "lon", None), P(None, ("lat", "lon"))),
        check_vma=False,
    )
```

```python
import math

import jax
import jax.numpy as jnp
from jax import lax
from jax.experimental import pallas as pl
from jax.experimental.pallas import tpu as pltpu
from jax.sharding import Mesh
from jax.sharding import PartitionSpec as P

HEAD_DIM = 32
WIN = 8
PATCH = 8
BLK = 128
CELLS = PATCH * PATCH
LANES = 2 * CELLS

epsilon = 1e-05
spread_coef = 0.5

NT = (((1,), (1,)), ((), ()))
TN = (((0,), (0,)), ((), ()))


def params(mib):
    return pltpu.CompilerParams(vmem_limit_bytes=mib * 1024 * 1024)


def vmem():
    return pl.BlockSpec(memory_space=pltpu.VMEM)


def smem():
    return pl.BlockSpec(memory_space=pltpu.SMEM)


def normalize(values, gain_row):
    center = jnp.mean(values, axis=-1, keepdims=True)
    centered = values - center
    variance = jnp.mean(centered * centered, axis=-1, keepdims=True)
    return centered * lax.rsqrt(variance + epsilon) * gain_row


def block_weights(offsets):
    axis_id = lax.broadcasted_iota(jnp.int32, (PATCH, BLK), 0).astype(jnp.float32) + 0.5
    row_gap = axis_id - offsets[0:1]
    col_gap = axis_id - offsets[1:2]
    row_gap = row_gap * row_gap
    col_gap = col_gap * col_gap
    total = row_gap[:, None, :] + col_gap[None, :, :]
    return jnp.exp(-spread_coef * total).reshape(CELLS, BLK).astype(jnp.bfloat16)


def meta_rows(pairs):
    return -(-3 * pairs // 16) * 16


def encode_blocks(capacity, shape, place_ref, tile_ref, patch_ref, feat_ref, offset_ref, send_ref, slot_ref, count_ref):
    lat, depth, width = shape
    plane = lat * width
    devices = plane * depth
    blocks = feat_ref.shape[1] // BLK
    feat_width = feat_ref.shape[0]
    pairs = capacity // 2
    meta = meta_rows(pairs)
    chunk = pairs * feat_width + meta
    send_ref[...] = jnp.zeros_like(send_ref)

    def clear(t, _):
        count_ref[t] = 0
        return 0

    lax.fori_loop(0, devices, clear, 0)
    lane_half = lax.broadcasted_iota(jnp.int32, (feat_width, LANES), 1) // CELLS
    meta_half = lax.broadcasted_iota(jnp.int32, (meta, LANES), 1) // CELLS
    meta_row = lax.broadcasted_iota(jnp.int32, (meta, LANES), 0)
    ones = jnp.ones((16, BLK), jnp.bfloat16)

    def one(b):
        tile = tile_ref[b]
        rank = count_ref[tile]
        count_ref[tile] = rank + 1
        lon = tile % (depth * width)
        partner = (tile // (depth * width) * width + lon % width) ^ place_ref[0]
        hop = (lon // width + depth - place_ref[1]) % depth
        piece = jnp.where(hop == 0, partner, plane + partner * (depth - 1) + hop - 1)
        slot_ref[b] = piece * capacity + rank
        pair = rank // 2
        half = rank % 2
        col = pl.multiple_of(b * BLK, BLK)
        feat = jnp.concatenate([feat_ref[:, pl.ds(col, BLK)], ones], axis=0)
        weights = block_weights(offset_ref[:, pl.ds(col, BLK)].astype(jnp.float32))
        twice = jnp.concatenate([weights, weights], axis=0)
        sums = lax.dot_general(feat, twice, NT, preferred_element_type=jnp.float32)
        row = pl.multiple_of(piece * chunk + pair * feat_width, 16)
        old = send_ref[pl.ds(row, feat_width), :].astype(jnp.float32)
        send_ref[pl.ds(row, feat_width), :] = jnp.where(
            lane_half == half, sums[:feat_width], old
        ).astype(jnp.bfloat16)
        mass = sums[feat_width : feat_width + 1]
        high = mass.astype(jnp.bfloat16).astype(jnp.float32)
        low = mass - high
        tag = (patch_ref[b] + 1).astype(jnp.float32)
        row = pl.multiple_of(piece * chunk + pairs * feat_width, 16)
        old = send_ref[pl.ds(row, meta), :].astype(jnp.float32)
        new = jnp.where(
            meta_row == pair,
            high,
            jnp.where(
                meta_row == pairs + pair, low, jnp.where(meta_row == 2 * pairs + pair, tag, old)
            ),
        )
        send_ref[pl.ds(row, meta), :] = jnp.where(meta_half == half, new, old).astype(jnp.bfloat16)

    unroll = 32 if blocks % 32 == 0 else 1

    def body(i, _):
        for u in range(unroll):
            one(i * unroll + u)
        return 0

    lax.fori_loop(0, blocks // unroll, body, 0)


def dense_rows(pairs, feat_width):
    return pairs * feat_width + -(-2 * pairs // 16) * 16


def add_chunk(capacity, feat_width, id_ref, slot, recv_ref, base, acc_ref):
    pairs = capacity // 2
    first = lax.broadcasted_iota(jnp.int32, (feat_width + 8, LANES), 1) < CELLS
    tags = recv_ref[base + pairs * feat_width : base + pairs * feat_width + meta_rows(pairs), :]
    tags = tags.astype(jnp.float32)
    for k in range(pairs):
        at = base + k * feat_width
        sums = recv_ref[at : at + feat_width, :].astype(jnp.float32)
        mass = tags[k : k + 1] + tags[pairs + k : pairs + k + 1]
        both = jnp.concatenate([sums, jnp.broadcast_to(mass, (8, LANES))], axis=0)
        acc_ref[id_ref[slot + 2 * k]] += jnp.where(first, both, 0.0)
        acc_ref[id_ref[slot + 2 * k + 1]] += jnp.where(first, 0.0, both)


def paired(acc_ref, j):
    first = lax.broadcasted_iota(jnp.int32, acc_ref.shape[1:], 1) < CELLS
    even, odd = acc_ref[2 * j], acc_ref[2 * j + 1]
    even, odd = even + pltpu.roll(even, CELLS, 1), odd + pltpu.roll(odd, CELLS, 1)
    return jnp.where(first, even, odd)


def gather_planes(capacity, plane, hops, feat_width, id_ref, *refs):
    pieces, outs, acc_ref = refs[:plane], refs[plane : plane + hops], refs[plane + hops]
    pairs = capacity // 2
    chunk = pairs * feat_width + meta_rows(pairs)
    patch_pairs = acc_ref.shape[1] // 2
    acc_ref[...] = jnp.zeros_like(acc_ref)
    for r in range(plane):
        for hop in range(hops):
            slot = (r * hops + hop) * capacity
            add_chunk(capacity, feat_width, id_ref, slot, pieces[r], hop * chunk, acc_ref.at[hop])
    for hop in range(hops):
        masses = []
        for j in range(patch_pairs):
            pair = paired(acc_ref.at[hop], j)
            outs[hop][j * feat_width : (j + 1) * feat_width, :] = pair[:feat_width].astype(
                jnp.bfloat16
            )
            masses.append(pair[feat_width : feat_width + 1])
        masses = jnp.concatenate(masses, axis=0)
        high = masses.astype(jnp.bfloat16).astype(jnp.float32)
        spare = outs[hop].shape[0] - patch_pairs * (feat_width + 2)
        rows = [high, masses - high] + ([jnp.zeros((spare, LANES), jnp.float32)] if spare else [])
        outs[hop][patch_pairs * feat_width :, :] = jnp.concatenate(rows, axis=0).astype(jnp.bfloat16)


def start_tile(capacity, plane, hops, id_ref, *refs):
    pieces, parts = refs[:plane], refs[plane : plane + hops]
    embed_ref, base_ref, start_ref, acc_ref = refs[plane + hops :]
    feat_width, channels = embed_ref.shape
    tile_rows, tile_cols, _ = base_ref.shape
    patch_rows, patch_cols = tile_rows // PATCH, tile_cols // PATCH
    patch_pairs = patch_rows * patch_cols // 2
    acc_ref[...] = jnp.zeros_like(acc_ref)
    for r in range(plane):
        add_chunk(capacity, feat_width, id_ref, r * capacity, pieces[r], 0, acc_ref)
    embed = embed_ref[...]
    mass_rows = [part[patch_pairs * feat_width :, :].astype(jnp.float32) for part in parts]
    for pr in range(patch_rows):
        lifted = []
        for pc in range(patch_cols // 2):
            j = pr * (patch_cols // 2) + pc
            pair = paired(acc_ref, j)
            sums, mass = pair[:feat_width], pair[feat_width : feat_width + 1]
            for part, rows in zip(parts, mass_rows):
                sums = sums + part[j * feat_width : (j + 1) * feat_width, :].astype(jnp.float32)
                mass = mass + (rows[j : j + 1] + rows[patch_pairs + j : patch_pairs + j + 1])
            encoded = (sums * (1.0 / (1.0 + mass))).astype(jnp.bfloat16)
            lifted.append(lax.dot_general(encoded, embed, TN, preferred_element_type=jnp.float32))
        lifted = jnp.concatenate(lifted, axis=0).reshape(patch_cols, PATCH, PATCH, channels)
        lifted = lifted.transpose(1, 0, 2, 3).reshape(PATCH, tile_cols, channels)
        rows = slice(pr * PATCH, (pr + 1) * PATCH)
        start_ref[rows] = (base_ref[rows].astype(jnp.float32) + lifted).astype(jnp.bfloat16)


def grid_block(
    lat_cells, place_ref, ext_ref, norm_ref, qkv_ref, out_ref, mlp_ref,
    up_ref, down_ref, decode_ref, latent_ref, proj_ref, turned_ref, key_ref, pack_ref, att_ref,
    mixed_ref, score_ref, prob_ref,
):
    ext_rows, ext_cols, channels = ext_ref.shape
    tile_rows, tile_cols, _ = latent_ref.shape
    margin = WIN // 2
    win_rows, win_cols = ext_rows // WIN, ext_cols // WIN
    win_pairs = -(-win_cols // 2)
    patch_rows, patch_cols = tile_rows // PATCH, tile_cols // PATCH
    tokens = WIN * WIN
    group = 128
    heads = group // HEAD_DIM
    feat_width = decode_ref.shape[1]
    scale = HEAD_DIM ** (-0.5) / math.log(2.0)
    norm_gain = norm_ref[...]
    turned_ref[:channels] = qkv_ref[:, :channels].T
    turned_ref[channels:] = qkv_ref[:, 2 * channels :].T
    shape = (tokens, heads * LANES)
    own = lax.broadcasted_iota(jnp.int32, shape, 1) % LANES < tokens
    key_row = lax.broadcasted_iota(jnp.int32, (tokens, LANES), 0) // WIN
    query_row = lax.broadcasted_iota(jnp.int32, (tokens, LANES), 1) % tokens // WIN
    nothing = jnp.zeros(shape, jnp.bfloat16)
    empty = jnp.zeros((HEAD_DIM, LANES), jnp.bfloat16)

    def attend(wr):
        rows = pl.ds(wr * WIN, WIN)
        cells = ext_ref[rows].reshape(WIN, win_cols, WIN, channels).transpose(1, 0, 2, 3)
        normed = normalize(cells.reshape(win_cols * tokens, channels), norm_gain)
        normed = normed.astype(jnp.bfloat16)
        if win_cols % 2:
            normed = jnp.concatenate([normed, jnp.zeros((tokens, channels), jnp.bfloat16)], axis=0)
        key_ref[...] = jnp.dot(
            normed, qkv_ref[:, channels : 2 * channels], preferred_element_type=jnp.float32
        ).astype(jnp.bfloat16)
        pack_ref[...] = lax.dot_general(
            turned_ref[...], normed, NT, preferred_element_type=jnp.float32
        ).astype(jnp.bfloat16)
        edge = wr in (0, win_rows - 1)
        if edge:
            top = place_ref[2] * tile_rows - margin + wr * WIN
            side = lambda r: (r >= 0).astype(jnp.int32) + (r >= lat_cells).astype(jnp.int32)
            bias = jnp.where(side(top + key_row) == side(top + query_row), 0.0, -1e30)
            bias = jnp.concatenate([bias] * heads, axis=1)
        parts = [(p, g) for p in range(win_pairs) for g in range(channels // group)]
        for n, (p, g) in enumerate(parts):
            span = slice(p * LANES, (p + 1) * LANES)
            at = slice(g * group, (g + 1) * group)
            query = pack_ref[at, span]
            stack = jnp.concatenate(
                [
                    jnp.concatenate(
                        [
                            query[h * HEAD_DIM : (h + 1) * HEAD_DIM] if i == h else empty
                            for i in range(heads)
                        ],
                        axis=0,
                    )
                    for h in range(heads)
                ],
                axis=1,
            )
            scores = jnp.dot(key_ref[span, at], stack, preferred_element_type=jnp.float32)
            scores = jnp.where(own, scores[:tokens], scores[tokens:])
            score_ref[n] = scores + bias if edge else scores
        for n, (p, g) in enumerate(parts):
            scores = score_ref[n]
            peak = jnp.max(scores, axis=0, keepdims=True)
            raised = jnp.exp2((scores - peak) * scale)
            total = jnp.sum(raised, axis=0, keepdims=True)
            probs = (raised * (1.0 / total)).astype(jnp.bfloat16)
            prob_ref[n, :tokens] = jnp.where(own, probs, nothing)
            prob_ref[n, tokens:] = jnp.where(own, nothing, probs)
        for n, (p, g) in enumerate(parts):
            span = slice(p * LANES, (p + 1) * LANES)
            for h in range(0, heads, 2):
                at = g * group + h * HEAD_DIM
                both = jnp.dot(
                    pack_ref[channels + at : channels + at + 2 * HEAD_DIM, span],
                    prob_ref[n, :, h * LANES : (h + 2) * LANES],
                    preferred_element_type=jnp.float32,
                ).astype(jnp.bfloat16)
                att_ref[at : at + HEAD_DIM, span] = both[:HEAD_DIM, :LANES]
                att_ref[at + HEAD_DIM : at + 2 * HEAD_DIM, span] = both[HEAD_DIM:, LANES:]
        mixed = lax.dot_general(att_ref[...], out_ref[...], TN, preferred_element_type=jnp.float32)
        for w in range(win_cols):
            mixed_ref[rows, w * WIN : (w + 1) * WIN, :] = mixed[w * tokens : (w + 1) * tokens].reshape(
                WIN, WIN, channels
            )

    for wr in range(win_rows):
        attend(wr)
    mlp_gain = mlp_ref[...]

    def by_patch(values):
        values = values.reshape(PATCH, patch_cols, PATCH, channels).transpose(1, 0, 2, 3)
        return values.reshape(patch_cols * CELLS, channels)

    def finish(pr, _):
        rows = pl.ds(margin + pr * PATCH, PATCH)
        inner = slice(margin, margin + tile_cols)
        residual = by_patch(ext_ref[rows, inner, :] + mixed_ref[rows, inner, :])
        normed = normalize(residual, mlp_gain).astype(jnp.bfloat16)
        hidden = jax.nn.gelu(
            jnp.dot(normed, up_ref[...], preferred_element_type=jnp.float32)
        ).astype(jnp.bfloat16)
        latent = residual + jnp.dot(hidden, down_ref[...], preferred_element_type=jnp.float32)
        placed = latent.reshape(patch_cols, PATCH, PATCH, channels).transpose(1, 0, 2, 3)
        latent_ref[pl.ds(pr * PATCH, PATCH)] = placed.reshape(PATCH, tile_cols, channels).astype(
            jnp.bfloat16
        )
        latent = latent.astype(jnp.bfloat16)
        projected = jnp.dot(latent, decode_ref[...], preferred_element_type=jnp.float32)
        for pc in range(0, patch_cols, 2):
            turned = projected[pc * CELLS : pc * CELLS + LANES].T
            j = pr * (patch_cols // 2) + pc // 2
            proj_ref[pl.ds(pl.multiple_of(j * feat_width, 16), feat_width), :] = turned.astype(
                jnp.bfloat16
            )
        return 0

    lax.fori_loop(0, patch_rows, finish, 0, unroll=True)


def reply_patches(capacity, plane, tiles, feat_width, id_ref, *refs):
    tile_refs, out_ref, both_ref = refs[:tiles], refs[tiles], refs[tiles + 1]
    pairs = capacity // 2
    first = lax.broadcasted_iota(jnp.int32, (feat_width, LANES), 1) < CELLS
    for t in range(tiles):
        for j in range(both_ref.shape[1] // 2):
            pair = tile_refs[t][j * feat_width : (j + 1) * feat_width, :].astype(jnp.float32)
            swapped = pltpu.roll(pair, CELLS, 1)
            both_ref[t, 2 * j] = jnp.where(first, pair, swapped)
            both_ref[t, 2 * j + 1] = jnp.where(first, swapped, pair)
    for r in range(plane):
        for t in range(tiles):
            for k in range(pairs):
                slot = (r * tiles + t) * capacity + 2 * k
                pair = jnp.where(
                    first, both_ref[t, id_ref[slot]], both_ref[t, id_ref[slot + 1]]
                )
                at = ((r * tiles + t) * pairs + k) * feat_width
                out_ref[at : at + feat_width, :] = pair.astype(jnp.bfloat16)


def decode_blocks(slot_ref, offset_ref, *refs):
    pieces, out_ref, back_ref = refs[:-2], refs[-2], refs[-1]
    at = 0
    for piece in pieces:
        back_ref[at : at + piece.shape[0], :] = piece[...]
        at += piece.shape[0]
    feat_width, count = out_ref.shape
    blocks = count // BLK

    def one(b):
        slot = slot_ref[b]
        col = pl.multiple_of(b * BLK, BLK)
        weights = block_weights(offset_ref[:, pl.ds(col, BLK)].astype(jnp.float32))
        total = jnp.sum(weights.astype(jnp.float32), axis=0, keepdims=True)
        nothing = jnp.zeros_like(weights)
        low = slot % 2 == 0
        both = jnp.concatenate(
            [jnp.where(low, weights, nothing), jnp.where(low, nothing, weights)], axis=0
        )
        values = back_ref[pl.ds(pl.multiple_of(slot // 2 * feat_width, 16), feat_width), :]
        mean = jnp.dot(values, both, preferred_element_type=jnp.float32) * (1.0 / total)
        out_ref[:, pl.ds(col, BLK)] = mean.astype(jnp.bfloat16)

    unroll = 32 if blocks % 32 == 0 else 1

    def body(i, _):
        for u in range(unroll):
            one(i * unroll + u)
        return 0

    lax.fori_loop(0, blocks // unroll, body, 0)


def with_halo(array, sides, width):
    for axis, dim in sides:
        size, length = (axis_count(axis), array.shape[dim])
        up = [(i, (i + 1) % size) for i in range(size)]
        down = [(j, i) for i, j in up]
        last = lax.slice_in_dim(array, length - width, length, axis=dim)
        initial = lax.slice_in_dim(array, 0, width, axis=dim)
        before = lax.ppermute(last, axis, up)
        after = lax.ppermute(initial, axis, down)
        array = jnp.concatenate([before, array, after], axis=dim)
    return array


def axis_count(axes):
    axes = axes if isinstance(axes, tuple) else (axes,)
    return math.prod([lax.axis_size(axis) for axis in axes])


def swap_in_plane(arrays):
    plane = len(arrays)
    return arrays[:1] + [
        lax.ppermute(arrays[r], ("lat", "x"), [(i, i ^ r) for i in range(plane)])
        for r in range(1, plane)
    ]


def shift_planes(array, hop):
    depth = lax.axis_size("z")
    return lax.ppermute(array, "z", [(i, (i + hop) % depth) for i in range(depth)])


def local(
    obs_feat,
    obs_offset,
    block_tile,
    block_patch,
    embed_weight,
    grid_base,
    norm_gain,
    qkv_weight,
    out_weight,
    mlp_gain,
    up_weight,
    down_weight,
    decode_weight,
):
    lat, depth, width = (lax.axis_size(axis) for axis in ("lat", "z", "x"))
    plane, hops = lat * width, depth - 1
    devices = plane * depth
    feat_width, obs_count = obs_feat.shape
    blocks = obs_count // BLK
    capacity = max(2, 2 * blocks // devices)
    capacity += capacity % 2
    pairs = capacity // 2
    tile_rows, tile_cols, channels = grid_base.shape
    patch_total = (tile_rows // PATCH) * (tile_cols // PATCH)
    chunk = pairs * feat_width + meta_rows(pairs)
    dense = dense_rows(patch_total // 2, feat_width)
    lat_id = lax.axis_index("lat").astype(jnp.int32)
    place = jnp.stack(
        [lat_id * width + lax.axis_index("x"), lax.axis_index("z"), lat_id]
    ).astype(jnp.int32)

    send, slots = pl.pallas_call(
        lambda *refs: encode_blocks(capacity, (lat, depth, width), *refs),
        out_shape=(
            jax.ShapeDtypeStruct((devices * chunk, LANES), jnp.bfloat16),
            jax.ShapeDtypeStruct((blocks,), jnp.int32),
        ),
        in_specs=[smem(), smem(), smem(), vmem(), vmem()],
        out_specs=(vmem(), smem()),
        scratch_shapes=[pltpu.SMEM((devices,), jnp.int32)],
        compiler_params=params(8),
        name="encode_blocks",
    )(place, block_tile.reshape(blocks), block_patch, obs_feat, obs_offset)

    def cut(array, start, rows):
        return [
            lax.slice_in_dim(array, start + r * rows, start + (r + 1) * rows) for r in range(plane)
        ]

    def ids_of(pieces, tiles):
        at = pairs * feat_width + 2 * pairs
        tags = jnp.stack(
            [p.reshape(tiles, chunk, LANES)[:, at : at + pairs, 0::CELLS] for p in pieces]
        )
        ids = tags.astype(jnp.float32).astype(jnp.int32) - 1
        return jnp.clip(ids, 0, patch_total - 1).reshape(-1)

    far = swap_in_plane(cut(send, plane * chunk, hops * chunk))
    near = swap_in_plane(cut(send, 0, chunk))
    far_ids = ids_of(far, hops)
    sums = pl.pallas_call(
        lambda *refs: gather_planes(capacity, plane, hops, feat_width, *refs),
        out_shape=[jax.ShapeDtypeStruct((dense, LANES), jnp.bfloat16)] * hops,
        in_specs=[smem()] + [vmem()] * plane,
        out_specs=[vmem()] * hops,
        scratch_shapes=[pltpu.VMEM((hops, patch_total, feat_width + 8, LANES), jnp.float32)],
        compiler_params=params(8),
        name="gather_planes",
    )(far_ids, *far)
    parts = [shift_planes(sums[hop], hop + 1) for hop in range(hops)]
    near_ids = ids_of(near, 1)

    start = pl.pallas_call(
        lambda *refs: start_tile(capacity, plane, hops, *refs),
        out_shape=jax.ShapeDtypeStruct(grid_base.shape, jnp.bfloat16),
        in_specs=[smem()] + [vmem()] * (plane + hops + 2),
        out_specs=vmem(),
        scratch_shapes=[pltpu.VMEM((patch_total, feat_width + 8, LANES), jnp.float32)],
        compiler_params=params(8),
        name="start_tile",
    )(near_ids, *near, *parts, embed_weight, grid_base)

    margin = WIN // 2
    ext = with_halo(start, (("lat", 0), (("z", "x"), 1)), margin).astype(jnp.float32)
    ext_rows, ext_cols, _ = ext.shape
    padded = -(-ext_cols // (2 * WIN)) * LANES

    latent, projected = pl.pallas_call(
        lambda *refs: grid_block(tile_rows * lat, *refs),
        out_shape=(
            jax.ShapeDtypeStruct(grid_base.shape, jnp.bfloat16),
            jax.ShapeDtypeStruct((patch_total // 2 * feat_width, LANES), jnp.bfloat16),
        ),
        in_specs=[smem()] + [vmem()] * 8,
        out_specs=(vmem(), vmem()),
        scratch_shapes=[
            pltpu.VMEM((2 * channels, channels), jnp.bfloat16),
            pltpu.VMEM((padded, channels), jnp.bfloat16),
            pltpu.VMEM((2 * channels, padded), jnp.bfloat16),
            pltpu.VMEM((channels, padded), jnp.bfloat16),
            pltpu.VMEM((ext_rows, ext_cols, channels), jnp.float32),
            pltpu.VMEM((padded * channels // LANES // 128, WIN * WIN, 4 * LANES), jnp.float32),
            pltpu.VMEM((padded * channels // LANES // 128, LANES, 4 * LANES), jnp.bfloat16),
        ],
        compiler_params=params(20),
        name="grid_block",
    )(
        place,
        ext,
        norm_gain.reshape(1, channels),
        qkv_weight,
        out_weight,
        mlp_gain.reshape(1, channels),
        up_weight,
        down_weight,
        decode_weight,
    )

    def reply(ids, tiles, name):
        count = len(tiles)
        rows = count * pairs * feat_width
        out = pl.pallas_call(
            lambda *refs: reply_patches(capacity, plane, count, feat_width, *refs),
            out_shape=jax.ShapeDtypeStruct((plane * rows, LANES), jnp.bfloat16),
            in_specs=[smem()] + [vmem()] * count,
            out_specs=vmem(),
            scratch_shapes=[pltpu.VMEM((count, patch_total, feat_width, LANES), jnp.float32)],
            compiler_params=params(8),
            name=name,
        )(ids, *tiles)
        return swap_in_plane(cut(out, 0, rows))

    others = [shift_planes(projected, -hop) for hop in range(1, depth)]
    near_back = reply(near_ids, [projected], "reply_near")
    far_back = reply(far_ids, others, "reply_far")

    obs_out = pl.pallas_call(
        decode_blocks,
        out_shape=jax.ShapeDtypeStruct((feat_width, obs_count), jnp.bfloat16),
        in_specs=[smem(), vmem()] + [vmem()] * (2 * plane),
        out_specs=vmem(),
        scratch_shapes=[pltpu.VMEM((devices * pairs * feat_width, LANES), jnp.bfloat16)],
        compiler_params=params(10),
        name="decode_blocks",
    )(slots, obs_offset, *near_back, *far_back)
    return (latent, obs_out)


def solution(mesh):
    lat, lon = mesh.devices.shape
    width = lat // 2 if lat % 2 == 0 and lon % (lat // 2) == 0 else 1
    split = Mesh(mesh.devices.reshape(lat, lon // width, width), ("lat", "z", "x"))
    every = ("lat", "z", "x")
    placed = (
        P(None, every),
        P(None, every),
        P(every, None),
        P(every),
        P(),
        P("lat", ("z", "x"), None),
        P(),
        P(),
        P(),
        P(),
        P(),
        P(),
        P(),
    )
    return jax.shard_map(
        local,
        mesh=split,
        in_specs=placed,
        out_specs=(P("lat", ("z", "x"), None), P(None, every)),
        check_vma=False,
    )
```

```python
import math

import jax
import jax.numpy as jnp
from jax import lax
from jax.experimental import pallas as pl
from jax.experimental.pallas import tpu as pltpu
from jax.sharding import Mesh
from jax.sharding import PartitionSpec as P

HEAD_DIM = 32
WIN = 8
PATCH = 8
BLK = 128
CELLS = PATCH * PATCH
LANES = 2 * CELLS

epsilon = 1e-05
spread_coef = 0.5

NT = (((1,), (1,)), ((), ()))
TN = (((0,), (0,)), ((), ()))


def params(mib):
    return pltpu.CompilerParams(vmem_limit_bytes=mib * 1024 * 1024)


def vmem():
    return pl.BlockSpec(memory_space=pltpu.VMEM)


def smem():
    return pl.BlockSpec(memory_space=pltpu.SMEM)


def normalize(values, gain_row):
    center = jnp.mean(values, axis=-1, keepdims=True)
    centered = values - center
    variance = jnp.mean(centered * centered, axis=-1, keepdims=True)
    return centered * lax.rsqrt(variance + epsilon) * gain_row


def block_weights(offsets):
    axis_id = lax.broadcasted_iota(jnp.int32, (PATCH, BLK), 0).astype(jnp.float32) + 0.5
    row_gap = axis_id - offsets[0:1]
    col_gap = axis_id - offsets[1:2]
    row_gap = row_gap * row_gap
    col_gap = col_gap * col_gap
    total = row_gap[:, None, :] + col_gap[None, :, :]
    return jnp.exp(-spread_coef * total).reshape(CELLS, BLK).astype(jnp.bfloat16)


def meta_rows(pairs):
    return -(-3 * pairs // 16) * 16


def encode_blocks(
    capacity, shape, place_ref, tile_ref, patch_ref, feat_ref, offset_ref, near_ref, far_ref,
    slot_ref, send_ref, count_ref,
):
    lat, depth, width = shape
    plane = lat * width
    devices = plane * depth
    blocks = feat_ref.shape[1] // BLK
    feat_width = feat_ref.shape[0]
    pairs = capacity // 2
    meta = meta_rows(pairs)
    chunk = pairs * feat_width + meta
    send_ref[...] = jnp.zeros_like(send_ref)

    def clear(t, _):
        count_ref[t] = 0
        return 0

    lax.fori_loop(0, devices, clear, 0)
    lane_half = lax.broadcasted_iota(jnp.int32, (feat_width, LANES), 1) // CELLS
    meta_half = lax.broadcasted_iota(jnp.int32, (meta, LANES), 1) // CELLS
    meta_row = lax.broadcasted_iota(jnp.int32, (meta, LANES), 0)
    ones = jnp.ones((16, BLK), jnp.bfloat16)

    def one(b):
        tile = tile_ref[b]
        rank = count_ref[tile]
        count_ref[tile] = rank + 1
        lon = tile % (depth * width)
        partner = (tile // (depth * width) * width + lon % width)
        hop = (lon // width + depth - place_ref[1]) % depth
        piece = jnp.where(hop == 0, partner, plane + partner * (depth - 1) + hop - 1)
        slot_ref[b] = piece * capacity + rank
        pair = rank // 2
        half = rank % 2
        col = pl.multiple_of(b * BLK, BLK)
        feat = jnp.concatenate([feat_ref[:, pl.ds(col, BLK)], ones], axis=0)
        weights = block_weights(offset_ref[:, pl.ds(col, BLK)].astype(jnp.float32))
        twice = jnp.concatenate([weights, weights], axis=0)
        sums = lax.dot_general(feat, twice, NT, preferred_element_type=jnp.float32)
        row = pl.multiple_of(piece * chunk + pair * feat_width, 16)
        old = send_ref[pl.ds(row, feat_width), :].astype(jnp.float32)
        send_ref[pl.ds(row, feat_width), :] = jnp.where(
            lane_half == half, sums[:feat_width], old
        ).astype(jnp.bfloat16)
        mass = sums[feat_width : feat_width + 1]
        high = mass.astype(jnp.bfloat16).astype(jnp.float32)
        low = mass - high
        tag = (patch_ref[b] + 1).astype(jnp.float32)
        row = pl.multiple_of(piece * chunk + pairs * feat_width, 16)
        old = send_ref[pl.ds(row, meta), :].astype(jnp.float32)
        new = jnp.where(
            meta_row == pair,
            high,
            jnp.where(
                meta_row == pairs + pair, low, jnp.where(meta_row == 2 * pairs + pair, tag, old)
            ),
        )
        send_ref[pl.ds(row, meta), :] = jnp.where(meta_half == half, new, old).astype(jnp.bfloat16)

    unroll = 32 if blocks % 32 == 0 else 1

    def body(i, _):
        for u in range(unroll):
            one(i * unroll + u)
        return 0

    lax.fori_loop(0, blocks // unroll, body, 0)
    near_ref[...] = send_ref[: near_ref.shape[0]]
    far_ref[...] = send_ref[near_ref.shape[0] :]


def dense_rows(pairs, feat_width):
    return pairs * feat_width + -(-2 * pairs // 16) * 16


def add_chunk(capacity, feat_width, id_ref, slot, recv_ref, base, acc_ref):
    pairs = capacity // 2
    first = lax.broadcasted_iota(jnp.int32, (feat_width + 8, LANES), 1) < CELLS
    tags = recv_ref[base + pairs * feat_width : base + pairs * feat_width + meta_rows(pairs), :]
    tags = tags.astype(jnp.float32)
    for k in range(pairs):
        at = base + k * feat_width
        sums = recv_ref[at : at + feat_width, :].astype(jnp.float32)
        mass = tags[k : k + 1] + tags[pairs + k : pairs + k + 1]
        both = jnp.concatenate([sums, jnp.broadcast_to(mass, (8, LANES))], axis=0)
        acc_ref[id_ref[slot + 2 * k]] += jnp.where(first, both, 0.0)
        acc_ref[id_ref[slot + 2 * k + 1]] += jnp.where(first, 0.0, both)


def paired(acc_ref, j):
    first = lax.broadcasted_iota(jnp.int32, acc_ref.shape[1:], 1) < CELLS
    even, odd = acc_ref[2 * j], acc_ref[2 * j + 1]
    even, odd = even + pltpu.roll(even, CELLS, 1), odd + pltpu.roll(odd, CELLS, 1)
    return jnp.where(first, even, odd)


def gather_planes(capacity, plane, hops, feat_width, id_ref, recv_ref, *refs):
    outs, acc_ref = refs[:hops], refs[hops]
    pairs = capacity // 2
    chunk = pairs * feat_width + meta_rows(pairs)
    patch_pairs = acc_ref.shape[1] // 2
    acc_ref[...] = jnp.zeros_like(acc_ref)
    for r in range(plane):
        for hop in range(hops):
            n = r * hops + hop
            add_chunk(
                capacity, feat_width, id_ref, n * capacity, recv_ref, n * chunk, acc_ref.at[hop]
            )
    for hop in range(hops):
        masses = []
        for j in range(patch_pairs):
            pair = paired(acc_ref.at[hop], j)
            outs[hop][j * feat_width : (j + 1) * feat_width, :] = pair[:feat_width].astype(
                jnp.bfloat16
            )
            masses.append(pair[feat_width : feat_width + 1])
        masses = jnp.concatenate(masses, axis=0)
        high = masses.astype(jnp.bfloat16).astype(jnp.float32)
        spare = outs[hop].shape[0] - patch_pairs * (feat_width + 2)
        rows = [high, masses - high] + ([jnp.zeros((spare, LANES), jnp.float32)] if spare else [])
        outs[hop][patch_pairs * feat_width :, :] = jnp.concatenate(rows, axis=0).astype(jnp.bfloat16)


def start_tile(capacity, plane, hops, id_ref, recv_ref, *refs):
    parts = refs[:hops]
    embed_ref, base_ref, start_ref, acc_ref = refs[hops:]
    chunk = recv_ref.shape[0] // plane
    feat_width, channels = embed_ref.shape
    tile_rows, tile_cols, _ = base_ref.shape
    patch_rows, patch_cols = tile_rows // PATCH, tile_cols // PATCH
    patch_pairs = patch_rows * patch_cols // 2
    acc_ref[...] = jnp.zeros_like(acc_ref)
    for r in range(plane):
        add_chunk(capacity, feat_width, id_ref, r * capacity, recv_ref, r * chunk, acc_ref)
    embed = embed_ref[...]
    mass_rows = [part[patch_pairs * feat_width :, :].astype(jnp.float32) for part in parts]
    for pr in range(patch_rows):
        lifted = []
        for pc in range(patch_cols // 2):
            j = pr * (patch_cols // 2) + pc
            pair = paired(acc_ref, j)
            sums, mass = pair[:feat_width], pair[feat_width : feat_width + 1]
            for part, rows in zip(parts, mass_rows):
                sums = sums + part[j * feat_width : (j + 1) * feat_width, :].astype(jnp.float32)
                mass = mass + (rows[j : j + 1] + rows[patch_pairs + j : patch_pairs + j + 1])
            encoded = (sums * (1.0 / (1.0 + mass))).astype(jnp.bfloat16)
            lifted.append(lax.dot_general(encoded, embed, TN, preferred_element_type=jnp.float32))
        lifted = jnp.concatenate(lifted, axis=0).reshape(patch_cols, PATCH, PATCH, channels)
        lifted = lifted.transpose(1, 0, 2, 3).reshape(PATCH, tile_cols, channels)
        rows = slice(pr * PATCH, (pr + 1) * PATCH)
        start_ref[rows] = (base_ref[rows].astype(jnp.float32) + lifted).astype(jnp.bfloat16)


def grid_block(
    lat_cells, place_ref, ext_ref, norm_ref, qkv_ref, out_ref, mlp_ref,
    up_ref, down_ref, decode_ref, latent_ref, proj_ref, turned_ref, key_ref, pack_ref, att_ref,
    mixed_ref, score_ref, prob_ref,
):
    ext_rows, ext_cols, channels = ext_ref.shape
    tile_rows, tile_cols, _ = latent_ref.shape
    margin = WIN // 2
    win_rows, win_cols = ext_rows // WIN, ext_cols // WIN
    win_pairs = -(-win_cols // 2)
    patch_rows, patch_cols = tile_rows // PATCH, tile_cols // PATCH
    tokens = WIN * WIN
    group = 128
    heads = group // HEAD_DIM
    feat_width = decode_ref.shape[1]
    scale = HEAD_DIM ** (-0.5) / math.log(2.0)
    norm_gain = norm_ref[...]
    turned_ref[:channels] = qkv_ref[:, :channels].T
    turned_ref[channels:] = qkv_ref[:, 2 * channels :].T
    shape = (tokens, heads * LANES)
    own = lax.broadcasted_iota(jnp.int32, shape, 1) % LANES < tokens
    key_row = lax.broadcasted_iota(jnp.int32, (tokens, LANES), 0) // WIN
    query_row = lax.broadcasted_iota(jnp.int32, (tokens, LANES), 1) % tokens // WIN
    nothing = jnp.zeros(shape, jnp.bfloat16)
    empty = jnp.zeros((HEAD_DIM, LANES), jnp.bfloat16)

    def attend(wr):
        rows = pl.ds(wr * WIN, WIN)
        cells = ext_ref[rows].reshape(WIN, win_cols, WIN, channels).transpose(1, 0, 2, 3)
        normed = normalize(cells.reshape(win_cols * tokens, channels), norm_gain)
        normed = normed.astype(jnp.bfloat16)
        if win_cols % 2:
            normed = jnp.concatenate([normed, jnp.zeros((tokens, channels), jnp.bfloat16)], axis=0)
        key_ref[...] = jnp.dot(
            normed, qkv_ref[:, channels : 2 * channels], preferred_element_type=jnp.float32
        ).astype(jnp.bfloat16)
        pack_ref[...] = lax.dot_general(
            turned_ref[...], normed, NT, preferred_element_type=jnp.float32
        ).astype(jnp.bfloat16)
        edge = wr in (0, win_rows - 1)
        if edge:
            top = place_ref[2] * tile_rows - margin + wr * WIN
            side = lambda r: (r >= 0).astype(jnp.int32) + (r >= lat_cells).astype(jnp.int32)
            bias = jnp.where(side(top + key_row) == side(top + query_row), 0.0, -1e30)
            bias = jnp.concatenate([bias] * heads, axis=1)
        parts = [(p, g) for p in range(win_pairs) for g in range(channels // group)]
        for n, (p, g) in enumerate(parts):
            span = slice(p * LANES, (p + 1) * LANES)
            at = slice(g * group, (g + 1) * group)
            query = pack_ref[at, span]
            stack = jnp.concatenate(
                [
                    jnp.concatenate(
                        [
                            query[h * HEAD_DIM : (h + 1) * HEAD_DIM] if i == h else empty
                            for i in range(heads)
                        ],
                        axis=0,
                    )
                    for h in range(heads)
                ],
                axis=1,
            )
            scores = jnp.dot(key_ref[span, at], stack, preferred_element_type=jnp.float32)
            scores = jnp.where(own, scores[:tokens], scores[tokens:])
            score_ref[n] = scores + bias if edge else scores
        for n, (p, g) in enumerate(parts):
            scores = score_ref[n]
            peak = jnp.max(scores, axis=0, keepdims=True)
            raised = jnp.exp2((scores - peak) * scale)
            total = jnp.sum(raised, axis=0, keepdims=True)
            probs = (raised * (1.0 / total)).astype(jnp.bfloat16)
            prob_ref[n, :tokens] = jnp.where(own, probs, nothing)
            prob_ref[n, tokens:] = jnp.where(own, nothing, probs)
        for n, (p, g) in enumerate(parts):
            span = slice(p * LANES, (p + 1) * LANES)
            for h in range(0, heads, 2):
                at = g * group + h * HEAD_DIM
                both = jnp.dot(
                    pack_ref[channels + at : channels + at + 2 * HEAD_DIM, span],
                    prob_ref[n, :, h * LANES : (h + 2) * LANES],
                    preferred_element_type=jnp.float32,
                ).astype(jnp.bfloat16)
                att_ref[at : at + HEAD_DIM, span] = both[:HEAD_DIM, :LANES]
                att_ref[at + HEAD_DIM : at + 2 * HEAD_DIM, span] = both[HEAD_DIM:, LANES:]
        mixed = lax.dot_general(att_ref[...], out_ref[...], TN, preferred_element_type=jnp.float32)
        for w in range(win_cols):
            mixed_ref[rows, w * WIN : (w + 1) * WIN, :] = mixed[w * tokens : (w + 1) * tokens].reshape(
                WIN, WIN, channels
            )

    for wr in range(win_rows):
        attend(wr)
    mlp_gain = mlp_ref[...]

    def by_patch(values):
        values = values.reshape(PATCH, patch_cols, PATCH, channels).transpose(1, 0, 2, 3)
        return values.reshape(patch_cols * CELLS, channels)

    def finish(pr, _):
        rows = pl.ds(margin + pr * PATCH, PATCH)
        inner = slice(margin, margin + tile_cols)
        residual = by_patch(ext_ref[rows, inner, :] + mixed_ref[rows, inner, :])
        normed = normalize(residual, mlp_gain).astype(jnp.bfloat16)
        hidden = jax.nn.gelu(
            jnp.dot(normed, up_ref[...], preferred_element_type=jnp.float32)
        ).astype(jnp.bfloat16)
        latent = residual + jnp.dot(hidden, down_ref[...], preferred_element_type=jnp.float32)
        placed = latent.reshape(patch_cols, PATCH, PATCH, channels).transpose(1, 0, 2, 3)
        latent_ref[pl.ds(pr * PATCH, PATCH)] = placed.reshape(PATCH, tile_cols, channels).astype(
            jnp.bfloat16
        )
        latent = latent.astype(jnp.bfloat16)
        projected = jnp.dot(latent, decode_ref[...], preferred_element_type=jnp.float32)
        for pc in range(0, patch_cols, 2):
            turned = projected[pc * CELLS : pc * CELLS + LANES].T
            j = pr * (patch_cols // 2) + pc // 2
            proj_ref[pl.ds(pl.multiple_of(j * feat_width, 16), feat_width), :] = turned.astype(
                jnp.bfloat16
            )
        return 0

    lax.fori_loop(0, patch_rows, finish, 0, unroll=True)


def reply_patches(capacity, plane, tiles, feat_width, id_ref, *refs):
    tile_refs, out_ref, both_ref = refs[:tiles], refs[tiles], refs[tiles + 1]
    pairs = capacity // 2
    first = lax.broadcasted_iota(jnp.int32, (feat_width, LANES), 1) < CELLS
    for t in range(tiles):
        for j in range(both_ref.shape[1] // 2):
            pair = tile_refs[t][j * feat_width : (j + 1) * feat_width, :].astype(jnp.float32)
            swapped = pltpu.roll(pair, CELLS, 1)
            both_ref[t, 2 * j] = jnp.where(first, pair, swapped)
            both_ref[t, 2 * j + 1] = jnp.where(first, swapped, pair)
    for r in range(plane):
        for t in range(tiles):
            for k in range(pairs):
                slot = (r * tiles + t) * capacity + 2 * k
                pair = jnp.where(
                    first, both_ref[t, id_ref[slot]], both_ref[t, id_ref[slot + 1]]
                )
                at = ((r * tiles + t) * pairs + k) * feat_width
                out_ref[at : at + feat_width, :] = pair.astype(jnp.bfloat16)


def decode_blocks(slot_ref, offset_ref, *refs):
    pieces, out_ref, back_ref = refs[:-2], refs[-2], refs[-1]
    at = 0
    for piece in pieces:
        back_ref[at : at + piece.shape[0], :] = piece[...]
        at += piece.shape[0]
    feat_width, count = out_ref.shape
    blocks = count // BLK

    def one(b):
        slot = slot_ref[b]
        col = pl.multiple_of(b * BLK, BLK)
        weights = block_weights(offset_ref[:, pl.ds(col, BLK)].astype(jnp.float32))
        total = jnp.sum(weights.astype(jnp.float32), axis=0, keepdims=True)
        nothing = jnp.zeros_like(weights)
        low = slot % 2 == 0
        both = jnp.concatenate(
            [jnp.where(low, weights, nothing), jnp.where(low, nothing, weights)], axis=0
        )
        values = back_ref[pl.ds(pl.multiple_of(slot // 2 * feat_width, 16), feat_width), :]
        mean = jnp.dot(values, both, preferred_element_type=jnp.float32) * (1.0 / total)
        out_ref[:, pl.ds(col, BLK)] = mean.astype(jnp.bfloat16)

    unroll = 32 if blocks % 32 == 0 else 1

    def body(i, _):
        for u in range(unroll):
            one(i * unroll + u)
        return 0

    lax.fori_loop(0, blocks // unroll, body, 0)


def with_halo(array, sides, width):
    for axis, dim in sides:
        size, length = (axis_count(axis), array.shape[dim])
        up = [(i, (i + 1) % size) for i in range(size)]
        down = [(j, i) for i, j in up]
        last = lax.slice_in_dim(array, length - width, length, axis=dim)
        initial = lax.slice_in_dim(array, 0, width, axis=dim)
        before = lax.ppermute(last, axis, up)
        after = lax.ppermute(initial, axis, down)
        array = jnp.concatenate([before, array, after], axis=dim)
    return array


def axis_count(axes):
    axes = axes if isinstance(axes, tuple) else (axes,)
    return math.prod([lax.axis_size(axis) for axis in axes])


def swap_in_plane(array):
    plane = axis_count(("lat", "x"))
    parts = array.reshape(plane, -1, LANES)
    parts = lax.all_to_all(parts, ("lat", "x"), split_axis=0, concat_axis=0, tiled=True)
    return parts.reshape(array.shape)


def shift_planes(array, hop):
    depth = lax.axis_size("z")
    return lax.ppermute(array, "z", [(i, (i + hop) % depth) for i in range(depth)])


def local(
    obs_feat,
    obs_offset,
    block_tile,
    block_patch,
    embed_weight,
    grid_base,
    norm_gain,
    qkv_weight,
    out_weight,
    mlp_gain,
    up_weight,
    down_weight,
    decode_weight,
):
    lat, depth, width = (lax.axis_size(axis) for axis in ("lat", "z", "x"))
    plane, hops = lat * width, depth - 1
    devices = plane * depth
    feat_width, obs_count = obs_feat.shape
    blocks = obs_count // BLK
    capacity = max(2, 2 * blocks // devices)
    capacity += capacity % 2
    pairs = capacity // 2
    tile_rows, tile_cols, channels = grid_base.shape
    patch_total = (tile_rows // PATCH) * (tile_cols // PATCH)
    chunk = pairs * feat_width + meta_rows(pairs)
    dense = dense_rows(patch_total // 2, feat_width)
    lat_id = lax.axis_index("lat").astype(jnp.int32)
    place = jnp.stack(
        [lat_id * width + lax.axis_index("x"), lax.axis_index("z"), lat_id]
    ).astype(jnp.int32)

    send_near, send_far, slots = pl.pallas_call(
        lambda *refs: encode_blocks(capacity, (lat, depth, width), *refs),
        out_shape=(
            jax.ShapeDtypeStruct((plane * chunk, LANES), jnp.bfloat16),
            jax.ShapeDtypeStruct((plane * hops * chunk, LANES), jnp.bfloat16),
            jax.ShapeDtypeStruct((blocks,), jnp.int32),
        ),
        in_specs=[smem(), smem(), smem(), vmem(), vmem()],
        out_specs=(vmem(), vmem(), smem()),
        scratch_shapes=[
            pltpu.VMEM((devices * chunk, LANES), jnp.bfloat16),
            pltpu.SMEM((devices,), jnp.int32),
        ],
        compiler_params=params(10),
        name="encode_blocks",
    )(place, block_tile.reshape(blocks), block_patch, obs_feat, obs_offset)

    def ids_of(recv, tiles):
        at = pairs * feat_width + 2 * pairs
        tags = recv.reshape(plane * tiles, chunk, LANES)[:, at : at + pairs, 0::CELLS]
        ids = tags.astype(jnp.float32).astype(jnp.int32) - 1
        return jnp.clip(ids, 0, patch_total - 1).reshape(-1)

    far = swap_in_plane(send_far)
    far_ids = ids_of(far, hops)
    sums = pl.pallas_call(
        lambda *refs: gather_planes(capacity, plane, hops, feat_width, *refs),
        out_shape=[jax.ShapeDtypeStruct((dense, LANES), jnp.bfloat16)] * hops,
        in_specs=[smem(), vmem()],
        out_specs=[vmem()] * hops,
        scratch_shapes=[pltpu.VMEM((hops, patch_total, feat_width + 8, LANES), jnp.float32)],
        compiler_params=params(8),
        name="gather_planes",
    )(far_ids, far)
    send_near, sums = lax.optimization_barrier((send_near, sums))
    parts = [shift_planes(sums[hop], hop + 1) for hop in range(hops)]
    near = swap_in_plane(send_near)
    near_ids = ids_of(near, 1)

    start = pl.pallas_call(
        lambda *refs: start_tile(capacity, plane, hops, *refs),
        out_shape=jax.ShapeDtypeStruct(grid_base.shape, jnp.bfloat16),
        in_specs=[smem()] + [vmem()] * (hops + 3),
        out_specs=vmem(),
        scratch_shapes=[pltpu.VMEM((patch_total, feat_width + 8, LANES), jnp.float32)],
        compiler_params=params(8),
        name="start_tile",
    )(near_ids, near, *parts, embed_weight, grid_base)

    margin = WIN // 2
    ext = with_halo(start, (("lat", 0), (("z", "x"), 1)), margin).astype(jnp.float32)
    ext_rows, ext_cols, _ = ext.shape
    padded = -(-ext_cols // (2 * WIN)) * LANES

    latent, projected = pl.pallas_call(
        lambda *refs: grid_block(tile_rows * lat, *refs),
        out_shape=(
            jax.ShapeDtypeStruct(grid_base.shape, jnp.bfloat16),
            jax.ShapeDtypeStruct((patch_total // 2 * feat_width, LANES), jnp.bfloat16),
        ),
        in_specs=[smem()] + [vmem()] * 8,
        out_specs=(vmem(), vmem()),
        scratch_shapes=[
            pltpu.VMEM((2 * channels, channels), jnp.bfloat16),
            pltpu.VMEM((padded, channels), jnp.bfloat16),
            pltpu.VMEM((2 * channels, padded), jnp.bfloat16),
            pltpu.VMEM((channels, padded), jnp.bfloat16),
            pltpu.VMEM((ext_rows, ext_cols, channels), jnp.float32),
            pltpu.VMEM((padded * channels // LANES // 128, WIN * WIN, 4 * LANES), jnp.float32),
            pltpu.VMEM((padded * channels // LANES // 128, LANES, 4 * LANES), jnp.bfloat16),
        ],
        compiler_params=params(20),
        name="grid_block",
    )(
        place,
        ext,
        norm_gain.reshape(1, channels),
        qkv_weight,
        out_weight,
        mlp_gain.reshape(1, channels),
        up_weight,
        down_weight,
        decode_weight,
    )

    def reply(ids, tiles, name):
        count = len(tiles)
        rows = count * pairs * feat_width
        out = pl.pallas_call(
            lambda *refs: reply_patches(capacity, plane, count, feat_width, *refs),
            out_shape=jax.ShapeDtypeStruct((plane * rows, LANES), jnp.bfloat16),
            in_specs=[smem()] + [vmem()] * count,
            out_specs=vmem(),
            scratch_shapes=[pltpu.VMEM((count, patch_total, feat_width, LANES), jnp.float32)],
            compiler_params=params(8),
            name=name,
        )(ids, *tiles)
        return swap_in_plane(out)

    others = [shift_planes(projected, -hop) for hop in range(1, depth)]
    near_back = reply(near_ids, [projected], "reply_near")
    far_back = reply(far_ids, others, "reply_far")

    obs_out = pl.pallas_call(
        decode_blocks,
        out_shape=jax.ShapeDtypeStruct((feat_width, obs_count), jnp.bfloat16),
        in_specs=[smem(), vmem()] + [vmem()] * 2,
        out_specs=vmem(),
        scratch_shapes=[pltpu.VMEM((devices * pairs * feat_width, LANES), jnp.bfloat16)],
        compiler_params=params(10),
        name="decode_blocks",
    )(slots, obs_offset, near_back, far_back)
    return (latent, obs_out)


def solution(mesh):
    lat, lon = mesh.devices.shape
    width = lat // 2 if lat % 2 == 0 and lon % (lat // 2) == 0 else 1
    split = Mesh(mesh.devices.reshape(lat, lon // width, width), ("lat", "z", "x"))
    every = ("lat", "z", "x")
    placed = (
        P(None, every),
        P(None, every),
        P(every, None),
        P(every),
        P(),
        P("lat", ("z", "x"), None),
        P(),
        P(),
        P(),
        P(),
        P(),
        P(),
        P(),
    )
    return jax.shard_map(
        local,
        mesh=split,
        in_specs=placed,
        out_specs=(P("lat", ("z", "x"), None), P(None, every)),
        check_vma=False,
    )
```

```python
import math

import jax
import jax.numpy as jnp
from jax import lax
from jax.experimental import pallas as pl
from jax.experimental.pallas import tpu as pltpu
from jax.sharding import Mesh
from jax.sharding import PartitionSpec as P

HEAD_DIM = 32
WIN = 8
PATCH = 8
BLK = 128
CELLS = PATCH * PATCH
LANES = 2 * CELLS

epsilon = 1e-05
spread_coef = 0.5

NT = (((1,), (1,)), ((), ()))
TN = (((0,), (0,)), ((), ()))


def params(mib):
    return pltpu.CompilerParams(vmem_limit_bytes=mib * 1024 * 1024)


def vmem():
    return pl.BlockSpec(memory_space=pltpu.VMEM)


def smem():
    return pl.BlockSpec(memory_space=pltpu.SMEM)


def normalize(values, gain_row):
    center = jnp.mean(values, axis=-1, keepdims=True)
    centered = values - center
    variance = jnp.mean(centered * centered, axis=-1, keepdims=True)
    return centered * lax.rsqrt(variance + epsilon) * gain_row


def block_weights(offsets):
    axis_id = lax.broadcasted_iota(jnp.int32, (PATCH, BLK), 0).astype(jnp.float32) + 0.5
    row_gap = axis_id - offsets[0:1]
    col_gap = axis_id - offsets[1:2]
    row_gap = row_gap * row_gap
    col_gap = col_gap * col_gap
    total = row_gap[:, None, :] + col_gap[None, :, :]
    return jnp.exp(-spread_coef * total).reshape(CELLS, BLK).astype(jnp.bfloat16)


def meta_rows(pairs):
    return -(-3 * pairs // 16) * 16


def encode_blocks(
    capacity, shape, place_ref, tile_hbm, patch_hbm, feat_hbm, offset_hbm, near_ref, far_ref,
    slot_ref, send_ref, tile_ref, patch_ref, feat_ref, offset_ref, count_ref, sems,
):
    lat, depth, width = shape
    devices = lat * depth * width
    feat_width = feat_ref.shape[0]
    blocks = feat_ref.shape[1] // BLK
    step = sems.shape[0] - 3
    size = blocks // step
    pairs = capacity // 2
    meta = meta_rows(pairs)
    chunk = pairs * feat_width + meta
    small = [
        pltpu.make_async_copy(tile_hbm, tile_ref, sems.at[step]),
        pltpu.make_async_copy(patch_hbm, patch_ref, sems.at[step + 1]),
        pltpu.make_async_copy(offset_hbm, offset_ref, sems.at[step + 2]),
    ]
    large = []
    for i in range(step):
        span = pl.ds(i * size * BLK, size * BLK)
        large.append(pltpu.make_async_copy(feat_hbm.at[:, span], feat_ref.at[:, span], sems.at[i]))
    for copy in small + large:
        copy.start()
    send_ref[...] = jnp.zeros_like(send_ref)

    def clear(t, _):
        count_ref[t] = 0
        return 0

    lax.fori_loop(0, devices, clear, 0)
    lane_half = lax.broadcasted_iota(jnp.int32, (feat_width, LANES), 1) // CELLS
    meta_half = lax.broadcasted_iota(jnp.int32, (meta, LANES), 1) // CELLS
    meta_row = lax.broadcasted_iota(jnp.int32, (meta, LANES), 0)
    ones = jnp.ones((16, BLK), jnp.bfloat16)

    def one(b):
        tile = tile_ref[b]
        rank = count_ref[tile]
        count_ref[tile] = rank + 1
        lon = tile % (depth * width)
        partner = tile // (depth * width) * width + lon % width
        hop = (lon // width + depth - place_ref[1]) % depth
        piece = jnp.where(hop == 0, partner, lat * width + partner * (depth - 1) + hop - 1)
        slot_ref[b] = piece * capacity + rank
        pair = rank // 2
        half = rank % 2
        col = pl.multiple_of(b * BLK, BLK)
        feat = jnp.concatenate([feat_ref[:, pl.ds(col, BLK)], ones], axis=0)
        weights = block_weights(offset_ref[:, pl.ds(col, BLK)].astype(jnp.float32))
        twice = jnp.concatenate([weights, weights], axis=0)
        sums = lax.dot_general(feat, twice, NT, preferred_element_type=jnp.float32)
        row = pl.multiple_of(piece * chunk + pair * feat_width, 16)
        old = send_ref[pl.ds(row, feat_width), :].astype(jnp.float32)
        send_ref[pl.ds(row, feat_width), :] = jnp.where(
            lane_half == half, sums[:feat_width], old
        ).astype(jnp.bfloat16)
        mass = sums[feat_width : feat_width + 1]
        high = mass.astype(jnp.bfloat16).astype(jnp.float32)
        low = mass - high
        tag = (patch_ref[b] + 1).astype(jnp.float32)
        row = pl.multiple_of(piece * chunk + pairs * feat_width, 16)
        old = send_ref[pl.ds(row, meta), :].astype(jnp.float32)
        new = jnp.where(
            meta_row == pair,
            high,
            jnp.where(
                meta_row == pairs + pair, low, jnp.where(meta_row == 2 * pairs + pair, tag, old)
            ),
        )
        send_ref[pl.ds(row, meta), :] = jnp.where(meta_half == half, new, old).astype(jnp.bfloat16)

    for copy in small:
        copy.wait()
    for i in range(step):
        large[i].wait()
        for b in range(i * size, (i + 1) * size):
            one(b)
    near_ref[...] = send_ref[: near_ref.shape[0]]
    far_ref[...] = send_ref[near_ref.shape[0] :]


def dense_rows(pairs, feat_width):
    return pairs * feat_width + -(-2 * pairs // 16) * 16


def add_chunk(capacity, feat_width, id_ref, slot, recv_ref, base, acc_ref):
    pairs = capacity // 2
    first = lax.broadcasted_iota(jnp.int32, (feat_width + 8, LANES), 1) < CELLS
    tags = recv_ref[base + pairs * feat_width : base + pairs * feat_width + meta_rows(pairs), :]
    tags = tags.astype(jnp.float32)
    for k in range(pairs):
        at = base + k * feat_width
        sums = recv_ref[at : at + feat_width, :].astype(jnp.float32)
        mass = tags[k : k + 1] + tags[pairs + k : pairs + k + 1]
        both = jnp.concatenate([sums, jnp.broadcast_to(mass, (8, LANES))], axis=0)
        acc_ref[id_ref[slot + 2 * k]] += jnp.where(first, both, 0.0)
        acc_ref[id_ref[slot + 2 * k + 1]] += jnp.where(first, 0.0, both)


def paired(acc_ref, j):
    first = lax.broadcasted_iota(jnp.int32, acc_ref.shape[1:], 1) < CELLS
    even, odd = acc_ref[2 * j], acc_ref[2 * j + 1]
    even, odd = even + pltpu.roll(even, CELLS, 1), odd + pltpu.roll(odd, CELLS, 1)
    return jnp.where(first, even, odd)


def gather_planes(capacity, plane, hops, feat_width, id_ref, recv_ref, *refs):
    outs, acc_ref = refs[:hops], refs[hops]
    pairs = capacity // 2
    chunk = pairs * feat_width + meta_rows(pairs)
    patch_pairs = acc_ref.shape[1] // 2
    acc_ref[...] = jnp.zeros_like(acc_ref)
    for r in range(plane):
        for hop in range(hops):
            n = r * hops + hop
            add_chunk(
                capacity, feat_width, id_ref, n * capacity, recv_ref, n * chunk, acc_ref.at[hop]
            )
    for hop in range(hops):
        masses = []
        for j in range(patch_pairs):
            pair = paired(acc_ref.at[hop], j)
            outs[hop][j * feat_width : (j + 1) * feat_width, :] = pair[:feat_width].astype(
                jnp.bfloat16
            )
            masses.append(pair[feat_width : feat_width + 1])
        masses = jnp.concatenate(masses, axis=0)
        high = masses.astype(jnp.bfloat16).astype(jnp.float32)
        spare = outs[hop].shape[0] - patch_pairs * (feat_width + 2)
        rows = [high, masses - high] + ([jnp.zeros((spare, LANES), jnp.float32)] if spare else [])
        outs[hop][patch_pairs * feat_width :, :] = jnp.concatenate(rows, axis=0).astype(jnp.bfloat16)


def gather_own(capacity, plane, feat_width, id_ref, recv_ref, own_ref, acc_ref):
    chunk = recv_ref.shape[0] // plane
    acc_ref[...] = jnp.zeros_like(acc_ref)
    for r in range(plane):
        add_chunk(capacity, feat_width, id_ref, r * capacity, recv_ref, r * chunk, acc_ref)
    for j in range(own_ref.shape[0]):
        own_ref[j] = paired(acc_ref, j)


def start_tile(hops, own_ref, *refs):
    parts = refs[:hops]
    embed_ref, base_ref, start_ref = refs[hops:]
    feat_width, channels = embed_ref.shape
    tile_rows, tile_cols, _ = base_ref.shape
    patch_rows, patch_cols = tile_rows // PATCH, tile_cols // PATCH
    patch_pairs = patch_rows * patch_cols // 2
    embed = embed_ref[...]
    mass_rows = [part[patch_pairs * feat_width :, :].astype(jnp.float32) for part in parts]
    for pr in range(patch_rows):
        lifted = []
        for pc in range(patch_cols // 2):
            j = pr * (patch_cols // 2) + pc
            pair = own_ref[j]
            sums, mass = pair[:feat_width], pair[feat_width : feat_width + 1]
            for part, rows in zip(parts, mass_rows):
                sums = sums + part[j * feat_width : (j + 1) * feat_width, :].astype(jnp.float32)
                mass = mass + (rows[j : j + 1] + rows[patch_pairs + j : patch_pairs + j + 1])
            encoded = (sums * (1.0 / (1.0 + mass))).astype(jnp.bfloat16)
            lifted.append(lax.dot_general(encoded, embed, TN, preferred_element_type=jnp.float32))
        lifted = jnp.concatenate(lifted, axis=0).reshape(patch_cols, PATCH, PATCH, channels)
        lifted = lifted.transpose(1, 0, 2, 3).reshape(PATCH, tile_cols, channels)
        rows = slice(pr * PATCH, (pr + 1) * PATCH)
        start_ref[rows] = (base_ref[rows].astype(jnp.float32) + lifted).astype(jnp.bfloat16)


def turn_weights(qkv_ref, turned_ref):
    channels = qkv_ref.shape[0]
    turned_ref[:channels] = qkv_ref[:, :channels].T
    turned_ref[channels:] = qkv_ref[:, 2 * channels :].T


def attend(
    cells_ref, windows, side, norm_gain, qkv_ref, out_ref, turned_ref, key_ref, pack_ref, att_ref,
    score_ref, prob_ref,
):
    channels = qkv_ref.shape[0]
    tokens = WIN * WIN
    group = 128
    heads = group // HEAD_DIM
    count = -(-len(windows) // 2)
    size = count * LANES
    scale = HEAD_DIM ** (-0.5) / math.log(2.0)
    shape = (tokens, heads * LANES)
    own = lax.broadcasted_iota(jnp.int32, shape, 1) % LANES < tokens
    nothing = jnp.zeros(shape, jnp.bfloat16)
    empty = jnp.zeros((HEAD_DIM, LANES), jnp.bfloat16)
    cells = jnp.concatenate(
        [
            cells_ref[row : row + WIN, col : col + WIN, :].reshape(tokens, channels)
            for row, col in windows
        ],
        axis=0,
    )
    normed = normalize(cells, norm_gain).astype(jnp.bfloat16)
    if len(windows) % 2:
        normed = jnp.concatenate([normed, jnp.zeros((tokens, channels), jnp.bfloat16)], axis=0)
    key_ref[:size] = jnp.dot(
        normed, qkv_ref[:, channels : 2 * channels], preferred_element_type=jnp.float32
    ).astype(jnp.bfloat16)
    pack_ref[:, :size] = lax.dot_general(
        turned_ref[...], normed, NT, preferred_element_type=jnp.float32
    ).astype(jnp.bfloat16)
    if side is not None:
        key_row = lax.broadcasted_iota(jnp.int32, (tokens, LANES), 0) // WIN
        query_row = lax.broadcasted_iota(jnp.int32, (tokens, LANES), 1) % tokens // WIN
        bias = jnp.where(side(key_row) == side(query_row), 0.0, -1e30)
        bias = jnp.concatenate([bias] * heads, axis=1)
    parts = [(p, g) for p in range(count) for g in range(channels // group)]
    for n, (p, g) in enumerate(parts):
        span = slice(p * LANES, (p + 1) * LANES)
        at = slice(g * group, (g + 1) * group)
        query = pack_ref[at, span]
        stack = jnp.concatenate(
            [
                jnp.concatenate(
                    [
                        query[h * HEAD_DIM : (h + 1) * HEAD_DIM] if i == h else empty
                        for i in range(heads)
                    ],
                    axis=0,
                )
                for h in range(heads)
            ],
            axis=1,
        )
        scores = jnp.dot(key_ref[span, at], stack, preferred_element_type=jnp.float32)
        scores = jnp.where(own, scores[:tokens], scores[tokens:])
        score_ref[n] = scores if side is None else scores + bias
    for n in range(len(parts)):
        scores = score_ref[n]
        peak = jnp.max(scores, axis=0, keepdims=True)
        raised = jnp.exp2((scores - peak) * scale)
        total = jnp.sum(raised, axis=0, keepdims=True)
        probs = (raised * (1.0 / total)).astype(jnp.bfloat16)
        prob_ref[n, :tokens] = jnp.where(own, probs, nothing)
        prob_ref[n, tokens:] = jnp.where(own, nothing, probs)
    for n, (p, g) in enumerate(parts):
        span = slice(p * LANES, (p + 1) * LANES)
        for h in range(0, heads, 2):
            at = g * group + h * HEAD_DIM
            both = jnp.dot(
                pack_ref[channels + at : channels + at + 2 * HEAD_DIM, span],
                prob_ref[n, :, h * LANES : (h + 2) * LANES],
                preferred_element_type=jnp.float32,
            ).astype(jnp.bfloat16)
            att_ref[at : at + HEAD_DIM, span] = both[:HEAD_DIM, :LANES]
            att_ref[at + HEAD_DIM : at + 2 * HEAD_DIM, span] = both[HEAD_DIM:, LANES:]
    mixed = lax.dot_general(
        att_ref[:, :size], out_ref[...], TN, preferred_element_type=jnp.float32
    )
    return [
        mixed[w * tokens : (w + 1) * tokens].reshape(WIN, WIN, channels)
        for w in range(len(windows))
    ]


def finish(begun, mixed, mlp_gain, up_ref, down_ref, decode_ref):
    residual = jnp.concatenate([a.reshape(CELLS, -1) + b.reshape(CELLS, -1) for a, b in zip(begun, mixed)])
    normed = normalize(residual, mlp_gain).astype(jnp.bfloat16)
    hidden = jax.nn.gelu(jnp.dot(normed, up_ref[...], preferred_element_type=jnp.float32))
    latent = residual + jnp.dot(
        hidden.astype(jnp.bfloat16), down_ref[...], preferred_element_type=jnp.float32
    )
    projected = jnp.dot(
        latent.astype(jnp.bfloat16), decode_ref[...], preferred_element_type=jnp.float32
    )
    turned = [
        projected[i * CELLS : i * CELLS + LANES].T.astype(jnp.bfloat16)
        for i in range(0, len(begun), 2)
    ]
    return latent, turned


def patch_order(patch_rows, patch_cols):
    inner = lambda r, c: 0 < r < patch_rows - 1 and 0 < c < patch_cols - 1
    every = [(r, c) for r in range(patch_rows) for c in range(patch_cols)]
    first = [at for at in every if inner(*at)]
    sides = [at for at in every if 0 < at[0] < patch_rows - 1 and not inner(*at)]
    ends = [at for at in every if not 0 < at[0] < patch_rows - 1]
    return first, sides, ends


def inner_block(
    start_ref, norm_ref, qkv_ref, out_ref, mlp_ref, up_ref, down_ref, decode_ref, latent_ref,
    proj_ref, mixed_ref, cells_ref, turned_ref, key_ref, pack_ref, att_ref, score_ref, prob_ref,
):
    tile_rows, tile_cols, channels = cells_ref.shape
    margin = WIN // 2
    feat_width = decode_ref.shape[1]
    cells_ref[...] = start_ref[...].astype(jnp.float32)
    turn_weights(qkv_ref, turned_ref)
    for row in range(0, tile_rows - WIN, WIN):
        cols = range(0, tile_cols - WIN, WIN)
        mixed = attend(
            cells_ref, [(row + margin, col + margin) for col in cols], None, norm_ref[...],
            qkv_ref, out_ref, turned_ref, key_ref, pack_ref, att_ref, score_ref, prob_ref,
        )
        for col, block in zip(cols, mixed):
            mixed_ref[row : row + WIN, col : col + WIN, :] = block
    first, _, _ = patch_order(tile_rows // PATCH, tile_cols // PATCH)
    done = 0
    for pr in sorted(set(r for r, _ in first)):
        here = [c for r, c in first if r == pr]
        row = pr * PATCH
        latent, turned = finish(
            [cells_ref[row : row + PATCH, c * PATCH : (c + 1) * PATCH, :] for c in here],
            [
                mixed_ref[
                    row - margin : row - margin + PATCH,
                    c * PATCH - margin : c * PATCH - margin + PATCH,
                    :,
                ]
                for c in here
            ],
            mlp_ref[...], up_ref, down_ref, decode_ref,
        )
        placed = latent.reshape(len(here), PATCH, PATCH, channels).transpose(1, 0, 2, 3)
        latent_ref[row - PATCH : row] = placed.reshape(PATCH, len(here) * PATCH, channels).astype(
            jnp.bfloat16
        )
        for pair in turned:
            proj_ref[done : done + feat_width, :] = pair
            done += feat_width


def outer_block(
    lat_cells, place_ref, ext_ref, inner_latent_ref, inner_proj_ref, inner_mixed_ref, norm_ref, qkv_ref, out_ref,
    mlp_ref, up_ref, down_ref, decode_ref, latent_ref, proj_ref, mixed_ref, turned_ref, key_ref,
    pack_ref, att_ref, score_ref, prob_ref,
):
    ext_rows, ext_cols, channels = ext_ref.shape
    tile_rows, tile_cols, _ = latent_ref.shape
    margin = WIN // 2
    feat_width = decode_ref.shape[1]
    last_row, last_col = ext_rows - WIN, ext_cols - WIN
    top = place_ref[2] * tile_rows - margin
    turn_weights(qkv_ref, turned_ref)

    def place(windows, side):
        mixed = attend(
            ext_ref, windows, side, norm_ref[...], qkv_ref, out_ref, turned_ref, key_ref,
            pack_ref, att_ref, score_ref, prob_ref,
        )
        for (row, col), block in zip(windows, mixed):
            mixed_ref[row : row + WIN, col : col + WIN, :] = block

    for row in (0, last_row):
        side = lambda r: (top + row + r >= 0).astype(jnp.int32) + (
            top + row + r >= lat_cells
        ).astype(jnp.int32)
        place([(row, col) for col in range(0, ext_cols, WIN)], side)
    place([(row, col) for row in range(WIN, last_row, WIN) for col in (0, last_col)], None)
    mixed_ref[WIN:last_row, WIN:last_col, :] = inner_mixed_ref[...]
    _, sides, ends = patch_order(tile_rows // PATCH, tile_cols // PATCH)
    done = inner_proj_ref.shape[0]
    proj_ref[:done, :] = inner_proj_ref[...]

    def patches(here):
        at = [
            (
                slice(r * PATCH + margin, (r + 1) * PATCH + margin),
                slice(c * PATCH + margin, (c + 1) * PATCH + margin),
            )
            for r, c in here
        ]
        latent, turned = finish(
            [ext_ref[r, c, :] for r, c in at],
            [mixed_ref[r, c, :] for r, c in at],
            mlp_ref[...], up_ref, down_ref, decode_ref,
        )
        for i, pair in enumerate(turned):
            at = done + i * feat_width
            proj_ref[at : at + feat_width, :] = pair
        return latent.reshape(len(here), PATCH, PATCH, channels), len(turned) * feat_width

    latent, used = patches(sides)
    done += used
    for pr in sorted(set(r for r, _ in sides)):
        left, right = [latent[i] for i, (r, _) in enumerate(sides) if r == pr]
        inner = inner_latent_ref[(pr - 1) * PATCH : pr * PATCH].astype(jnp.float32)
        whole = jnp.concatenate([left, inner, right], axis=1)
        latent_ref[pr * PATCH : (pr + 1) * PATCH] = whole.astype(jnp.bfloat16)
    for pr in sorted(set(r for r, _ in ends)):
        latent, used = patches([at for at in ends if at[0] == pr])
        done += used
        placed = latent.transpose(1, 0, 2, 3).reshape(PATCH, tile_cols, channels)
        latent_ref[pr * PATCH : (pr + 1) * PATCH] = placed.astype(jnp.bfloat16)


def reply_patches(capacity, plane, tiles, order, feat_width, id_ref, *refs):
    tile_refs, out_ref, both_ref = refs[:tiles], refs[tiles], refs[tiles + 1]
    pairs = capacity // 2
    first = lax.broadcasted_iota(jnp.int32, (feat_width, LANES), 1) < CELLS
    for t in range(tiles):
        for i in range(0, len(order), 2):
            at = i // 2 * feat_width
            pair = tile_refs[t][at : at + feat_width, :].astype(jnp.float32)
            swapped = pltpu.roll(pair, CELLS, 1)
            both_ref[t, order[i]] = jnp.where(first, pair, swapped)
            both_ref[t, order[i + 1]] = jnp.where(first, swapped, pair)
    for r in range(plane):
        for t in range(tiles):
            for k in range(pairs):
                slot = (r * tiles + t) * capacity + 2 * k
                pair = jnp.where(
                    first, both_ref[t, id_ref[slot]], both_ref[t, id_ref[slot + 1]]
                )
                at = ((r * tiles + t) * pairs + k) * feat_width
                out_ref[at : at + feat_width, :] = pair.astype(jnp.bfloat16)


def decode_blocks(slot_ref, offset_ref, near_ref, far_ref, out_ref, back_ref):
    back_ref[: near_ref.shape[0], :] = near_ref[...]
    back_ref[near_ref.shape[0] :, :] = far_ref[...]
    feat_width, count = out_ref.shape
    blocks = count // BLK

    def one(b):
        slot = slot_ref[b]
        col = pl.multiple_of(b * BLK, BLK)
        weights = block_weights(offset_ref[:, pl.ds(col, BLK)].astype(jnp.float32))
        total = jnp.sum(weights.astype(jnp.float32), axis=0, keepdims=True)
        nothing = jnp.zeros_like(weights)
        low = slot % 2 == 0
        both = jnp.concatenate(
            [jnp.where(low, weights, nothing), jnp.where(low, nothing, weights)], axis=0
        )
        values = back_ref[pl.ds(pl.multiple_of(slot // 2 * feat_width, 16), feat_width), :]
        mean = jnp.dot(values, both, preferred_element_type=jnp.float32) * (1.0 / total)
        out_ref[:, pl.ds(col, BLK)] = mean.astype(jnp.bfloat16)

    unroll = 32 if blocks % 32 == 0 else 1

    def body(i, _):
        for u in range(unroll):
            one(i * unroll + u)
        return 0

    lax.fori_loop(0, blocks // unroll, body, 0)


def with_halo(array, sides, width):
    for axis, dim in sides:
        size, length = (axis_count(axis), array.shape[dim])
        up = [(i, (i + 1) % size) for i in range(size)]
        down = [(j, i) for i, j in up]
        last = lax.slice_in_dim(array, length - width, length, axis=dim)
        initial = lax.slice_in_dim(array, 0, width, axis=dim)
        before = lax.ppermute(last, axis, up)
        after = lax.ppermute(initial, axis, down)
        array = jnp.concatenate([before, array, after], axis=dim)
    return array


def axis_count(axes):
    axes = axes if isinstance(axes, tuple) else (axes,)
    return math.prod([lax.axis_size(axis) for axis in axes])


def swap_in_plane(array):
    plane = axis_count(("lat", "x"))
    parts = array.reshape(plane, -1, LANES)
    parts = lax.all_to_all(parts, ("lat", "x"), split_axis=0, concat_axis=0, tiled=True)
    return parts.reshape(array.shape)


def swap_at_once(gains, array):
    def apart(array):
        lat, width = lax.axis_size("lat"), lax.axis_size("x")
        parts = array.reshape(lat, width, -1, LANES)
        for dim, axis in enumerate(("lat", "x")):
            parts = lax.all_to_all(parts, axis, split_axis=dim, concat_axis=dim, tiled=True)
        return parts.reshape(array.shape)

    return lax.cond(gains[0] > 0.0, swap_in_plane, apart, array)


def shift_planes(array, hop):
    depth = lax.axis_size("z")
    return lax.ppermute(array, "z", [(i, (i + hop) % depth) for i in range(depth)])


def local(
    obs_feat,
    obs_offset,
    block_tile,
    block_patch,
    embed_weight,
    grid_base,
    norm_gain,
    qkv_weight,
    out_weight,
    mlp_gain,
    up_weight,
    down_weight,
    decode_weight,
):
    lat, depth, width = (lax.axis_size(axis) for axis in ("lat", "z", "x"))
    plane, hops = lat * width, depth - 1
    devices = plane * depth
    feat_width, obs_count = obs_feat.shape
    blocks = obs_count // BLK
    capacity = max(2, 2 * blocks // devices)
    capacity += capacity % 2
    pairs = capacity // 2
    tile_rows, tile_cols, channels = grid_base.shape
    patch_total = (tile_rows // PATCH) * (tile_cols // PATCH)
    chunk = pairs * feat_width + meta_rows(pairs)
    dense = dense_rows(patch_total // 2, feat_width)
    lat_id = lax.axis_index("lat").astype(jnp.int32)
    place = jnp.stack(
        [lat_id * width + lax.axis_index("x"), lax.axis_index("z"), lat_id]
    ).astype(jnp.int32)

    steps = 3 if blocks % 3 == 0 else 1
    send_near, send_far, slots = pl.pallas_call(
        lambda *refs: encode_blocks(capacity, (lat, depth, width), *refs),
        out_shape=(
            jax.ShapeDtypeStruct((plane * chunk, LANES), jnp.bfloat16),
            jax.ShapeDtypeStruct((plane * hops * chunk, LANES), jnp.bfloat16),
            jax.ShapeDtypeStruct((blocks,), jnp.int32),
        ),
        in_specs=[smem()] + [pl.BlockSpec(memory_space=pltpu.HBM)] * 4,
        out_specs=(vmem(), vmem(), smem()),
        scratch_shapes=[
            pltpu.VMEM((devices * chunk, LANES), jnp.bfloat16),
            pltpu.SMEM((blocks,), jnp.int32),
            pltpu.SMEM((blocks,), jnp.int32),
            pltpu.VMEM(obs_feat.shape, jnp.bfloat16),
            pltpu.VMEM(obs_offset.shape, jnp.bfloat16),
            pltpu.SMEM((devices,), jnp.int32),
            pltpu.SemaphoreType.DMA((steps + 3,)),
        ],
        compiler_params=params(10),
        name="encode_blocks",
    )(place, block_tile.reshape(blocks), block_patch, obs_feat, obs_offset)

    def ids_of(recv, tiles):
        at = pairs * feat_width + 2 * pairs
        tags = recv.reshape(plane * tiles, chunk, LANES)[:, at : at + pairs, 0::CELLS]
        ids = tags.astype(jnp.float32).astype(jnp.int32) - 1
        return jnp.clip(ids, 0, patch_total - 1).reshape(-1)

    far = swap_in_plane(send_far)
    far_ids = ids_of(far, hops)
    sums = pl.pallas_call(
        lambda *refs: gather_planes(capacity, plane, hops, feat_width, *refs),
        out_shape=[jax.ShapeDtypeStruct((dense, LANES), jnp.bfloat16)] * hops,
        in_specs=[smem(), vmem()],
        out_specs=[vmem()] * hops,
        scratch_shapes=[pltpu.VMEM((hops, patch_total, feat_width + 8, LANES), jnp.float32)],
        compiler_params=params(10),
        name="gather_planes",
    )(far_ids, far)
    parts = [shift_planes(sums[hop], hop + 1) for hop in range(hops)]
    send_near, _ = lax.optimization_barrier((send_near, sums))
    near = swap_at_once(norm_gain, send_near)
    near_ids = ids_of(near, 1)
    own = pl.pallas_call(
        lambda *refs: gather_own(capacity, plane, feat_width, *refs),
        out_shape=jax.ShapeDtypeStruct((patch_total // 2, feat_width + 8, LANES), jnp.float32),
        in_specs=[smem(), vmem()],
        out_specs=vmem(),
        scratch_shapes=[pltpu.VMEM((patch_total, feat_width + 8, LANES), jnp.float32)],
        compiler_params=params(10),
        cost_estimate=pl.CostEstimate(flops=10**9, bytes_accessed=10**7, transcendentals=0),
        name="gather_own",
    )(near_ids, near)

    start = pl.pallas_call(
        lambda *refs: start_tile(hops, *refs),
        out_shape=jax.ShapeDtypeStruct(grid_base.shape, jnp.bfloat16),
        in_specs=[vmem()] * (hops + 3),
        out_specs=vmem(),
        compiler_params=params(10),
        name="start_tile",
    )(own, *parts, embed_weight, grid_base)

    margin = WIN // 2
    ext = with_halo(start, (("lat", 0), (("z", "x"), 1)), margin).astype(jnp.float32)
    ext_rows, ext_cols, _ = ext.shape
    group = 128
    gains = (norm_gain.reshape(1, channels), mlp_gain.reshape(1, channels))
    weights = (gains[0], qkv_weight, out_weight, gains[1], up_weight, down_weight, decode_weight)
    patch_rows, patch_cols = tile_rows // PATCH, tile_cols // PATCH
    inner, sides, ends = patch_order(patch_rows, patch_cols)
    order = [r * patch_cols + c for r, c in inner + sides + ends]
    inner_cells = (tile_rows - 2 * PATCH, tile_cols - 2 * PATCH, channels)
    inner_mixed = (tile_rows - WIN, tile_cols - WIN, channels)

    def scratch(windows):
        count = -(-windows // 2)
        parts = count * channels // group
        lanes = group // HEAD_DIM * LANES
        return [
            pltpu.VMEM((2 * channels, channels), jnp.bfloat16),
            pltpu.VMEM((count * LANES, channels), jnp.bfloat16),
            pltpu.VMEM((2 * channels, count * LANES), jnp.bfloat16),
            pltpu.VMEM((channels, count * LANES), jnp.bfloat16),
            pltpu.VMEM((parts, WIN * WIN, lanes), jnp.float32),
            pltpu.VMEM((parts, LANES, lanes), jnp.bfloat16),
        ]

    latent_inner, proj_inner, mixed_inner = pl.pallas_call(
        inner_block,
        out_shape=(
            jax.ShapeDtypeStruct(inner_cells, jnp.bfloat16),
            jax.ShapeDtypeStruct((len(inner) // 2 * feat_width, LANES), jnp.bfloat16),
            jax.ShapeDtypeStruct(inner_mixed, jnp.float32),
        ),
        in_specs=[vmem()] * 8,
        out_specs=(vmem(), vmem(), vmem()),
        scratch_shapes=[pltpu.VMEM(grid_base.shape, jnp.float32)]
        + scratch(tile_cols // WIN - 1),
        compiler_params=params(16),
        cost_estimate=pl.CostEstimate(flops=6 * 10**9, bytes_accessed=10**7, transcendentals=0),
        name="inner_block",
    )(start, *weights)

    latent, projected = pl.pallas_call(
        lambda *refs: outer_block(tile_rows * lat, *refs),
        out_shape=(
            jax.ShapeDtypeStruct(grid_base.shape, jnp.bfloat16),
            jax.ShapeDtypeStruct((patch_total // 2 * feat_width, LANES), jnp.bfloat16),
        ),
        in_specs=[smem()] + [vmem()] * 11,
        out_specs=(vmem(), vmem()),
        scratch_shapes=[pltpu.VMEM((ext_rows, ext_cols, channels), jnp.float32)]
        + scratch(max(ext_cols // WIN, 2 * (ext_rows // WIN - 2))),
        compiler_params=params(20),
        cost_estimate=pl.CostEstimate(flops=8 * 10**9, bytes_accessed=10**7, transcendentals=0),
        name="outer_block",
    )(place, ext, latent_inner, proj_inner, mixed_inner, *weights)

    def reply(ids, tiles, name):
        count = len(tiles)
        return pl.pallas_call(
            lambda *refs: reply_patches(capacity, plane, count, order, feat_width, *refs),
            out_shape=jax.ShapeDtypeStruct(
                (plane * count * pairs * feat_width, LANES), jnp.bfloat16
            ),
            in_specs=[smem()] + [vmem()] * count,
            out_specs=vmem(),
            scratch_shapes=[pltpu.VMEM((count, patch_total, feat_width, LANES), jnp.float32)],
            compiler_params=params(12),
            cost_estimate=pl.CostEstimate(flops=10**9, bytes_accessed=10**7, transcendentals=0),
            name=name,
        )(ids, *tiles)

    others = [shift_planes(projected, -hop) for hop in range(1, depth)]
    near_reply = reply(near_ids, [projected], "reply_near")
    near_back = swap_at_once(norm_gain, near_reply)
    far_back = swap_in_plane(reply(far_ids, others, "reply_far"))

    obs_out = pl.pallas_call(
        decode_blocks,
        out_shape=jax.ShapeDtypeStruct((feat_width, obs_count), jnp.bfloat16),
        in_specs=[smem(), vmem()] + [vmem()] * 2,
        out_specs=vmem(),
        scratch_shapes=[pltpu.VMEM((devices * pairs * feat_width, LANES), jnp.bfloat16)],
        compiler_params=params(10),
        name="decode_blocks",
    )(slots, obs_offset, near_back, far_back)
    return (latent, obs_out)


def solution(mesh):
    lat, lon = mesh.devices.shape
    width = lat // 2 if lat % 2 == 0 and lon % (lat // 2) == 0 else 1
    split = Mesh(mesh.devices.reshape(lat, lon // width, width), ("lat", "z", "x"))
    every = ("lat", "z", "x")
    placed = (
        P(None, every),
        P(None, every),
        P(every, None),
        P(every),
        P(),
        P("lat", ("z", "x"), None),
        P(),
        P(),
        P(),
        P(),
        P(),
        P(),
        P(),
    )
    return jax.shard_map(
        local,
        mesh=split,
        in_specs=placed,
        out_specs=(P("lat", ("z", "x"), None), P(None, every)),
        check_vma=False,
    )
```

```python
import math

import jax
import jax.numpy as jnp
from jax import lax
from jax.experimental import pallas as pl
from jax.experimental.pallas import tpu as pltpu
from jax.sharding import Mesh
from jax.sharding import PartitionSpec as P

HEAD_DIM = 32
WIN = 8
PATCH = 8
BLK = 128
CELLS = PATCH * PATCH
LANES = 2 * CELLS

epsilon = 1e-05
spread_coef = 0.5

NT = (((1,), (1,)), ((), ()))
TN = (((0,), (0,)), ((), ()))


def params(mib):
    return pltpu.CompilerParams(vmem_limit_bytes=mib * 1024 * 1024)


def vmem():
    return pl.BlockSpec(memory_space=pltpu.VMEM)


def smem():
    return pl.BlockSpec(memory_space=pltpu.SMEM)


def normalize(values, gain_row):
    center = jnp.mean(values, axis=-1, keepdims=True)
    centered = values - center
    variance = jnp.mean(centered * centered, axis=-1, keepdims=True)
    return centered * lax.rsqrt(variance + epsilon) * gain_row


def block_weights(offsets):
    axis_id = lax.broadcasted_iota(jnp.int32, (PATCH, BLK), 0).astype(jnp.float32) + 0.5
    row_gap = axis_id - offsets[0:1]
    col_gap = axis_id - offsets[1:2]
    row_gap = row_gap * row_gap
    col_gap = col_gap * col_gap
    total = row_gap[:, None, :] + col_gap[None, :, :]
    return jnp.exp(-spread_coef * total).reshape(CELLS, BLK).astype(jnp.bfloat16)


def meta_rows(pairs):
    return -(-3 * pairs // 16) * 16


def encode_blocks(
    capacity, shape, place_ref, tile_hbm, patch_hbm, feat_hbm, offset_hbm, near_ref, far_ref,
    slot_ref, send_ref, tile_ref, patch_ref, feat_ref, offset_ref, count_ref, sems,
):
    lat, depth, width = shape
    devices = lat * depth * width
    feat_width = feat_ref.shape[0]
    blocks = feat_ref.shape[1] // BLK
    step = sems.shape[0] - 3
    size = blocks // step
    pairs = capacity // 2
    meta = meta_rows(pairs)
    chunk = pairs * feat_width + meta
    small = [
        pltpu.make_async_copy(tile_hbm, tile_ref, sems.at[step]),
        pltpu.make_async_copy(patch_hbm, patch_ref, sems.at[step + 1]),
        pltpu.make_async_copy(offset_hbm, offset_ref, sems.at[step + 2]),
    ]
    large = []
    for i in range(step):
        span = pl.ds(i * size * BLK, size * BLK)
        large.append(pltpu.make_async_copy(feat_hbm.at[:, span], feat_ref.at[:, span], sems.at[i]))
    for copy in small + large:
        copy.start()
    send_ref[...] = jnp.zeros_like(send_ref)

    def clear(t, _):
        count_ref[t] = 0
        return 0

    lax.fori_loop(0, devices, clear, 0)
    lane_half = lax.broadcasted_iota(jnp.int32, (feat_width, LANES), 1) // CELLS
    meta_half = lax.broadcasted_iota(jnp.int32, (meta, LANES), 1) // CELLS
    meta_row = lax.broadcasted_iota(jnp.int32, (meta, LANES), 0)
    ones = jnp.ones((16, BLK), jnp.bfloat16)

    def one(b):
        tile = tile_ref[b]
        rank = count_ref[tile]
        count_ref[tile] = rank + 1
        lon = tile % (depth * width)
        partner = tile // (depth * width) * width + lon % width
        hop = lon // width ^ place_ref[1]
        piece = jnp.where(hop == 0, partner, lat * width + partner * (depth - 1) + hop - 1)
        slot_ref[b] = piece * capacity + rank
        pair = rank // 2
        half = rank % 2
        col = pl.multiple_of(b * BLK, BLK)
        feat = jnp.concatenate([feat_ref[:, pl.ds(col, BLK)], ones], axis=0)
        weights = block_weights(offset_ref[:, pl.ds(col, BLK)].astype(jnp.float32))
        twice = jnp.concatenate([weights, weights], axis=0)
        sums = lax.dot_general(feat, twice, NT, preferred_element_type=jnp.float32)
        row = pl.multiple_of(piece * chunk + pair * feat_width, 16)
        old = send_ref[pl.ds(row, feat_width), :].astype(jnp.float32)
        send_ref[pl.ds(row, feat_width), :] = jnp.where(
            lane_half == half, sums[:feat_width], old
        ).astype(jnp.bfloat16)
        mass = sums[feat_width : feat_width + 1]
        high = mass.astype(jnp.bfloat16).astype(jnp.float32)
        low = mass - high
        tag = (patch_ref[b] + 1).astype(jnp.float32)
        row = pl.multiple_of(piece * chunk + pairs * feat_width, 16)
        old = send_ref[pl.ds(row, meta), :].astype(jnp.float32)
        new = jnp.where(
            meta_row == pair,
            high,
            jnp.where(
                meta_row == pairs + pair, low, jnp.where(meta_row == 2 * pairs + pair, tag, old)
            ),
        )
        send_ref[pl.ds(row, meta), :] = jnp.where(meta_half == half, new, old).astype(jnp.bfloat16)

    for copy in small:
        copy.wait()
    for i in range(step):
        large[i].wait()
        for b in range(i * size, (i + 1) * size):
            one(b)
    near_ref[...] = send_ref[: near_ref.shape[0]]
    far_ref[...] = send_ref[near_ref.shape[0] :]


def dense_rows(pairs, feat_width):
    return pairs * feat_width + -(-2 * pairs // 16) * 16


def add_chunk(capacity, feat_width, id_ref, slot, recv_ref, base, low_ref, high_ref):
    pairs = capacity // 2
    tags = recv_ref[base + pairs * feat_width : base + pairs * feat_width + meta_rows(pairs), :]
    tags = tags.astype(jnp.float32)
    for k in range(pairs):
        at = base + k * feat_width
        sums = recv_ref[at : at + feat_width, :].astype(jnp.float32)
        mass = tags[k : k + 1] + tags[pairs + k : pairs + k + 1]
        both = jnp.concatenate([sums, jnp.broadcast_to(mass, (8, LANES))], axis=0)
        low_ref[id_ref[slot + 2 * k]] += both
        high_ref[id_ref[slot + 2 * k + 1]] += both


def paired(low_ref, high_ref, j):
    first = lax.broadcasted_iota(jnp.int32, low_ref.shape[1:], 1) < CELLS
    even = low_ref[2 * j] + pltpu.roll(high_ref[2 * j], CELLS, 1)
    odd = high_ref[2 * j + 1] + pltpu.roll(low_ref[2 * j + 1], CELLS, 1)
    return jnp.where(first, even, odd)


def gather_planes(capacity, plane, hops, feat_width, id_ref, recv_ref, *refs):
    outs, lows, highs = refs[:hops], refs[hops : 2 * hops], refs[2 * hops :]
    pairs = capacity // 2
    chunk = pairs * feat_width + meta_rows(pairs)
    patch_pairs = lows[0].shape[0] // 2
    for ref in lows + highs:
        ref[...] = jnp.zeros_like(ref)
    for r in range(plane):
        for hop in range(hops):
            n = r * hops + hop
            add_chunk(
                capacity, feat_width, id_ref, n * capacity, recv_ref, n * chunk, lows[hop], highs[hop]
            )
    for hop in range(hops):
        masses = []
        for j in range(patch_pairs):
            pair = paired(lows[hop], highs[hop], j)
            outs[hop][j * feat_width : (j + 1) * feat_width, :] = pair[:feat_width].astype(
                jnp.bfloat16
            )
            masses.append(pair[feat_width : feat_width + 1])
        masses = jnp.concatenate(masses, axis=0)
        high = masses.astype(jnp.bfloat16).astype(jnp.float32)
        spare = outs[hop].shape[0] - patch_pairs * (feat_width + 2)
        rows = [high, masses - high] + ([jnp.zeros((spare, LANES), jnp.float32)] if spare else [])
        outs[hop][patch_pairs * feat_width :, :] = jnp.concatenate(rows, axis=0).astype(jnp.bfloat16)


def gather_own(capacity, plane, feat_width, id_ref, recv_ref, *refs):
    own_ref, low_ref, high_ref = refs[-3:]
    chunk = recv_ref.shape[0] // plane
    low_ref[...] = jnp.zeros_like(low_ref)
    high_ref[...] = jnp.zeros_like(high_ref)
    for r in range(plane):
        add_chunk(
            capacity, feat_width, id_ref, r * capacity, recv_ref, r * chunk, low_ref, high_ref
        )
    for j in range(own_ref.shape[0]):
        own_ref[j] = paired(low_ref, high_ref, j)


def start_tile(hops, own_ref, *refs):
    parts = refs[:hops]
    embed_ref, base_ref, start_ref = refs[hops:]
    feat_width, channels = embed_ref.shape
    tile_rows, tile_cols, _ = base_ref.shape
    patch_rows, patch_cols = tile_rows // PATCH, tile_cols // PATCH
    patch_pairs = patch_rows * patch_cols // 2
    embed = embed_ref[...]
    mass_rows = [part[patch_pairs * feat_width :, :].astype(jnp.float32) for part in parts]
    for pr in range(patch_rows):
        lifted = []
        for pc in range(patch_cols // 2):
            j = pr * (patch_cols // 2) + pc
            pair = own_ref[j]
            sums, mass = pair[:feat_width], pair[feat_width : feat_width + 1]
            for part, rows in zip(parts, mass_rows):
                sums = sums + part[j * feat_width : (j + 1) * feat_width, :].astype(jnp.float32)
                mass = mass + (rows[j : j + 1] + rows[patch_pairs + j : patch_pairs + j + 1])
            encoded = (sums * (1.0 / (1.0 + mass))).astype(jnp.bfloat16)
            lifted.append(lax.dot_general(encoded, embed, TN, preferred_element_type=jnp.float32))
        lifted = jnp.concatenate(lifted, axis=0).reshape(patch_cols, PATCH, PATCH, channels)
        lifted = lifted.transpose(1, 0, 2, 3).reshape(PATCH, tile_cols, channels)
        rows = slice(pr * PATCH, (pr + 1) * PATCH)
        start_ref[rows] = (base_ref[rows].astype(jnp.float32) + lifted).astype(jnp.bfloat16)


def turn_weights(qkv_ref, turned_ref):
    channels = qkv_ref.shape[0]
    turned_ref[:channels] = qkv_ref[:, :channels].T
    turned_ref[channels:] = qkv_ref[:, 2 * channels :].T


def attend(
    cells_ref, windows, side, norm_gain, qkv_ref, out_ref, turned_ref, key_ref, pack_ref, att_ref,
    score_ref, prob_ref,
):
    channels = qkv_ref.shape[0]
    tokens = WIN * WIN
    group = 128
    heads = group // HEAD_DIM
    count = -(-len(windows) // 2)
    size = count * LANES
    scale = HEAD_DIM ** (-0.5) / math.log(2.0)
    shape = (tokens, heads * LANES)
    own = lax.broadcasted_iota(jnp.int32, shape, 1) % LANES < tokens
    nothing = jnp.zeros(shape, jnp.bfloat16)
    empty = jnp.zeros((HEAD_DIM, LANES), jnp.bfloat16)
    cells = jnp.concatenate(
        [
            cells_ref[row : row + WIN, col : col + WIN, :].reshape(tokens, channels)
            for row, col in windows
        ],
        axis=0,
    )
    normed = normalize(cells, norm_gain).astype(jnp.bfloat16)
    if len(windows) % 2:
        normed = jnp.concatenate([normed, jnp.zeros((tokens, channels), jnp.bfloat16)], axis=0)
    key_ref[:size] = jnp.dot(
        normed, qkv_ref[:, channels : 2 * channels], preferred_element_type=jnp.float32
    ).astype(jnp.bfloat16)
    pack_ref[:, :size] = lax.dot_general(
        turned_ref[...], normed, NT, preferred_element_type=jnp.float32
    ).astype(jnp.bfloat16)
    if side is not None:
        key_row = lax.broadcasted_iota(jnp.int32, (tokens, LANES), 0) // WIN
        query_row = lax.broadcasted_iota(jnp.int32, (tokens, LANES), 1) % tokens // WIN
        bias = jnp.where(side(key_row) == side(query_row), 0.0, -1e30)
        bias = jnp.concatenate([bias] * heads, axis=1)
    parts = [(p, g) for p in range(count) for g in range(channels // group)]
    for n, (p, g) in enumerate(parts):
        span = slice(p * LANES, (p + 1) * LANES)
        at = slice(g * group, (g + 1) * group)
        query = pack_ref[at, span]
        stack = jnp.concatenate(
            [
                jnp.concatenate(
                    [
                        query[h * HEAD_DIM : (h + 1) * HEAD_DIM] if i == h else empty
                        for i in range(heads)
                    ],
                    axis=0,
                )
                for h in range(heads)
            ],
            axis=1,
        )
        scores = jnp.dot(key_ref[span, at], stack, preferred_element_type=jnp.float32)
        scores = jnp.where(own, scores[:tokens], scores[tokens:])
        score_ref[n] = scores if side is None else scores + bias
    for n in range(len(parts)):
        scores = score_ref[n]
        peak = jnp.max(scores, axis=0, keepdims=True)
        raised = jnp.exp2((scores - peak) * scale)
        total = jnp.sum(raised, axis=0, keepdims=True)
        probs = (raised * (1.0 / total)).astype(jnp.bfloat16)
        prob_ref[n, :tokens] = jnp.where(own, probs, nothing)
        prob_ref[n, tokens:] = jnp.where(own, nothing, probs)
    for n, (p, g) in enumerate(parts):
        span = slice(p * LANES, (p + 1) * LANES)
        for h in range(0, heads, 2):
            at = g * group + h * HEAD_DIM
            both = jnp.dot(
                pack_ref[channels + at : channels + at + 2 * HEAD_DIM, span],
                prob_ref[n, :, h * LANES : (h + 2) * LANES],
                preferred_element_type=jnp.float32,
            ).astype(jnp.bfloat16)
            att_ref[at : at + HEAD_DIM, span] = both[:HEAD_DIM, :LANES]
            att_ref[at + HEAD_DIM : at + 2 * HEAD_DIM, span] = both[HEAD_DIM:, LANES:]
    mixed = lax.dot_general(
        att_ref[:, :size], out_ref[...], TN, preferred_element_type=jnp.float32
    )
    return [
        mixed[w * tokens : (w + 1) * tokens].reshape(WIN, WIN, channels)
        for w in range(len(windows))
    ]


def finish(begun, mixed, mlp_gain, up_ref, down_ref, decode_ref):
    residual = jnp.concatenate([a.reshape(CELLS, -1) + b.reshape(CELLS, -1) for a, b in zip(begun, mixed)])
    normed = normalize(residual, mlp_gain).astype(jnp.bfloat16)
    hidden = jax.nn.gelu(jnp.dot(normed, up_ref[...], preferred_element_type=jnp.float32))
    latent = residual + jnp.dot(
        hidden.astype(jnp.bfloat16), down_ref[...], preferred_element_type=jnp.float32
    )
    rounded = latent.astype(jnp.bfloat16)
    turned = [
        lax.dot_general(
            decode_ref[...],
            rounded[i * CELLS : i * CELLS + LANES],
            NT,
            preferred_element_type=jnp.float32,
        ).astype(jnp.bfloat16)
        for i in range(0, len(begun), 2)
    ]
    return latent, turned


def patch_order(patch_rows, patch_cols):
    inner = lambda r, c: 0 < r < patch_rows - 1 and 0 < c < patch_cols - 1
    every = [(r, c) for r in range(patch_rows) for c in range(patch_cols)]
    first = [at for at in every if inner(*at)]
    sides = [at for at in every if 0 < at[0] < patch_rows - 1 and not inner(*at)]
    ends = [at for at in every if not 0 < at[0] < patch_rows - 1]
    return first, sides, ends


def inner_block(
    start_ref, norm_ref, qkv_ref, out_ref, mlp_ref, up_ref, down_ref, decode_ref, latent_ref,
    proj_ref, mixed_ref, cells_ref, turned_ref, key_ref, pack_ref, att_ref, score_ref, prob_ref,
):
    tile_rows, tile_cols, channels = cells_ref.shape
    margin = WIN // 2
    feat_width = decode_ref.shape[0]
    cells_ref[...] = start_ref[...].astype(jnp.float32)
    turn_weights(qkv_ref, turned_ref)
    for row in range(0, tile_rows - WIN, WIN):
        cols = range(0, tile_cols - WIN, WIN)
        mixed = attend(
            cells_ref, [(row + margin, col + margin) for col in cols], None, norm_ref[...],
            qkv_ref, out_ref, turned_ref, key_ref, pack_ref, att_ref, score_ref, prob_ref,
        )
        for col, block in zip(cols, mixed):
            mixed_ref[row : row + WIN, col : col + WIN, :] = block
    first, _, _ = patch_order(tile_rows // PATCH, tile_cols // PATCH)
    done = 0
    for pr in sorted(set(r for r, _ in first)):
        here = [c for r, c in first if r == pr]
        row = pr * PATCH
        latent, turned = finish(
            [cells_ref[row : row + PATCH, c * PATCH : (c + 1) * PATCH, :] for c in here],
            [
                mixed_ref[
                    row - margin : row - margin + PATCH,
                    c * PATCH - margin : c * PATCH - margin + PATCH,
                    :,
                ]
                for c in here
            ],
            mlp_ref[...], up_ref, down_ref, decode_ref,
        )
        placed = latent.reshape(len(here), PATCH, PATCH, channels).transpose(1, 0, 2, 3)
        latent_ref[row - PATCH : row] = placed.reshape(PATCH, len(here) * PATCH, channels).astype(
            jnp.bfloat16
        )
        for pair in turned:
            proj_ref[done : done + feat_width, :] = pair
            done += feat_width


def outer_block(
    lat_cells, place_ref, ext_ref, inner_latent_ref, inner_proj_ref, inner_mixed_ref, norm_ref, qkv_ref, out_ref,
    mlp_ref, up_ref, down_ref, decode_ref, latent_ref, proj_ref, mixed_ref, turned_ref, key_ref,
    pack_ref, att_ref, score_ref, prob_ref,
):
    ext_rows, ext_cols, channels = ext_ref.shape
    tile_rows, tile_cols, _ = latent_ref.shape
    margin = WIN // 2
    feat_width = decode_ref.shape[0]
    last_row, last_col = ext_rows - WIN, ext_cols - WIN
    top = place_ref[2] * tile_rows - margin
    turn_weights(qkv_ref, turned_ref)

    def place(windows, side):
        mixed = attend(
            ext_ref, windows, side, norm_ref[...], qkv_ref, out_ref, turned_ref, key_ref,
            pack_ref, att_ref, score_ref, prob_ref,
        )
        for (row, col), block in zip(windows, mixed):
            mixed_ref[row : row + WIN, col : col + WIN, :] = block

    for row in (0, last_row):
        side = lambda r: (top + row + r >= 0).astype(jnp.int32) + (
            top + row + r >= lat_cells
        ).astype(jnp.int32)
        place([(row, col) for col in range(0, ext_cols, WIN)], side)
    place([(row, col) for row in range(WIN, last_row, WIN) for col in (0, last_col)], None)
    mixed_ref[WIN:last_row, WIN:last_col, :] = inner_mixed_ref[...]
    _, sides, ends = patch_order(tile_rows // PATCH, tile_cols // PATCH)
    done = inner_proj_ref.shape[0]
    proj_ref[:done, :] = inner_proj_ref[...]

    def patches(here):
        at = [
            (
                slice(r * PATCH + margin, (r + 1) * PATCH + margin),
                slice(c * PATCH + margin, (c + 1) * PATCH + margin),
            )
            for r, c in here
        ]
        latent, turned = finish(
            [ext_ref[r, c, :] for r, c in at],
            [mixed_ref[r, c, :] for r, c in at],
            mlp_ref[...], up_ref, down_ref, decode_ref,
        )
        for i, pair in enumerate(turned):
            at = done + i * feat_width
            proj_ref[at : at + feat_width, :] = pair
        return latent.reshape(len(here), PATCH, PATCH, channels), len(turned) * feat_width

    latent, used = patches(sides)
    done += used
    for pr in sorted(set(r for r, _ in sides)):
        left, right = [latent[i] for i, (r, _) in enumerate(sides) if r == pr]
        inner = inner_latent_ref[(pr - 1) * PATCH : pr * PATCH].astype(jnp.float32)
        whole = jnp.concatenate([left, inner, right], axis=1)
        latent_ref[pr * PATCH : (pr + 1) * PATCH] = whole.astype(jnp.bfloat16)
    for pr in sorted(set(r for r, _ in ends)):
        latent, used = patches([at for at in ends if at[0] == pr])
        done += used
        placed = latent.transpose(1, 0, 2, 3).reshape(PATCH, tile_cols, channels)
        latent_ref[pr * PATCH : (pr + 1) * PATCH] = placed.astype(jnp.bfloat16)


def reply_patches(capacity, plane, tiles, order, feat_width, id_ref, *refs):
    tile_refs, out_ref, both_ref = refs[:tiles], refs[tiles], refs[tiles + 1]
    pairs = capacity // 2
    first = lax.broadcasted_iota(jnp.int32, (feat_width, LANES), 1) < CELLS
    for t in range(tiles):
        for i in range(0, len(order), 2):
            at = i // 2 * feat_width
            pair = tile_refs[t][at : at + feat_width, :].astype(jnp.float32)
            swapped = pltpu.roll(pair, CELLS, 1)
            both_ref[t, order[i]] = jnp.where(first, pair, swapped)
            both_ref[t, order[i + 1]] = jnp.where(first, swapped, pair)
    for r in range(plane):
        for t in range(tiles):
            for k in range(pairs):
                slot = (r * tiles + t) * capacity + 2 * k
                pair = jnp.where(
                    first, both_ref[t, id_ref[slot]], both_ref[t, id_ref[slot + 1]]
                )
                at = ((r * tiles + t) * pairs + k) * feat_width
                out_ref[at : at + feat_width, :] = pair.astype(jnp.bfloat16)


def decode_blocks(slot_ref, offset_ref, near_ref, far_ref, out_ref, back_ref):
    back_ref[: near_ref.shape[0], :] = near_ref[...]
    back_ref[near_ref.shape[0] :, :] = far_ref[...]
    feat_width, count = out_ref.shape
    blocks = count // BLK

    def one(b):
        slot = slot_ref[b]
        col = pl.multiple_of(b * BLK, BLK)
        weights = block_weights(offset_ref[:, pl.ds(col, BLK)].astype(jnp.float32))
        total = jnp.sum(weights.astype(jnp.float32), axis=0, keepdims=True)
        nothing = jnp.zeros_like(weights)
        low = slot % 2 == 0
        both = jnp.concatenate(
            [jnp.where(low, weights, nothing), jnp.where(low, nothing, weights)], axis=0
        )
        values = back_ref[pl.ds(pl.multiple_of(slot // 2 * feat_width, 16), feat_width), :]
        mean = jnp.dot(values, both, preferred_element_type=jnp.float32) * (1.0 / total)
        out_ref[:, pl.ds(col, BLK)] = mean.astype(jnp.bfloat16)

    unroll = 32 if blocks % 32 == 0 else 1

    def body(i, _):
        for u in range(unroll):
            one(i * unroll + u)
        return 0

    lax.fori_loop(0, blocks // unroll, body, 0)


def with_halo(array, sides, width):
    for axis, dim in sides:
        size, length = (axis_count(axis), array.shape[dim])
        up = [(i, (i + 1) % size) for i in range(size)]
        down = [(j, i) for i, j in up]
        last = lax.slice_in_dim(array, length - width, length, axis=dim)
        initial = lax.slice_in_dim(array, 0, width, axis=dim)
        before = lax.ppermute(last, axis, up)
        after = lax.ppermute(initial, axis, down)
        array = jnp.concatenate([before, array, after], axis=dim)
    return array


def axis_count(axes):
    axes = axes if isinstance(axes, tuple) else (axes,)
    return math.prod([lax.axis_size(axis) for axis in axes])


def swap_in_plane(array):
    plane = axis_count(("lat", "x"))
    parts = array.reshape(plane, -1, LANES)
    parts = lax.all_to_all(parts, ("lat", "x"), split_axis=0, concat_axis=0, tiled=True)
    return parts.reshape(array.shape)


def swap_at_once(gains, array):
    def apart(array):
        lat, width = lax.axis_size("lat"), lax.axis_size("x")
        parts = array.reshape(lat, width, -1, LANES)
        for dim, axis in enumerate(("lat", "x")):
            parts = lax.all_to_all(parts, axis, split_axis=dim, concat_axis=dim, tiled=True)
        return parts.reshape(array.shape)

    return lax.cond(gains[0] > 0.0, swap_in_plane, apart, array)


def swap_planes(array, hop):
    depth = lax.axis_size("z")
    return lax.ppermute(array, "z", [(i, i ^ hop) for i in range(depth)])


def local(
    obs_feat,
    obs_offset,
    block_tile,
    block_patch,
    embed_weight,
    grid_base,
    norm_gain,
    qkv_weight,
    out_weight,
    mlp_gain,
    up_weight,
    down_weight,
    decode_weight,
):
    lat, depth, width = (lax.axis_size(axis) for axis in ("lat", "z", "x"))
    plane, hops = lat * width, depth - 1
    devices = plane * depth
    feat_width, obs_count = obs_feat.shape
    blocks = obs_count // BLK
    capacity = max(2, 2 * blocks // devices)
    capacity += capacity % 2
    pairs = capacity // 2
    tile_rows, tile_cols, channels = grid_base.shape
    patch_total = (tile_rows // PATCH) * (tile_cols // PATCH)
    chunk = pairs * feat_width + meta_rows(pairs)
    dense = dense_rows(patch_total // 2, feat_width)
    lat_id = lax.axis_index("lat").astype(jnp.int32)
    place = jnp.stack(
        [lat_id * width + lax.axis_index("x"), lax.axis_index("z"), lat_id]
    ).astype(jnp.int32)

    steps = 3 if blocks % 3 == 0 else 1
    send_near, send_far, slots = pl.pallas_call(
        lambda *refs: encode_blocks(capacity, (lat, depth, width), *refs),
        out_shape=(
            jax.ShapeDtypeStruct((plane * chunk, LANES), jnp.bfloat16),
            jax.ShapeDtypeStruct((plane * hops * chunk, LANES), jnp.bfloat16),
            jax.ShapeDtypeStruct((blocks,), jnp.int32),
        ),
        in_specs=[smem()] + [pl.BlockSpec(memory_space=pltpu.HBM)] * 4,
        out_specs=(vmem(), vmem(), smem()),
        scratch_shapes=[
            pltpu.VMEM((devices * chunk, LANES), jnp.bfloat16),
            pltpu.SMEM((blocks,), jnp.int32),
            pltpu.SMEM((blocks,), jnp.int32),
            pltpu.VMEM(obs_feat.shape, jnp.bfloat16),
            pltpu.VMEM(obs_offset.shape, jnp.bfloat16),
            pltpu.SMEM((devices,), jnp.int32),
            pltpu.SemaphoreType.DMA((steps + 3,)),
        ],
        compiler_params=params(61),
        name="encode_blocks",
    )(place, block_tile.reshape(blocks), block_patch, obs_feat, obs_offset)

    def ids_of(recv, tiles):
        at = pairs * feat_width + 2 * pairs
        tags = recv.reshape(plane * tiles, chunk, LANES)[:, at : at + pairs, 0::CELLS]
        ids = tags.astype(jnp.float32).astype(jnp.int32) - 1
        return jnp.clip(ids, 0, patch_total - 1).reshape(-1)

    far = swap_in_plane(send_far)
    far_ids = ids_of(far, hops)
    sums = pl.pallas_call(
        lambda *refs: gather_planes(capacity, plane, hops, feat_width, *refs),
        out_shape=[jax.ShapeDtypeStruct((dense, LANES), jnp.bfloat16)] * hops,
        in_specs=[smem(), vmem()],
        out_specs=[vmem()] * hops,
        scratch_shapes=[pltpu.VMEM((patch_total, feat_width + 8, LANES), jnp.float32)] * (2 * hops),
        compiler_params=params(14),
        name="gather_planes",
    )(far_ids, far)
    parts = [swap_planes(sums[hop - 1], hop) for hop in range(hops, 0, -1)]
    send_near, _ = lax.optimization_barrier((send_near, sums))
    near = swap_at_once(norm_gain, send_near)
    near_ids = ids_of(near, 1)
    own = pl.pallas_call(
        lambda *refs: gather_own(capacity, plane, feat_width, *refs),
        out_shape=jax.ShapeDtypeStruct((patch_total // 2, feat_width + 8, LANES), jnp.float32),
        in_specs=[smem()] + [vmem()] * 3,
        out_specs=vmem(),
        scratch_shapes=[pltpu.VMEM((patch_total, feat_width + 8, LANES), jnp.float32)] * 2,
        compiler_params=params(10),
        cost_estimate=pl.CostEstimate(flops=10**9, bytes_accessed=10**7, transcendentals=0),
        name="gather_own",
    )(near_ids, near, qkv_weight, out_weight)

    start = pl.pallas_call(
        lambda *refs: start_tile(hops, *refs),
        out_shape=jax.ShapeDtypeStruct(grid_base.shape, jnp.bfloat16),
        in_specs=[vmem()] * (hops + 3),
        out_specs=vmem(),
        compiler_params=params(10),
        name="start_tile",
    )(own, *parts, embed_weight, grid_base)

    margin = WIN // 2
    ext = with_halo(start, (("lat", 0), (("z", "x"), 1)), margin).astype(jnp.float32)
    ext_rows, ext_cols, _ = ext.shape
    group = 128
    gains = (norm_gain.reshape(1, channels), mlp_gain.reshape(1, channels))
    weights = (gains[0], qkv_weight, out_weight, gains[1], up_weight, down_weight, decode_weight.T)
    patch_rows, patch_cols = tile_rows // PATCH, tile_cols // PATCH
    inner, sides, ends = patch_order(patch_rows, patch_cols)
    order = [r * patch_cols + c for r, c in inner + sides + ends]
    inner_cells = (tile_rows - 2 * PATCH, tile_cols - 2 * PATCH, channels)
    inner_mixed = (tile_rows - WIN, tile_cols - WIN, channels)

    def scratch(windows):
        count = -(-windows // 2)
        parts = count * channels // group
        lanes = group // HEAD_DIM * LANES
        return [
            pltpu.VMEM((2 * channels, channels), jnp.bfloat16),
            pltpu.VMEM((count * LANES, channels), jnp.bfloat16),
            pltpu.VMEM((2 * channels, count * LANES), jnp.bfloat16),
            pltpu.VMEM((channels, count * LANES), jnp.bfloat16),
            pltpu.VMEM((parts, WIN * WIN, lanes), jnp.float32),
            pltpu.VMEM((parts, LANES, lanes), jnp.bfloat16),
        ]

    latent_inner, proj_inner, mixed_inner = pl.pallas_call(
        inner_block,
        out_shape=(
            jax.ShapeDtypeStruct(inner_cells, jnp.bfloat16),
            jax.ShapeDtypeStruct((len(inner) // 2 * feat_width, LANES), jnp.bfloat16),
            jax.ShapeDtypeStruct(inner_mixed, jnp.float32),
        ),
        in_specs=[vmem()] * 8,
        out_specs=(vmem(), vmem(), vmem()),
        scratch_shapes=[pltpu.VMEM(grid_base.shape, jnp.float32)]
        + scratch(tile_cols // WIN - 1),
        compiler_params=params(16),
        cost_estimate=pl.CostEstimate(flops=6 * 10**9, bytes_accessed=10**7, transcendentals=0),
        name="inner_block",
    )(start, *weights)

    latent, projected = pl.pallas_call(
        lambda *refs: outer_block(tile_rows * lat, *refs),
        out_shape=(
            jax.ShapeDtypeStruct(grid_base.shape, jnp.bfloat16),
            jax.ShapeDtypeStruct((patch_total // 2 * feat_width, LANES), jnp.bfloat16),
        ),
        in_specs=[smem()] + [vmem()] * 11,
        out_specs=(vmem(), vmem()),
        scratch_shapes=[pltpu.VMEM((ext_rows, ext_cols, channels), jnp.float32)]
        + scratch(max(ext_cols // WIN, 2 * (ext_rows // WIN - 2))),
        compiler_params=params(20),
        cost_estimate=pl.CostEstimate(flops=8 * 10**9, bytes_accessed=10**7, transcendentals=0),
        name="outer_block",
    )(place, ext, latent_inner, proj_inner, mixed_inner, *weights)

    def reply(ids, tiles, name):
        count = len(tiles)
        return pl.pallas_call(
            lambda *refs: reply_patches(capacity, plane, count, order, feat_width, *refs),
            out_shape=jax.ShapeDtypeStruct(
                (plane * count * pairs * feat_width, LANES), jnp.bfloat16
            ),
            in_specs=[smem()] + [vmem()] * count,
            out_specs=vmem(),
            scratch_shapes=[pltpu.VMEM((count, patch_total, feat_width, LANES), jnp.float32)],
            compiler_params=params(12),
            cost_estimate=pl.CostEstimate(flops=10**9, bytes_accessed=10**7, transcendentals=0),
            name=name,
        )(ids, *tiles)

    others = [swap_planes(projected, hop) for hop in range(hops, 0, -1)][::-1]
    near_reply = reply(near_ids, [projected], "reply_near")
    near_back = swap_at_once(norm_gain, near_reply)
    far_back = swap_in_plane(reply(far_ids, others, "reply_far"))

    obs_out = pl.pallas_call(
        decode_blocks,
        out_shape=jax.ShapeDtypeStruct((feat_width, obs_count), jnp.bfloat16),
        in_specs=[smem(), vmem()] + [vmem()] * 2,
        out_specs=vmem(),
        scratch_shapes=[pltpu.VMEM((devices * pairs * feat_width, LANES), jnp.bfloat16)],
        compiler_params=params(10),
        name="decode_blocks",
    )(slots, obs_offset, near_back, far_back)
    return (latent, obs_out)


def solution(mesh):
    lat, lon = mesh.devices.shape
    width = lat // 2 if lat % 2 == 0 and lon % (lat // 2) == 0 else 1
    split = Mesh(mesh.devices.reshape(lat, lon // width, width), ("lat", "z", "x"))
    every = ("lat", "z", "x")
    placed = (
        P(None, every),
        P(None, every),
        P(every, None),
        P(every),
        P(),
        P("lat", ("z", "x"), None),
        P(),
        P(),
        P(),
        P(),
        P(),
        P(),
        P(),
    )
    return jax.shard_map(
        local,
        mesh=split,
        in_specs=placed,
        out_specs=(P("lat", ("z", "x"), None), P(None, every)),
        check_vma=False,
    )
```

```python
import math

import jax
import jax.numpy as jnp
from jax import lax
from jax.experimental import pallas as pl
from jax.experimental.pallas import tpu as pltpu
from jax.sharding import Mesh
from jax.sharding import PartitionSpec as P

HEAD_DIM = 32
WIN = 8
PATCH = 8
BLK = 128
CELLS = PATCH * PATCH
LANES = 2 * CELLS

epsilon = 1e-05
spread_coef = 0.5

NT = (((1,), (1,)), ((), ()))
TN = (((0,), (0,)), ((), ()))


def params(mib):
    return pltpu.CompilerParams(vmem_limit_bytes=mib * 1024 * 1024)


def vmem():
    return pl.BlockSpec(memory_space=pltpu.VMEM)


def smem():
    return pl.BlockSpec(memory_space=pltpu.SMEM)


def normalize(values, gain_row):
    center = jnp.mean(values, axis=-1, keepdims=True)
    centered = values - center
    variance = jnp.mean(centered * centered, axis=-1, keepdims=True)
    return centered * lax.rsqrt(variance + epsilon) * gain_row


def block_weights(offsets):
    axis_id = lax.broadcasted_iota(jnp.int32, (PATCH, BLK), 0).astype(jnp.float32) + 0.5
    row_gap = axis_id - offsets[0:1]
    col_gap = axis_id - offsets[1:2]
    row_gap = row_gap * row_gap
    col_gap = col_gap * col_gap
    total = row_gap[:, None, :] + col_gap[None, :, :]
    return jnp.exp(-spread_coef * total).reshape(CELLS, BLK).astype(jnp.bfloat16)


def meta_rows(pairs):
    return -(-3 * pairs // 16) * 16


def encode_blocks(
    capacity, shape, tile_hbm, patch_hbm, feat_hbm, offset_hbm, near_ref, far_ref,
    slot_ref, send_ref, tile_ref, patch_ref, feat_ref, offset_ref, count_ref, sems,
):
    lat, depth, width = shape
    devices = lat * depth * width
    plane_id = lax.axis_index("z")
    feat_width = feat_ref.shape[0]
    blocks = feat_ref.shape[1] // BLK
    step = sems.shape[0] - 3
    size = blocks // step
    pairs = capacity // 2
    meta = meta_rows(pairs)
    chunk = pairs * feat_width + meta
    small = [
        pltpu.make_async_copy(tile_hbm, tile_ref, sems.at[step]),
        pltpu.make_async_copy(patch_hbm, patch_ref, sems.at[step + 1]),
        pltpu.make_async_copy(offset_hbm, offset_ref, sems.at[step + 2]),
    ]
    large = []
    for i in range(step):
        span = pl.ds(i * size * BLK, size * BLK)
        large.append(pltpu.make_async_copy(feat_hbm.at[:, span], feat_ref.at[:, span], sems.at[i]))
    for copy in small + large:
        copy.start()
    send_ref[...] = jnp.zeros_like(send_ref)

    def clear(t, _):
        count_ref[t] = 0
        return 0

    lax.fori_loop(0, devices, clear, 0)
    lane_half = lax.broadcasted_iota(jnp.int32, (feat_width, LANES), 1) // CELLS
    meta_half = lax.broadcasted_iota(jnp.int32, (meta, LANES), 1) // CELLS
    meta_row = lax.broadcasted_iota(jnp.int32, (meta, LANES), 0)
    ones = jnp.ones((16, BLK), jnp.bfloat16)

    def one(b):
        tile = tile_ref[b]
        rank = count_ref[tile]
        count_ref[tile] = rank + 1
        lon = lax.rem(tile, depth * width)
        partner = lax.div(tile, depth * width) * width + lax.rem(lon, width)
        hop = lax.div(lon, width) ^ plane_id
        piece = jnp.where(hop == 0, partner, lat * width + partner * (depth - 1) + hop - 1)
        slot_ref[b] = piece * capacity + rank
        pair = lax.div(rank, 2)
        half = lax.rem(rank, 2)
        col = pl.multiple_of(b * BLK, BLK)
        feat = jnp.concatenate([feat_ref[:, pl.ds(col, BLK)], ones], axis=0)
        weights = block_weights(offset_ref[:, pl.ds(col, BLK)].astype(jnp.float32))
        twice = jnp.concatenate([weights, weights], axis=0)
        sums = lax.dot_general(feat, twice, NT, preferred_element_type=jnp.float32)
        row = pl.multiple_of(piece * chunk + pair * feat_width, 16)
        old = send_ref[pl.ds(row, feat_width), :].astype(jnp.float32)
        send_ref[pl.ds(row, feat_width), :] = jnp.where(
            lane_half == half, sums[:feat_width], old
        ).astype(jnp.bfloat16)
        mass = sums[feat_width : feat_width + 1]
        high = mass.astype(jnp.bfloat16).astype(jnp.float32)
        low = mass - high
        tag = (patch_ref[b] + 1).astype(jnp.float32)
        row = pl.multiple_of(piece * chunk + pairs * feat_width, 16)
        old = send_ref[pl.ds(row, meta), :].astype(jnp.float32)
        new = jnp.where(
            meta_row == pair,
            high,
            jnp.where(
                meta_row == pairs + pair, low, jnp.where(meta_row == 2 * pairs + pair, tag, old)
            ),
        )
        send_ref[pl.ds(row, meta), :] = jnp.where(meta_half == half, new, old).astype(jnp.bfloat16)

    for copy in small:
        copy.wait()
    for i in range(step):
        large[i].wait()
        for b in range(i * size, (i + 1) * size):
            one(b)
    near_ref[...] = send_ref[: near_ref.shape[0]]
    far_ref[...] = send_ref[near_ref.shape[0] :]


def dense_rows(pairs, feat_width):
    return pairs * feat_width + -(-2 * pairs // 16) * 16


def add_chunk(capacity, feat_width, id_ref, slot, recv_ref, base, low_ref, high_ref):
    pairs = capacity // 2
    tags = recv_ref[base + pairs * feat_width : base + pairs * feat_width + meta_rows(pairs), :]
    tags = tags.astype(jnp.float32)
    for k in range(pairs):
        at = base + k * feat_width
        sums = recv_ref[at : at + feat_width, :].astype(jnp.float32)
        mass = tags[k : k + 1] + tags[pairs + k : pairs + k + 1]
        both = jnp.concatenate([sums, jnp.broadcast_to(mass, (8, LANES))], axis=0)
        low_ref[id_ref[slot + 2 * k]] += both
        high_ref[id_ref[slot + 2 * k + 1]] += both


def paired(low_ref, high_ref, j):
    first = lax.broadcasted_iota(jnp.int32, low_ref.shape[1:], 1) < CELLS
    even = low_ref[2 * j] + pltpu.roll(high_ref[2 * j], CELLS, 1)
    odd = high_ref[2 * j + 1] + pltpu.roll(low_ref[2 * j + 1], CELLS, 1)
    return jnp.where(first, even, odd)


def gather_planes(capacity, plane, hops, feat_width, id_ref, recv_ref, *refs):
    outs, lows, highs = refs[:hops], refs[hops : 2 * hops], refs[2 * hops :]
    pairs = capacity // 2
    chunk = pairs * feat_width + meta_rows(pairs)
    patch_pairs = lows[0].shape[0] // 2
    for ref in lows + highs:
        ref[...] = jnp.zeros_like(ref)
    for r in range(plane):
        for hop in range(hops):
            n = r * hops + hop
            add_chunk(
                capacity, feat_width, id_ref, n * capacity, recv_ref, n * chunk, lows[hop], highs[hop]
            )
    for hop in range(hops):
        masses = []
        for j in range(patch_pairs):
            pair = paired(lows[hop], highs[hop], j)
            outs[hop][j * feat_width : (j + 1) * feat_width, :] = pair[:feat_width].astype(
                jnp.bfloat16
            )
            masses.append(pair[feat_width : feat_width + 1])
        masses = jnp.concatenate(masses, axis=0)
        high = masses.astype(jnp.bfloat16).astype(jnp.float32)
        spare = outs[hop].shape[0] - patch_pairs * (feat_width + 2)
        rows = [high, masses - high] + ([jnp.zeros((spare, LANES), jnp.float32)] if spare else [])
        outs[hop][patch_pairs * feat_width :, :] = jnp.concatenate(rows, axis=0).astype(jnp.bfloat16)


def gather_own(capacity, plane, feat_width, id_ref, recv_ref, *refs):
    own_ref, low_ref, high_ref = refs[-3:]
    chunk = recv_ref.shape[0] // plane
    low_ref[...] = jnp.zeros_like(low_ref)
    high_ref[...] = jnp.zeros_like(high_ref)
    for r in range(plane):
        add_chunk(
            capacity, feat_width, id_ref, r * capacity, recv_ref, r * chunk, low_ref, high_ref
        )
    for j in range(own_ref.shape[0]):
        own_ref[j] = paired(low_ref, high_ref, j)


def start_tile(hops, own_ref, *refs):
    parts = refs[:hops]
    embed_ref, base_ref, start_ref = refs[hops:]
    feat_width, channels = embed_ref.shape
    tile_rows, tile_cols, _ = base_ref.shape
    patch_rows, patch_cols = tile_rows // PATCH, tile_cols // PATCH
    patch_pairs = patch_rows * patch_cols // 2
    embed = embed_ref[...]
    mass_rows = [part[patch_pairs * feat_width :, :].astype(jnp.float32) for part in parts]
    for pr in range(patch_rows):
        lifted = []
        for pc in range(patch_cols // 2):
            j = pr * (patch_cols // 2) + pc
            pair = own_ref[j]
            sums, mass = pair[:feat_width], pair[feat_width : feat_width + 1]
            for part, rows in zip(parts, mass_rows):
                sums = sums + part[j * feat_width : (j + 1) * feat_width, :].astype(jnp.float32)
                mass = mass + (rows[j : j + 1] + rows[patch_pairs + j : patch_pairs + j + 1])
            encoded = (sums * (1.0 / (1.0 + mass))).astype(jnp.bfloat16)
            lifted.append(lax.dot_general(encoded, embed, TN, preferred_element_type=jnp.float32))
        lifted = jnp.concatenate(lifted, axis=0).reshape(patch_cols, PATCH, PATCH, channels)
        lifted = lifted.transpose(1, 0, 2, 3).reshape(PATCH, tile_cols, channels)
        rows = slice(pr * PATCH, (pr + 1) * PATCH)
        start_ref[rows] = (base_ref[rows].astype(jnp.float32) + lifted).astype(jnp.bfloat16)


def turn_weights(qkv_ref, turned_ref):
    channels = qkv_ref.shape[0]
    turned_ref[:channels] = qkv_ref[:, :channels].T
    turned_ref[channels:] = qkv_ref[:, 2 * channels :].T


def attend(
    cells_ref, windows, side, norm_gain, qkv_ref, out_ref, turned_ref, key_ref, pack_ref, att_ref,
    score_ref, prob_ref,
):
    channels = qkv_ref.shape[0]
    tokens = WIN * WIN
    group = 128
    heads = group // HEAD_DIM
    count = -(-len(windows) // 2)
    size = count * LANES
    scale = HEAD_DIM ** (-0.5) / math.log(2.0)
    shape = (tokens, heads * LANES)
    own = lax.broadcasted_iota(jnp.int32, shape, 1) % LANES < tokens
    nothing = jnp.zeros(shape, jnp.bfloat16)
    empty = jnp.zeros((HEAD_DIM, LANES), jnp.bfloat16)
    cells = jnp.concatenate(
        [
            cells_ref[row : row + WIN, col : col + WIN, :].reshape(tokens, channels)
            for row, col in windows
        ],
        axis=0,
    )
    normed = normalize(cells, norm_gain).astype(jnp.bfloat16)
    if len(windows) % 2:
        normed = jnp.concatenate([normed, jnp.zeros((tokens, channels), jnp.bfloat16)], axis=0)
    key_ref[:size] = jnp.dot(
        normed, qkv_ref[:, channels : 2 * channels], preferred_element_type=jnp.float32
    ).astype(jnp.bfloat16)
    pack_ref[:, :size] = lax.dot_general(
        turned_ref[...], normed, NT, preferred_element_type=jnp.float32
    ).astype(jnp.bfloat16)
    if side is not None:
        key_row = lax.broadcasted_iota(jnp.int32, (tokens, LANES), 0) // WIN
        query_row = lax.broadcasted_iota(jnp.int32, (tokens, LANES), 1) % tokens // WIN
        bias = jnp.where(side(key_row) == side(query_row), 0.0, -1e30)
        bias = jnp.concatenate([bias] * heads, axis=1)
    parts = [(p, g) for p in range(count) for g in range(channels // group)]
    for n, (p, g) in enumerate(parts):
        span = slice(p * LANES, (p + 1) * LANES)
        at = slice(g * group, (g + 1) * group)
        query = pack_ref[at, span]
        stack = jnp.concatenate(
            [
                jnp.concatenate(
                    [
                        query[h * HEAD_DIM : (h + 1) * HEAD_DIM] if i == h else empty
                        for i in range(heads)
                    ],
                    axis=0,
                )
                for h in range(heads)
            ],
            axis=1,
        )
        scores = jnp.dot(key_ref[span, at], stack, preferred_element_type=jnp.float32)
        scores = jnp.where(own, scores[:tokens], scores[tokens:])
        score_ref[n] = scores if side is None else scores + bias
    for n in range(len(parts)):
        scores = score_ref[n]
        peak = jnp.max(scores, axis=0, keepdims=True)
        raised = jnp.exp2((scores - peak) * scale)
        total = jnp.sum(raised, axis=0, keepdims=True)
        probs = (raised * (1.0 / total)).astype(jnp.bfloat16)
        prob_ref[n, :tokens] = jnp.where(own, probs, nothing)
        prob_ref[n, tokens:] = jnp.where(own, nothing, probs)
    for n, (p, g) in enumerate(parts):
        span = slice(p * LANES, (p + 1) * LANES)
        for h in range(0, heads, 2):
            at = g * group + h * HEAD_DIM
            both = jnp.dot(
                pack_ref[channels + at : channels + at + 2 * HEAD_DIM, span],
                prob_ref[n, :, h * LANES : (h + 2) * LANES],
                preferred_element_type=jnp.float32,
            ).astype(jnp.bfloat16)
            att_ref[at : at + HEAD_DIM, span] = both[:HEAD_DIM, :LANES]
            att_ref[at + HEAD_DIM : at + 2 * HEAD_DIM, span] = both[HEAD_DIM:, LANES:]
    mixed = lax.dot_general(
        att_ref[:, :size], out_ref[...], TN, preferred_element_type=jnp.float32
    )
    return [
        mixed[w * tokens : (w + 1) * tokens].reshape(WIN, WIN, channels)
        for w in range(len(windows))
    ]


def finish(begun, mixed, mlp_gain, up_ref, down_ref, decode_ref):
    residual = jnp.concatenate([a.reshape(CELLS, -1) + b.reshape(CELLS, -1) for a, b in zip(begun, mixed)])
    normed = normalize(residual, mlp_gain).astype(jnp.bfloat16)
    hidden = jax.nn.gelu(jnp.dot(normed, up_ref[...], preferred_element_type=jnp.float32))
    latent = residual + jnp.dot(
        hidden.astype(jnp.bfloat16), down_ref[...], preferred_element_type=jnp.float32
    )
    rounded = latent.astype(jnp.bfloat16)
    turned = [
        lax.dot_general(
            decode_ref[...],
            rounded[i * CELLS : i * CELLS + LANES],
            NT,
            preferred_element_type=jnp.float32,
        ).astype(jnp.bfloat16)
        for i in range(0, len(begun), 2)
    ]
    return latent, turned


def patch_order(patch_rows, patch_cols):
    inner = lambda r, c: 0 < r < patch_rows - 1 and 0 < c < patch_cols - 1
    every = [(r, c) for r in range(patch_rows) for c in range(patch_cols)]
    first = [at for at in every if inner(*at)]
    sides = [at for at in every if 0 < at[0] < patch_rows - 1 and not inner(*at)]
    ends = [at for at in every if not 0 < at[0] < patch_rows - 1]
    return first, sides, ends


def inner_block(
    start_ref, norm_ref, qkv_ref, out_ref, mlp_ref, up_ref, down_ref, decode_ref, latent_ref,
    proj_ref, mixed_ref, cells_ref, turned_ref, key_ref, pack_ref, att_ref, score_ref, prob_ref,
):
    tile_rows, tile_cols, channels = cells_ref.shape
    margin = WIN // 2
    feat_width = decode_ref.shape[0]
    cells_ref[...] = start_ref[...].astype(jnp.float32)
    turn_weights(qkv_ref, turned_ref)
    for row in range(0, tile_rows - WIN, WIN):
        cols = range(0, tile_cols - WIN, WIN)
        mixed = attend(
            cells_ref, [(row + margin, col + margin) for col in cols], None, norm_ref[...],
            qkv_ref, out_ref, turned_ref, key_ref, pack_ref, att_ref, score_ref, prob_ref,
        )
        for col, block in zip(cols, mixed):
            mixed_ref[row : row + WIN, col : col + WIN, :] = block
    first, _, _ = patch_order(tile_rows // PATCH, tile_cols // PATCH)
    done = 0
    for pr in sorted(set(r for r, _ in first)):
        here = [c for r, c in first if r == pr]
        row = pr * PATCH
        latent, turned = finish(
            [cells_ref[row : row + PATCH, c * PATCH : (c + 1) * PATCH, :] for c in here],
            [
                mixed_ref[
                    row - margin : row - margin + PATCH,
                    c * PATCH - margin : c * PATCH - margin + PATCH,
                    :,
                ]
                for c in here
            ],
            mlp_ref[...], up_ref, down_ref, decode_ref,
        )
        placed = latent.reshape(len(here), PATCH, PATCH, channels).transpose(1, 0, 2, 3)
        latent_ref[row - PATCH : row] = placed.reshape(PATCH, len(here) * PATCH, channels).astype(
            jnp.bfloat16
        )
        for pair in turned:
            proj_ref[done : done + feat_width, :] = pair
            done += feat_width


def outer_block(
    lat_cells, ext_ref, inner_latent_ref, inner_proj_ref, inner_mixed_ref, norm_ref, qkv_ref, out_ref,
    mlp_ref, up_ref, down_ref, decode_ref, latent_ref, proj_ref, mixed_ref, turned_ref, key_ref,
    pack_ref, att_ref, score_ref, prob_ref,
):
    ext_rows, ext_cols, channels = ext_ref.shape
    tile_rows, tile_cols, _ = latent_ref.shape
    margin = WIN // 2
    feat_width = decode_ref.shape[0]
    last_row, last_col = ext_rows - WIN, ext_cols - WIN
    top = lax.axis_index("lat") * tile_rows - margin
    turn_weights(qkv_ref, turned_ref)

    def place(windows, side):
        mixed = attend(
            ext_ref, windows, side, norm_ref[...], qkv_ref, out_ref, turned_ref, key_ref,
            pack_ref, att_ref, score_ref, prob_ref,
        )
        for (row, col), block in zip(windows, mixed):
            mixed_ref[row : row + WIN, col : col + WIN, :] = block

    for row in (0, last_row):
        side = lambda r: (top + row + r >= 0).astype(jnp.int32) + (
            top + row + r >= lat_cells
        ).astype(jnp.int32)
        place([(row, col) for col in range(0, ext_cols, WIN)], side)
    place([(row, col) for row in range(WIN, last_row, WIN) for col in (0, last_col)], None)
    mixed_ref[WIN:last_row, WIN:last_col, :] = inner_mixed_ref[...]
    _, sides, ends = patch_order(tile_rows // PATCH, tile_cols // PATCH)
    done = inner_proj_ref.shape[0]
    proj_ref[:done, :] = inner_proj_ref[...]

    def patches(here):
        at = [
            (
                slice(r * PATCH + margin, (r + 1) * PATCH + margin),
                slice(c * PATCH + margin, (c + 1) * PATCH + margin),
            )
            for r, c in here
        ]
        latent, turned = finish(
            [ext_ref[r, c, :] for r, c in at],
            [mixed_ref[r, c, :] for r, c in at],
            mlp_ref[...], up_ref, down_ref, decode_ref,
        )
        for i, pair in enumerate(turned):
            at = done + i * feat_width
            proj_ref[at : at + feat_width, :] = pair
        return latent.reshape(len(here), PATCH, PATCH, channels), len(turned) * feat_width

    latent, used = patches(sides)
    done += used
    for pr in sorted(set(r for r, _ in sides)):
        left, right = [latent[i] for i, (r, _) in enumerate(sides) if r == pr]
        inner = inner_latent_ref[(pr - 1) * PATCH : pr * PATCH].astype(jnp.float32)
        whole = jnp.concatenate([left, inner, right], axis=1)
        latent_ref[pr * PATCH : (pr + 1) * PATCH] = whole.astype(jnp.bfloat16)
    for pr in sorted(set(r for r, _ in ends)):
        latent, used = patches([at for at in ends if at[0] == pr])
        done += used
        placed = latent.transpose(1, 0, 2, 3).reshape(PATCH, tile_cols, channels)
        latent_ref[pr * PATCH : (pr + 1) * PATCH] = placed.astype(jnp.bfloat16)


def reply_patches(capacity, plane, tiles, order, feat_width, id_ref, *refs):
    tile_refs, out_ref, both_ref = refs[:tiles], refs[tiles], refs[tiles + 1]
    pairs = capacity // 2
    first = lax.broadcasted_iota(jnp.int32, (feat_width, LANES), 1) < CELLS
    for t in range(tiles):
        for i in range(0, len(order), 2):
            at = i // 2 * feat_width
            pair = tile_refs[t][at : at + feat_width, :].astype(jnp.float32)
            swapped = pltpu.roll(pair, CELLS, 1)
            both_ref[t, order[i]] = jnp.where(first, pair, swapped)
            both_ref[t, order[i + 1]] = jnp.where(first, swapped, pair)
    for r in range(plane):
        for t in range(tiles):
            for k in range(pairs):
                slot = (r * tiles + t) * capacity + 2 * k
                pair = jnp.where(
                    first, both_ref[t, id_ref[slot]], both_ref[t, id_ref[slot + 1]]
                )
                at = ((r * tiles + t) * pairs + k) * feat_width
                out_ref[at : at + feat_width, :] = pair.astype(jnp.bfloat16)


def decode_blocks(slot_ref, offset_ref, near_ref, far_ref, out_hbm, back_ref, out_ref, sems):
    feat_width, count = out_ref.shape
    blocks = count // BLK
    step = sems.shape[0]
    size = blocks // step
    back_ref[: near_ref.shape[0], :] = near_ref[...]
    back_ref[near_ref.shape[0] :, :] = far_ref[...]

    def one(b):
        slot = slot_ref[b]
        span = slice(b * BLK, (b + 1) * BLK)
        weights = block_weights(offset_ref[:, span].astype(jnp.float32))
        total = jnp.sum(weights.astype(jnp.float32), axis=0, keepdims=True)
        nothing = jnp.zeros_like(weights)
        low = lax.rem(slot, 2) == 0
        both = jnp.concatenate(
            [jnp.where(low, weights, nothing), jnp.where(low, nothing, weights)], axis=0
        )
        row = pl.multiple_of(lax.div(slot, 2) * feat_width, 16)
        values = back_ref[pl.ds(row, feat_width), :]
        mean = jnp.dot(values, both, preferred_element_type=jnp.float32) * (1.0 / total)
        out_ref[:, span] = mean.astype(jnp.bfloat16)

    copies = []
    for i in range(step):
        for b in range(i * size, (i + 1) * size):
            one(b)
        span = pl.ds(i * size * BLK, size * BLK)
        copies.append(pltpu.make_async_copy(out_ref.at[:, span], out_hbm.at[:, span], sems.at[i]))
        copies[i].start()
    for copy in copies:
        copy.wait()


def with_halo(array, sides, width):
    for axis, dim in sides:
        size, length = (axis_count(axis), array.shape[dim])
        up = [(i, (i + 1) % size) for i in range(size)]
        down = [(j, i) for i, j in up]
        last = lax.slice_in_dim(array, length - width, length, axis=dim)
        initial = lax.slice_in_dim(array, 0, width, axis=dim)
        before = lax.ppermute(last, axis, up)
        after = lax.ppermute(initial, axis, down)
        array = jnp.concatenate([before, array, after], axis=dim)
    return array


def axis_count(axes):
    axes = axes if isinstance(axes, tuple) else (axes,)
    return math.prod([lax.axis_size(axis) for axis in axes])


def swap_in_plane(array):
    plane = axis_count(("lat", "x"))
    parts = array.reshape(plane, -1, LANES)
    parts = lax.all_to_all(parts, ("lat", "x"), split_axis=0, concat_axis=0, tiled=True)
    return parts.reshape(array.shape)


def swap_at_once(gains, array):
    def apart(array):
        lat, width = lax.axis_size("lat"), lax.axis_size("x")
        parts = array.reshape(lat, width, -1, LANES)
        for dim, axis in enumerate(("lat", "x")):
            parts = lax.all_to_all(parts, axis, split_axis=dim, concat_axis=dim, tiled=True)
        return parts.reshape(array.shape)

    return lax.cond(gains[0] > 0.0, swap_in_plane, apart, array)


def swap_planes(array, hop):
    depth = lax.axis_size("z")
    return lax.ppermute(array, "z", [(i, i ^ hop) for i in range(depth)])


def local(
    obs_feat,
    obs_offset,
    block_tile,
    block_patch,
    embed_weight,
    grid_base,
    norm_gain,
    qkv_weight,
    out_weight,
    mlp_gain,
    up_weight,
    down_weight,
    decode_weight,
):
    lat, depth, width = (lax.axis_size(axis) for axis in ("lat", "z", "x"))
    plane, hops = lat * width, depth - 1
    devices = plane * depth
    feat_width, obs_count = obs_feat.shape
    blocks = obs_count // BLK
    capacity = max(2, 2 * blocks // devices)
    capacity += capacity % 2
    pairs = capacity // 2
    tile_rows, tile_cols, channels = grid_base.shape
    patch_total = (tile_rows // PATCH) * (tile_cols // PATCH)
    chunk = pairs * feat_width + meta_rows(pairs)
    dense = dense_rows(patch_total // 2, feat_width)
    steps = 3 if blocks % 3 == 0 else 1
    send_near, send_far, slots = pl.pallas_call(
        lambda *refs: encode_blocks(capacity, (lat, depth, width), *refs),
        out_shape=(
            jax.ShapeDtypeStruct((plane * chunk, LANES), jnp.bfloat16),
            jax.ShapeDtypeStruct((plane * hops * chunk, LANES), jnp.bfloat16),
            jax.ShapeDtypeStruct((blocks,), jnp.int32),
        ),
        in_specs=[pl.BlockSpec(memory_space=pltpu.HBM)] * 4,
        out_specs=(vmem(), vmem(), smem()),
        scratch_shapes=[
            pltpu.VMEM((devices * chunk, LANES), jnp.bfloat16),
            pltpu.SMEM((blocks,), jnp.int32),
            pltpu.SMEM((blocks,), jnp.int32),
            pltpu.VMEM(obs_feat.shape, jnp.bfloat16),
            pltpu.VMEM(obs_offset.shape, jnp.bfloat16),
            pltpu.SMEM((devices,), jnp.int32),
            pltpu.SemaphoreType.DMA((steps + 3,)),
        ],
        compiler_params=params(61),
        name="encode_blocks",
    )(block_tile.reshape(blocks), block_patch, obs_feat, obs_offset)

    def ids_of(recv, tiles):
        at = pairs * feat_width + 2 * pairs
        tags = recv.reshape(plane * tiles, chunk, LANES)[:, at : at + pairs, 0::CELLS]
        ids = tags.astype(jnp.float32).astype(jnp.int32) - 1
        return jnp.clip(ids, 0, patch_total - 1).reshape(-1)

    far = swap_in_plane(send_far)
    far_ids = ids_of(far, hops)
    sums = pl.pallas_call(
        lambda *refs: gather_planes(capacity, plane, hops, feat_width, *refs),
        out_shape=[jax.ShapeDtypeStruct((dense, LANES), jnp.bfloat16)] * hops,
        in_specs=[smem(), vmem()],
        out_specs=[vmem()] * hops,
        scratch_shapes=[pltpu.VMEM((patch_total, feat_width + 8, LANES), jnp.float32)] * (2 * hops),
        compiler_params=params(14),
        name="gather_planes",
    )(far_ids, far)
    parts = [swap_planes(sums[hop - 1], hop) for hop in range(hops, 0, -1)]
    send_near, _ = lax.optimization_barrier((send_near, sums))
    near = swap_at_once(norm_gain, send_near)
    near_ids = ids_of(near, 1)
    own = pl.pallas_call(
        lambda *refs: gather_own(capacity, plane, feat_width, *refs),
        out_shape=jax.ShapeDtypeStruct((patch_total // 2, feat_width + 8, LANES), jnp.float32),
        in_specs=[smem()] + [vmem()] * 3,
        out_specs=vmem(),
        scratch_shapes=[pltpu.VMEM((patch_total, feat_width + 8, LANES), jnp.float32)] * 2,
        compiler_params=params(10),
        cost_estimate=pl.CostEstimate(flops=10**9, bytes_accessed=10**7, transcendentals=0),
        name="gather_own",
    )(near_ids, near, qkv_weight, out_weight)

    start = pl.pallas_call(
        lambda *refs: start_tile(hops, *refs),
        out_shape=jax.ShapeDtypeStruct(grid_base.shape, jnp.bfloat16),
        in_specs=[vmem()] * (hops + 3),
        out_specs=vmem(),
        compiler_params=params(10),
        name="start_tile",
    )(own, *parts, embed_weight, grid_base)

    margin = WIN // 2
    ext = with_halo(start, (("lat", 0), (("z", "x"), 1)), margin).astype(jnp.float32)
    ext_rows, ext_cols, _ = ext.shape
    group = 128
    gains = (norm_gain.reshape(1, channels), mlp_gain.reshape(1, channels))
    weights = (gains[0], qkv_weight, out_weight, gains[1], up_weight, down_weight, decode_weight.T)
    patch_rows, patch_cols = tile_rows // PATCH, tile_cols // PATCH
    inner, sides, ends = patch_order(patch_rows, patch_cols)
    order = [r * patch_cols + c for r, c in inner + sides + ends]
    inner_cells = (tile_rows - 2 * PATCH, tile_cols - 2 * PATCH, channels)
    inner_mixed = (tile_rows - WIN, tile_cols - WIN, channels)

    def scratch(windows):
        count = -(-windows // 2)
        parts = count * channels // group
        lanes = group // HEAD_DIM * LANES
        return [
            pltpu.VMEM((2 * channels, channels), jnp.bfloat16),
            pltpu.VMEM((count * LANES, channels), jnp.bfloat16),
            pltpu.VMEM((2 * channels, count * LANES), jnp.bfloat16),
            pltpu.VMEM((channels, count * LANES), jnp.bfloat16),
            pltpu.VMEM((parts, WIN * WIN, lanes), jnp.float32),
            pltpu.VMEM((parts, LANES, lanes), jnp.bfloat16),
        ]

    latent_inner, proj_inner, mixed_inner = pl.pallas_call(
        inner_block,
        out_shape=(
            jax.ShapeDtypeStruct(inner_cells, jnp.bfloat16),
            jax.ShapeDtypeStruct((len(inner) // 2 * feat_width, LANES), jnp.bfloat16),
            jax.ShapeDtypeStruct(inner_mixed, jnp.float32),
        ),
        in_specs=[vmem()] * 8,
        out_specs=(vmem(), vmem(), vmem()),
        scratch_shapes=[pltpu.VMEM(grid_base.shape, jnp.float32)]
        + scratch(tile_cols // WIN - 1),
        compiler_params=params(16),
        cost_estimate=pl.CostEstimate(flops=6 * 10**9, bytes_accessed=10**7, transcendentals=0),
        name="inner_block",
    )(start, *weights)

    latent, projected = pl.pallas_call(
        lambda *refs: outer_block(tile_rows * lat, *refs),
        out_shape=(
            jax.ShapeDtypeStruct(grid_base.shape, jnp.bfloat16),
            jax.ShapeDtypeStruct((patch_total // 2 * feat_width, LANES), jnp.bfloat16),
        ),
        in_specs=[vmem()] * 11,
        out_specs=(vmem(), vmem()),
        scratch_shapes=[pltpu.VMEM((ext_rows, ext_cols, channels), jnp.float32)]
        + scratch(max(ext_cols // WIN, 2 * (ext_rows // WIN - 2))),
        compiler_params=params(20),
        cost_estimate=pl.CostEstimate(flops=8 * 10**9, bytes_accessed=10**7, transcendentals=0),
        name="outer_block",
    )(ext, latent_inner, proj_inner, mixed_inner, *weights)

    def reply(ids, tiles, name):
        count = len(tiles)
        return pl.pallas_call(
            lambda *refs: reply_patches(capacity, plane, count, order, feat_width, *refs),
            out_shape=jax.ShapeDtypeStruct(
                (plane * count * pairs * feat_width, LANES), jnp.bfloat16
            ),
            in_specs=[smem()] + [vmem()] * count,
            out_specs=vmem(),
            scratch_shapes=[pltpu.VMEM((count, patch_total, feat_width, LANES), jnp.float32)],
            compiler_params=params(12),
            cost_estimate=pl.CostEstimate(flops=10**9, bytes_accessed=10**7, transcendentals=0),
            name=name,
        )(ids, *tiles)

    others = [swap_planes(projected, hop) for hop in range(hops, 0, -1)][::-1]
    near_reply = reply(near_ids, [projected], "reply_near")
    near_back = swap_at_once(norm_gain, near_reply)
    far_back = swap_in_plane(reply(far_ids, others, "reply_far"))

    obs_out = pl.pallas_call(
        decode_blocks,
        out_shape=jax.ShapeDtypeStruct((feat_width, obs_count), jnp.bfloat16),
        in_specs=[smem(), vmem()] + [vmem()] * 2,
        out_specs=pl.BlockSpec(memory_space=pltpu.HBM),
        scratch_shapes=[
            pltpu.VMEM((devices * pairs * feat_width, LANES), jnp.bfloat16),
            pltpu.VMEM((feat_width, obs_count), jnp.bfloat16),
            pltpu.SemaphoreType.DMA((steps,)),
        ],
        compiler_params=params(12),
        name="decode_blocks",
    )(slots, obs_offset, near_back, far_back)
    return (latent, obs_out)


def solution(mesh):
    lat, lon = mesh.devices.shape
    width = lat // 2 if lat % 2 == 0 and lon % (lat // 2) == 0 else 1
    split = Mesh(mesh.devices.reshape(lat, lon // width, width), ("lat", "z", "x"))
    every = ("lat", "z", "x")
    placed = (
        P(None, every),
        P(None, every),
        P(every, None),
        P(every),
        P(),
        P("lat", ("z", "x"), None),
        P(),
        P(),
        P(),
        P(),
        P(),
        P(),
        P(),
    )
    return jax.shard_map(
        local,
        mesh=split,
        in_specs=placed,
        out_specs=(P("lat", ("z", "x"), None), P(None, every)),
        check_vma=False,
    )
```

```python
import math

import jax
import jax.numpy as jnp
from jax import lax
from jax.experimental import pallas as pl
from jax.experimental.pallas import tpu as pltpu
from jax.sharding import Mesh
from jax.sharding import PartitionSpec as P

HEAD_DIM = 32
WIN = 8
PATCH = 8
BLK = 128
CELLS = PATCH * PATCH
LANES = 2 * CELLS

epsilon = 1e-05
spread_coef = 0.5

NT = (((1,), (1,)), ((), ()))
TN = (((0,), (0,)), ((), ()))


def params(mib):
    return pltpu.CompilerParams(vmem_limit_bytes=mib * 1024 * 1024)


def vmem():
    return pl.BlockSpec(memory_space=pltpu.VMEM)


def smem():
    return pl.BlockSpec(memory_space=pltpu.SMEM)


def normalize(values, gain_row):
    center = jnp.mean(values, axis=-1, keepdims=True)
    centered = values - center
    variance = jnp.mean(centered * centered, axis=-1, keepdims=True)
    return centered * lax.rsqrt(variance + epsilon) * gain_row


def block_weights(offsets):
    axis_id = lax.broadcasted_iota(jnp.int32, (PATCH, BLK), 0).astype(jnp.float32) + 0.5
    row_gap = axis_id - offsets[0:1]
    col_gap = axis_id - offsets[1:2]
    row_gap = row_gap * row_gap
    col_gap = col_gap * col_gap
    total = row_gap[:, None, :] + col_gap[None, :, :]
    return jnp.exp(-spread_coef * total).reshape(CELLS, BLK).astype(jnp.bfloat16)


def meta_rows(pairs):
    return -(-3 * pairs // 16) * 16


def encode_blocks(
    capacity, shape, tile_hbm, patch_hbm, feat_hbm, offset_hbm, near_ref, far_ref,
    slot_ref, send_ref, tile_ref, patch_ref, feat_ref, offset_ref, count_ref, sems,
):
    lat, depth, width = shape
    devices = lat * depth * width
    plane_id = lax.axis_index("z")
    feat_width = feat_ref.shape[0]
    blocks = feat_ref.shape[1] // BLK
    step = sems.shape[0] - 3
    size = blocks // step
    pairs = capacity // 2
    meta = meta_rows(pairs)
    chunk = pairs * feat_width + meta
    small = [
        pltpu.make_async_copy(tile_hbm, tile_ref, sems.at[step]),
        pltpu.make_async_copy(patch_hbm, patch_ref, sems.at[step + 1]),
        pltpu.make_async_copy(offset_hbm, offset_ref, sems.at[step + 2]),
    ]
    large = []
    for i in range(step):
        span = pl.ds(i * size * BLK, size * BLK)
        large.append(pltpu.make_async_copy(feat_hbm.at[:, span], feat_ref.at[:, span], sems.at[i]))
    for copy in small + large:
        copy.start()
    send_ref[...] = jnp.zeros_like(send_ref)

    def clear(t, _):
        count_ref[t] = 0
        return 0

    lax.fori_loop(0, devices, clear, 0)
    lane_half = lax.broadcasted_iota(jnp.int32, (feat_width, LANES), 1) // CELLS
    meta_half = lax.broadcasted_iota(jnp.int32, (meta, LANES), 1) // CELLS
    meta_row = lax.broadcasted_iota(jnp.int32, (meta, LANES), 0)
    ones = jnp.ones((16, BLK), jnp.bfloat16)

    def one(b):
        tile = tile_ref[b]
        rank = count_ref[tile]
        count_ref[tile] = rank + 1
        lon = lax.rem(tile, depth * width)
        partner = lax.div(tile, depth * width) * width + lax.rem(lon, width)
        hop = lax.div(lon, width) ^ plane_id
        piece = jnp.where(hop == 0, partner, lat * width + partner * (depth - 1) + hop - 1)
        slot_ref[b] = piece * capacity + rank
        pair = lax.div(rank, 2)
        half = lax.rem(rank, 2)
        col = pl.multiple_of(b * BLK, BLK)
        feat = jnp.concatenate([feat_ref[:, pl.ds(col, BLK)], ones], axis=0)
        weights = block_weights(offset_ref[:, pl.ds(col, BLK)].astype(jnp.float32))
        twice = jnp.concatenate([weights, weights], axis=0)
        sums = lax.dot_general(feat, twice, NT, preferred_element_type=jnp.float32)
        row = pl.multiple_of(piece * chunk + pair * feat_width, 16)
        old = send_ref[pl.ds(row, feat_width), :].astype(jnp.float32)
        send_ref[pl.ds(row, feat_width), :] = jnp.where(
            lane_half == half, sums[:feat_width], old
        ).astype(jnp.bfloat16)
        mass = sums[feat_width : feat_width + 1]
        high = mass.astype(jnp.bfloat16).astype(jnp.float32)
        low = mass - high
        tag = (patch_ref[b] + 1).astype(jnp.float32)
        row = pl.multiple_of(piece * chunk + pairs * feat_width, 16)
        old = send_ref[pl.ds(row, meta), :].astype(jnp.float32)
        new = jnp.where(
            meta_row == pair,
            high,
            jnp.where(
                meta_row == pairs + pair, low, jnp.where(meta_row == 2 * pairs + pair, tag, old)
            ),
        )
        send_ref[pl.ds(row, meta), :] = jnp.where(meta_half == half, new, old).astype(jnp.bfloat16)

    for copy in small:
        copy.wait()
    for i in range(step):
        large[i].wait()
        for b in range(i * size, (i + 1) * size):
            one(b)
    near_ref[...] = send_ref[: near_ref.shape[0]]
    far_ref[...] = send_ref[near_ref.shape[0] :]


def dense_rows(pairs, feat_width):
    return pairs * feat_width + -(-2 * pairs // 16) * 16


def add_chunk(capacity, feat_width, id_ref, slot, recv_ref, base, low_ref, high_ref):
    pairs = capacity // 2
    tags = recv_ref[base + pairs * feat_width : base + pairs * feat_width + meta_rows(pairs), :]
    tags = tags.astype(jnp.float32)
    for k in range(pairs):
        at = base + k * feat_width
        sums = recv_ref[at : at + feat_width, :].astype(jnp.float32)
        mass = tags[k : k + 1] + tags[pairs + k : pairs + k + 1]
        both = jnp.concatenate([sums, jnp.broadcast_to(mass, (8, LANES))], axis=0)
        low_ref[id_ref[slot + 2 * k]] += both
        high_ref[id_ref[slot + 2 * k + 1]] += both


def paired(low_ref, high_ref, j):
    first = lax.broadcasted_iota(jnp.int32, low_ref.shape[1:], 1) < CELLS
    even = low_ref[2 * j] + pltpu.roll(high_ref[2 * j], CELLS, 1)
    odd = high_ref[2 * j + 1] + pltpu.roll(low_ref[2 * j + 1], CELLS, 1)
    return jnp.where(first, even, odd)


def gather_planes(capacity, plane, hops, feat_width, id_ref, recv_ref, *refs):
    outs, lows, highs = refs[:hops], refs[hops : 2 * hops], refs[2 * hops :]
    pairs = capacity // 2
    chunk = pairs * feat_width + meta_rows(pairs)
    patch_pairs = lows[0].shape[0] // 2
    for ref in lows + highs:
        ref[...] = jnp.zeros_like(ref)
    for r in range(plane):
        for hop in range(hops):
            n = r * hops + hop
            add_chunk(
                capacity, feat_width, id_ref, n * capacity, recv_ref, n * chunk, lows[hop], highs[hop]
            )
    for hop in range(hops):
        masses = []
        for j in range(patch_pairs):
            pair = paired(lows[hop], highs[hop], j)
            outs[hop][j * feat_width : (j + 1) * feat_width, :] = pair[:feat_width].astype(
                jnp.bfloat16
            )
            masses.append(pair[feat_width : feat_width + 1])
        masses = jnp.concatenate(masses, axis=0)
        high = masses.astype(jnp.bfloat16).astype(jnp.float32)
        spare = outs[hop].shape[0] - patch_pairs * (feat_width + 2)
        rows = [high, masses - high] + ([jnp.zeros((spare, LANES), jnp.float32)] if spare else [])
        outs[hop][patch_pairs * feat_width :, :] = jnp.concatenate(rows, axis=0).astype(jnp.bfloat16)


def gather_own(capacity, plane, feat_width, id_ref, recv_ref, *refs):
    own_ref, low_ref, high_ref = refs[-3:]
    chunk = recv_ref.shape[0] // plane
    low_ref[...] = jnp.zeros_like(low_ref)
    high_ref[...] = jnp.zeros_like(high_ref)
    for r in range(plane):
        add_chunk(
            capacity, feat_width, id_ref, r * capacity, recv_ref, r * chunk, low_ref, high_ref
        )
    for j in range(own_ref.shape[0]):
        own_ref[j] = paired(low_ref, high_ref, j)


def start_tile(hops, own_ref, *refs):
    parts = refs[:hops]
    embed_ref, base_ref, start_ref = refs[hops:]
    feat_width, channels = embed_ref.shape
    tile_rows, tile_cols, _ = base_ref.shape
    patch_rows, patch_cols = tile_rows // PATCH, tile_cols // PATCH
    patch_pairs = patch_rows * patch_cols // 2
    embed = embed_ref[...]
    mass_rows = [part[patch_pairs * feat_width :, :].astype(jnp.float32) for part in parts]
    for pr in range(patch_rows):
        lifted = []
        for pc in range(patch_cols // 2):
            j = pr * (patch_cols // 2) + pc
            pair = own_ref[j]
            sums, mass = pair[:feat_width], pair[feat_width : feat_width + 1]
            for part, rows in zip(parts, mass_rows):
                sums = sums + part[j * feat_width : (j + 1) * feat_width, :].astype(jnp.float32)
                mass = mass + (rows[j : j + 1] + rows[patch_pairs + j : patch_pairs + j + 1])
            encoded = (sums * (1.0 / (1.0 + mass))).astype(jnp.bfloat16)
            lifted.append(lax.dot_general(encoded, embed, TN, preferred_element_type=jnp.float32))
        lifted = jnp.concatenate(lifted, axis=0).reshape(patch_cols, PATCH, PATCH, channels)
        lifted = lifted.transpose(1, 0, 2, 3).reshape(PATCH, tile_cols, channels)
        rows = slice(pr * PATCH, (pr + 1) * PATCH)
        start_ref[rows] = (base_ref[rows].astype(jnp.float32) + lifted).astype(jnp.bfloat16)


def turn_weights(qkv_ref, turned_ref):
    channels = qkv_ref.shape[0]
    turned_ref[:channels] = qkv_ref[:, :channels].T
    turned_ref[channels:] = qkv_ref[:, 2 * channels :].T


def attend(
    cells_ref, windows, sides, norm_gain, qkv_ref, out_ref, turned_ref, key_ref, pack_ref, att_ref,
    score_ref, prob_ref,
):
    channels = qkv_ref.shape[0]
    tokens = WIN * WIN
    group = 128
    heads = group // HEAD_DIM
    count = -(-len(windows) // 2)
    size = count * LANES
    scale = HEAD_DIM ** (-0.5) / math.log(2.0)
    shape = (tokens, heads * LANES)
    own = lax.broadcasted_iota(jnp.int32, shape, 1) % LANES < tokens
    nothing = jnp.zeros(shape, jnp.bfloat16)
    empty = jnp.zeros((HEAD_DIM, LANES), jnp.bfloat16)
    cells = jnp.concatenate(
        [
            cells_ref[row : row + WIN, col : col + WIN, :].reshape(tokens, channels)
            for row, col in windows
        ],
        axis=0,
    )
    normed = normalize(cells, norm_gain).astype(jnp.bfloat16)
    if len(windows) % 2:
        normed = jnp.concatenate([normed, jnp.zeros((tokens, channels), jnp.bfloat16)], axis=0)
    key_ref[:size] = jnp.dot(
        normed, qkv_ref[:, channels : 2 * channels], preferred_element_type=jnp.float32
    ).astype(jnp.bfloat16)
    pack_ref[:, :size] = lax.dot_general(
        turned_ref[...], normed, NT, preferred_element_type=jnp.float32
    ).astype(jnp.bfloat16)
    key_row = lax.broadcasted_iota(jnp.int32, (tokens, LANES), 0) // WIN
    query_row = lax.broadcasted_iota(jnp.int32, (tokens, LANES), 1) % tokens // WIN
    bias = [None] * count
    for p, side in enumerate(sides):
        if side is not None:
            apart = jnp.where(side(key_row) == side(query_row), 0.0, -1e30)
            bias[p] = jnp.concatenate([apart] * heads, axis=1)
    parts = [(p, g) for p in range(count) for g in range(channels // group)]
    for n, (p, g) in enumerate(parts):
        span = slice(p * LANES, (p + 1) * LANES)
        at = slice(g * group, (g + 1) * group)
        query = pack_ref[at, span]
        stack = jnp.concatenate(
            [
                jnp.concatenate(
                    [
                        query[h * HEAD_DIM : (h + 1) * HEAD_DIM] if i == h else empty
                        for i in range(heads)
                    ],
                    axis=0,
                )
                for h in range(heads)
            ],
            axis=1,
        )
        scores = jnp.dot(key_ref[span, at], stack, preferred_element_type=jnp.float32)
        scores = jnp.where(own, scores[:tokens], scores[tokens:])
        score_ref[n] = scores if bias[p] is None else scores + bias[p]
    for n in range(len(parts)):
        scores = score_ref[n]
        peak = jnp.max(scores, axis=0, keepdims=True)
        raised = jnp.exp2((scores - peak) * scale)
        total = jnp.sum(raised, axis=0, keepdims=True)
        probs = (raised * (1.0 / total)).astype(jnp.bfloat16)
        prob_ref[n, :tokens] = jnp.where(own, probs, nothing)
        prob_ref[n, tokens:] = jnp.where(own, nothing, probs)
    for n, (p, g) in enumerate(parts):
        span = slice(p * LANES, (p + 1) * LANES)
        for h in range(0, heads, 2):
            at = g * group + h * HEAD_DIM
            both = jnp.dot(
                pack_ref[channels + at : channels + at + 2 * HEAD_DIM, span],
                prob_ref[n, :, h * LANES : (h + 2) * LANES],
                preferred_element_type=jnp.float32,
            ).astype(jnp.bfloat16)
            att_ref[at : at + HEAD_DIM, span] = both[:HEAD_DIM, :LANES]
            att_ref[at + HEAD_DIM : at + 2 * HEAD_DIM, span] = both[HEAD_DIM:, LANES:]
    mixed = lax.dot_general(
        att_ref[:, :size], out_ref[...], TN, preferred_element_type=jnp.float32
    )
    return [
        mixed[w * tokens : (w + 1) * tokens].reshape(WIN, WIN, channels)
        for w in range(len(windows))
    ]


def finish(begun, mixed, mlp_gain, up_ref, down_ref, decode_ref):
    residual = jnp.concatenate([a.reshape(CELLS, -1) + b.reshape(CELLS, -1) for a, b in zip(begun, mixed)])
    normed = normalize(residual, mlp_gain).astype(jnp.bfloat16)
    hidden = jax.nn.gelu(jnp.dot(normed, up_ref[...], preferred_element_type=jnp.float32))
    latent = residual + jnp.dot(
        hidden.astype(jnp.bfloat16), down_ref[...], preferred_element_type=jnp.float32
    )
    rounded = latent.astype(jnp.bfloat16)
    turned = [
        lax.dot_general(
            decode_ref[...],
            rounded[i * CELLS : i * CELLS + LANES],
            NT,
            preferred_element_type=jnp.float32,
        ).astype(jnp.bfloat16)
        for i in range(0, len(begun), 2)
    ]
    return latent, turned


def patch_order(patch_rows, patch_cols):
    every = [(r, c) for r in range(patch_rows) for c in range(patch_cols)]
    middle = [(r, c) for r, c in every if 0 < c < patch_cols - 1]
    first = [(r, c) for r, c in middle if 0 < r < patch_rows - 1]
    ends = [at for at in middle if at not in first]
    return first, ends, [at for at in every if at not in middle]


def edge_side(top, row, lat_cells):
    return lambda r: (top + row + r >= 0).astype(jnp.int32) + (
        top + row + r >= lat_cells
    ).astype(jnp.int32)


def inner_block(
    start_ref, norm_ref, qkv_ref, out_ref, mlp_ref, up_ref, down_ref, decode_ref, latent_ref,
    proj_ref, mixed_ref, cells_ref, turned_ref, key_ref, pack_ref, att_ref, score_ref, prob_ref,
):
    tile_rows, tile_cols, channels = cells_ref.shape
    margin = WIN // 2
    feat_width = decode_ref.shape[0]
    cells_ref[...] = start_ref[...].astype(jnp.float32)
    turn_weights(qkv_ref, turned_ref)
    for row in range(0, tile_rows - WIN, WIN):
        cols = range(0, tile_cols - WIN, WIN)
        mixed = attend(
            cells_ref, [(row + margin, col + margin) for col in cols], [], norm_ref[...],
            qkv_ref, out_ref, turned_ref, key_ref, pack_ref, att_ref, score_ref, prob_ref,
        )
        for col, block in zip(cols, mixed):
            mixed_ref[row : row + WIN, col : col + WIN, :] = block
    first, _, _ = patch_order(tile_rows // PATCH, tile_cols // PATCH)
    done = 0
    for pr in sorted(set(r for r, _ in first)):
        here = [c for r, c in first if r == pr]
        row = pr * PATCH
        latent, turned = finish(
            [cells_ref[row : row + PATCH, c * PATCH : (c + 1) * PATCH, :] for c in here],
            [
                mixed_ref[
                    row - margin : row - margin + PATCH,
                    c * PATCH - margin : c * PATCH - margin + PATCH,
                    :,
                ]
                for c in here
            ],
            mlp_ref[...], up_ref, down_ref, decode_ref,
        )
        placed = latent.reshape(len(here), PATCH, PATCH, channels).transpose(1, 0, 2, 3)
        latent_ref[row - PATCH : row] = placed.reshape(PATCH, len(here) * PATCH, channels).astype(
            jnp.bfloat16
        )
        for pair in turned:
            proj_ref[done : done + feat_width, :] = pair
            done += feat_width


def tall_block(
    lat_cells, tall_ref, inner_mixed_ref, norm_ref, qkv_ref, out_ref, mlp_ref, up_ref, down_ref,
    decode_ref, latent_ref, proj_ref, mixed_ref, cells_ref, turned_ref, key_ref, pack_ref,
    att_ref, score_ref, prob_ref,
):
    rows, tile_cols, channels = tall_ref.shape
    margin = WIN // 2
    tile_rows = rows - 2 * margin
    feat_width = decode_ref.shape[0]
    last = rows - WIN
    top = lax.axis_index("lat") * tile_rows - margin
    turn_weights(qkv_ref, turned_ref)
    for part in (slice(0, 2 * WIN), slice(rows - 2 * WIN, rows)):
        cells_ref[part] = tall_ref[part].astype(jnp.float32)
    cols = range(0, tile_cols - WIN, WIN)
    for i, row in enumerate((0, last)):
        mixed = attend(
            cells_ref, [(row, col + margin) for col in cols],
            [edge_side(top, row, lat_cells)] * -(-len(cols) // 2), norm_ref[...], qkv_ref,
            out_ref, turned_ref, key_ref, pack_ref, att_ref, score_ref, prob_ref,
        )
        for col, block in zip(cols, mixed):
            mixed_ref[i * WIN : (i + 1) * WIN, col : col + WIN, :] = block
    here = range(1, tile_cols // PATCH - 1)
    done = 0
    for i, row in enumerate((margin, last - margin)):
        begun, mixed = [], []
        for c in here:
            span = slice(c * PATCH - margin, (c + 1) * PATCH - margin)
            begun.append(cells_ref[row : row + PATCH, c * PATCH : (c + 1) * PATCH, :])
            if i == 0:
                halves = [mixed_ref[margin:WIN, span, :], inner_mixed_ref[:margin, span, :]]
            else:
                halves = [
                    inner_mixed_ref[tile_rows - WIN - margin :, span, :],
                    mixed_ref[WIN : WIN + margin, span, :],
                ]
            mixed.append(jnp.concatenate(halves, axis=0))
        latent, turned = finish(begun, mixed, mlp_ref[...], up_ref, down_ref, decode_ref)
        placed = latent.reshape(len(here), PATCH, PATCH, channels).transpose(1, 0, 2, 3)
        latent_ref[i * PATCH : (i + 1) * PATCH] = placed.reshape(
            PATCH, len(here) * PATCH, channels
        ).astype(jnp.bfloat16)
        for pair in turned:
            proj_ref[done : done + feat_width, :] = pair
            done += feat_width


def outer_block(
    lat_cells, ext_ref, inner_latent_ref, inner_proj_ref, inner_mixed_ref, tall_latent_ref,
    tall_proj_ref, tall_mixed_ref, norm_ref, qkv_ref, out_ref, mlp_ref, up_ref, down_ref,
    decode_ref, latent_ref, proj_ref, mixed_ref, turned_ref, key_ref, pack_ref, att_ref,
    score_ref, prob_ref,
):
    ext_rows, ext_cols, channels = ext_ref.shape
    tile_rows, tile_cols, _ = latent_ref.shape
    margin = WIN // 2
    feat_width = decode_ref.shape[0]
    last_row, last_col = ext_rows - WIN, ext_cols - WIN
    top = lax.axis_index("lat") * tile_rows - margin
    turn_weights(qkv_ref, turned_ref)
    mixed_ref[WIN:last_row, WIN:last_col, :] = inner_mixed_ref[...]
    mixed_ref[:WIN, WIN:last_col, :] = tall_mixed_ref[:WIN]
    mixed_ref[last_row:, WIN:last_col, :] = tall_mixed_ref[WIN:]
    windows = [(row, col) for row in range(0, ext_rows, WIN) for col in (0, last_col)]
    sides = [
        edge_side(top, row, lat_cells) if row in (0, last_row) else None
        for row in range(0, ext_rows, WIN)
    ]
    mixed = attend(
        ext_ref, windows, sides, norm_ref[...], qkv_ref, out_ref, turned_ref, key_ref, pack_ref,
        att_ref, score_ref, prob_ref,
    )
    for (row, col), block in zip(windows, mixed):
        mixed_ref[row : row + WIN, col : col + WIN, :] = block
    done = inner_proj_ref.shape[0]
    proj_ref[:done, :] = inner_proj_ref[...]
    proj_ref[done : done + tall_proj_ref.shape[0], :] = tall_proj_ref[...]
    done += tall_proj_ref.shape[0]
    patch_rows = tile_rows // PATCH
    _, _, here = patch_order(patch_rows, tile_cols // PATCH)
    at = [
        (
            slice(r * PATCH + margin, (r + 1) * PATCH + margin),
            slice(c * PATCH + margin, (c + 1) * PATCH + margin),
        )
        for r, c in here
    ]
    latent, turned = finish(
        [ext_ref[r, c, :] for r, c in at],
        [mixed_ref[r, c, :] for r, c in at],
        mlp_ref[...], up_ref, down_ref, decode_ref,
    )
    for pair in turned:
        proj_ref[done : done + feat_width, :] = pair
        done += feat_width
    latent = latent.reshape(len(here), PATCH, PATCH, channels)
    for pr in range(patch_rows):
        left, right = [latent[i] for i, (r, _) in enumerate(here) if r == pr]
        if 0 < pr < patch_rows - 1:
            middle = inner_latent_ref[(pr - 1) * PATCH : pr * PATCH]
        else:
            middle = tall_latent_ref[:PATCH] if pr == 0 else tall_latent_ref[PATCH:]
        whole = jnp.concatenate([left, middle.astype(jnp.float32), right], axis=1)
        latent_ref[pr * PATCH : (pr + 1) * PATCH] = whole.astype(jnp.bfloat16)


def reply_patches(capacity, plane, tiles, order, feat_width, id_ref, *refs):
    tile_refs, out_ref, both_ref = refs[:tiles], refs[tiles], refs[tiles + 1]
    pairs = capacity // 2
    first = lax.broadcasted_iota(jnp.int32, (feat_width, LANES), 1) < CELLS
    for t in range(tiles):
        for i in range(0, len(order), 2):
            at = i // 2 * feat_width
            pair = tile_refs[t][at : at + feat_width, :].astype(jnp.float32)
            swapped = pltpu.roll(pair, CELLS, 1)
            both_ref[t, order[i]] = jnp.where(first, pair, swapped)
            both_ref[t, order[i + 1]] = jnp.where(first, swapped, pair)
    for r in range(plane):
        for t in range(tiles):
            for k in range(pairs):
                slot = (r * tiles + t) * capacity + 2 * k
                pair = jnp.where(
                    first, both_ref[t, id_ref[slot]], both_ref[t, id_ref[slot + 1]]
                )
                at = ((r * tiles + t) * pairs + k) * feat_width
                out_ref[at : at + feat_width, :] = pair.astype(jnp.bfloat16)


def decode_blocks(slot_ref, offset_ref, near_ref, far_ref, out_hbm, back_ref, out_ref, sems):
    feat_width, count = out_ref.shape
    blocks = count // BLK
    step = sems.shape[0]
    size = blocks // step
    back_ref[: near_ref.shape[0], :] = near_ref[...]
    back_ref[near_ref.shape[0] :, :] = far_ref[...]

    def one(b):
        slot = slot_ref[b]
        span = slice(b * BLK, (b + 1) * BLK)
        weights = block_weights(offset_ref[:, span].astype(jnp.float32))
        total = jnp.sum(weights.astype(jnp.float32), axis=0, keepdims=True)
        nothing = jnp.zeros_like(weights)
        low = lax.rem(slot, 2) == 0
        both = jnp.concatenate(
            [jnp.where(low, weights, nothing), jnp.where(low, nothing, weights)], axis=0
        )
        row = pl.multiple_of(lax.div(slot, 2) * feat_width, 16)
        values = back_ref[pl.ds(row, feat_width), :]
        mean = jnp.dot(values, both, preferred_element_type=jnp.float32) * (1.0 / total)
        out_ref[:, span] = mean.astype(jnp.bfloat16)

    copies = []
    for i in range(step):
        for b in range(i * size, (i + 1) * size):
            one(b)
        span = pl.ds(i * size * BLK, size * BLK)
        copies.append(pltpu.make_async_copy(out_ref.at[:, span], out_hbm.at[:, span], sems.at[i]))
        copies[i].start()
    for copy in copies:
        copy.wait()


def with_halo(array, axis, dim, width):
    size, length = (axis_count(axis), array.shape[dim])
    up = [(i, (i + 1) % size) for i in range(size)]
    down = [(j, i) for i, j in up]
    last = lax.slice_in_dim(array, length - width, length, axis=dim)
    initial = lax.slice_in_dim(array, 0, width, axis=dim)
    before = lax.ppermute(last, axis, up)
    after = lax.ppermute(initial, axis, down)
    return jnp.concatenate([before, array, after], axis=dim)


def axis_count(axes):
    axes = axes if isinstance(axes, tuple) else (axes,)
    return math.prod([lax.axis_size(axis) for axis in axes])


def swap_in_plane(array):
    plane = axis_count(("lat", "x"))
    parts = array.reshape(plane, -1, LANES)
    parts = lax.all_to_all(parts, ("lat", "x"), split_axis=0, concat_axis=0, tiled=True)
    return parts.reshape(array.shape)


def swap_at_once(gains, array):
    def apart(array):
        lat, width = lax.axis_size("lat"), lax.axis_size("x")
        parts = array.reshape(lat, width, -1, LANES)
        for dim, axis in enumerate(("lat", "x")):
            parts = lax.all_to_all(parts, axis, split_axis=dim, concat_axis=dim, tiled=True)
        return parts.reshape(array.shape)

    return lax.cond(gains[0] > 0.0, swap_in_plane, apart, array)


def swap_planes(array, hop):
    depth = lax.axis_size("z")
    return lax.ppermute(array, "z", [(i, i ^ hop) for i in range(depth)])


def local(
    obs_feat,
    obs_offset,
    block_tile,
    block_patch,
    embed_weight,
    grid_base,
    norm_gain,
    qkv_weight,
    out_weight,
    mlp_gain,
    up_weight,
    down_weight,
    decode_weight,
):
    lat, depth, width = (lax.axis_size(axis) for axis in ("lat", "z", "x"))
    plane, hops = lat * width, depth - 1
    devices = plane * depth
    feat_width, obs_count = obs_feat.shape
    blocks = obs_count // BLK
    capacity = max(2, 2 * blocks // devices)
    capacity += capacity % 2
    pairs = capacity // 2
    tile_rows, tile_cols, channels = grid_base.shape
    patch_total = (tile_rows // PATCH) * (tile_cols // PATCH)
    chunk = pairs * feat_width + meta_rows(pairs)
    dense = dense_rows(patch_total // 2, feat_width)
    steps = 3 if blocks % 3 == 0 else 1
    send_near, send_far, slots = pl.pallas_call(
        lambda *refs: encode_blocks(capacity, (lat, depth, width), *refs),
        out_shape=(
            jax.ShapeDtypeStruct((plane * chunk, LANES), jnp.bfloat16),
            jax.ShapeDtypeStruct((plane * hops * chunk, LANES), jnp.bfloat16),
            jax.ShapeDtypeStruct((blocks,), jnp.int32),
        ),
        in_specs=[pl.BlockSpec(memory_space=pltpu.HBM)] * 4,
        out_specs=(vmem(), vmem(), smem()),
        scratch_shapes=[
            pltpu.VMEM((devices * chunk, LANES), jnp.bfloat16),
            pltpu.SMEM((blocks,), jnp.int32),
            pltpu.SMEM((blocks,), jnp.int32),
            pltpu.VMEM(obs_feat.shape, jnp.bfloat16),
            pltpu.VMEM(obs_offset.shape, jnp.bfloat16),
            pltpu.SMEM((devices,), jnp.int32),
            pltpu.SemaphoreType.DMA((steps + 3,)),
        ],
        compiler_params=params(61),
        name="encode_blocks",
    )(block_tile.reshape(blocks), block_patch, obs_feat, obs_offset)

    def ids_of(recv, tiles):
        at = pairs * feat_width + 2 * pairs
        tags = recv.reshape(plane * tiles, chunk, LANES)[:, at : at + pairs, 0::CELLS]
        ids = tags.astype(jnp.float32).astype(jnp.int32) - 1
        return jnp.clip(ids, 0, patch_total - 1).reshape(-1)

    far = swap_in_plane(send_far)
    far_ids = ids_of(far, hops)
    sums = pl.pallas_call(
        lambda *refs: gather_planes(capacity, plane, hops, feat_width, *refs),
        out_shape=[jax.ShapeDtypeStruct((dense, LANES), jnp.bfloat16)] * hops,
        in_specs=[smem(), vmem()],
        out_specs=[vmem()] * hops,
        scratch_shapes=[pltpu.VMEM((patch_total, feat_width + 8, LANES), jnp.float32)] * (2 * hops),
        compiler_params=params(14),
        name="gather_planes",
    )(far_ids, far)
    parts = [swap_planes(sums[hop - 1], hop) for hop in range(hops, 0, -1)]
    send_near, _ = lax.optimization_barrier((send_near, sums))
    near = swap_at_once(norm_gain, send_near)
    near_ids = ids_of(near, 1)
    own = pl.pallas_call(
        lambda *refs: gather_own(capacity, plane, feat_width, *refs),
        out_shape=jax.ShapeDtypeStruct((patch_total // 2, feat_width + 8, LANES), jnp.float32),
        in_specs=[smem()] + [vmem()] * 3,
        out_specs=vmem(),
        scratch_shapes=[pltpu.VMEM((patch_total, feat_width + 8, LANES), jnp.float32)] * 2,
        compiler_params=params(10),
        cost_estimate=pl.CostEstimate(flops=10**9, bytes_accessed=10**7, transcendentals=0),
        name="gather_own",
    )(near_ids, near, qkv_weight, out_weight)

    start = pl.pallas_call(
        lambda *refs: start_tile(hops, *refs),
        out_shape=jax.ShapeDtypeStruct(grid_base.shape, jnp.bfloat16),
        in_specs=[vmem()] * (hops + 3),
        out_specs=vmem(),
        compiler_params=params(10),
        name="start_tile",
    )(own, *parts, embed_weight, grid_base)

    margin = WIN // 2
    ext_rows, ext_cols = tile_rows + 2 * margin, tile_cols + 2 * margin
    tall = with_halo(start, "lat", 0, margin)
    group = 128
    gains = (norm_gain.reshape(1, channels), mlp_gain.reshape(1, channels))
    weights = (gains[0], qkv_weight, out_weight, gains[1], up_weight, down_weight, decode_weight.T)
    patch_rows, patch_cols = tile_rows // PATCH, tile_cols // PATCH
    inner, ends, sides = patch_order(patch_rows, patch_cols)
    order = [r * patch_cols + c for r, c in inner + ends + sides]
    inner_cells = (tile_rows - 2 * PATCH, tile_cols - 2 * PATCH, channels)
    inner_mixed = (tile_rows - WIN, tile_cols - WIN, channels)

    def scratch(windows):
        count = -(-windows // 2)
        parts = count * channels // group
        lanes = group // HEAD_DIM * LANES
        return [
            pltpu.VMEM((2 * channels, channels), jnp.bfloat16),
            pltpu.VMEM((count * LANES, channels), jnp.bfloat16),
            pltpu.VMEM((2 * channels, count * LANES), jnp.bfloat16),
            pltpu.VMEM((channels, count * LANES), jnp.bfloat16),
            pltpu.VMEM((parts, WIN * WIN, lanes), jnp.float32),
            pltpu.VMEM((parts, LANES, lanes), jnp.bfloat16),
        ]

    latent_inner, proj_inner, mixed_inner = pl.pallas_call(
        inner_block,
        out_shape=(
            jax.ShapeDtypeStruct(inner_cells, jnp.bfloat16),
            jax.ShapeDtypeStruct((len(inner) // 2 * feat_width, LANES), jnp.bfloat16),
            jax.ShapeDtypeStruct(inner_mixed, jnp.float32),
        ),
        in_specs=[vmem()] * 8,
        out_specs=(vmem(), vmem(), vmem()),
        scratch_shapes=[pltpu.VMEM(grid_base.shape, jnp.float32)]
        + scratch(tile_cols // WIN - 1),
        compiler_params=params(16),
        cost_estimate=pl.CostEstimate(flops=6 * 10**9, bytes_accessed=10**7, transcendentals=0),
        name="inner_block",
    )(start, *weights)

    tall, proj_inner = lax.optimization_barrier((tall, proj_inner))
    ext = with_halo(tall, ("z", "x"), 1, margin).astype(jnp.float32)

    latent_tall, proj_tall, mixed_tall = pl.pallas_call(
        lambda *refs: tall_block(tile_rows * lat, *refs),
        out_shape=(
            jax.ShapeDtypeStruct((2 * PATCH,) + inner_cells[1:], jnp.bfloat16),
            jax.ShapeDtypeStruct((len(ends) // 2 * feat_width, LANES), jnp.bfloat16),
            jax.ShapeDtypeStruct((2 * WIN,) + inner_mixed[1:], jnp.float32),
        ),
        in_specs=[vmem()] * 9,
        out_specs=(vmem(), vmem(), vmem()),
        scratch_shapes=[pltpu.VMEM(tall.shape, jnp.float32)] + scratch(tile_cols // WIN - 1),
        compiler_params=params(16),
        cost_estimate=pl.CostEstimate(flops=5 * 10**9, bytes_accessed=10**7, transcendentals=0),
        name="tall_block",
    )(tall, mixed_inner, *weights)

    latent, projected = pl.pallas_call(
        lambda *refs: outer_block(tile_rows * lat, *refs),
        out_shape=(
            jax.ShapeDtypeStruct(grid_base.shape, jnp.bfloat16),
            jax.ShapeDtypeStruct((patch_total // 2 * feat_width, LANES), jnp.bfloat16),
        ),
        in_specs=[vmem()] * 14,
        out_specs=(vmem(), vmem()),
        scratch_shapes=[pltpu.VMEM((ext_rows, ext_cols, channels), jnp.float32)]
        + scratch(2 * (ext_rows // WIN)),
        compiler_params=params(20),
        cost_estimate=pl.CostEstimate(flops=5 * 10**9, bytes_accessed=10**7, transcendentals=0),
        name="outer_block",
    )(
        ext, latent_inner, proj_inner, mixed_inner, latent_tall, proj_tall, mixed_tall, *weights
    )

    def reply(ids, tiles, name):
        count = len(tiles)
        return pl.pallas_call(
            lambda *refs: reply_patches(capacity, plane, count, order, feat_width, *refs),
            out_shape=jax.ShapeDtypeStruct(
                (plane * count * pairs * feat_width, LANES), jnp.bfloat16
            ),
            in_specs=[smem()] + [vmem()] * count,
            out_specs=vmem(),
            scratch_shapes=[pltpu.VMEM((count, patch_total, feat_width, LANES), jnp.float32)],
            compiler_params=params(12),
            cost_estimate=pl.CostEstimate(flops=10**9, bytes_accessed=10**7, transcendentals=0),
            name=name,
        )(ids, *tiles)

    others = [swap_planes(projected, hop) for hop in range(hops, 0, -1)][::-1]
    near_reply = reply(near_ids, [projected], "reply_near")
    near_back = swap_at_once(norm_gain, near_reply)
    far_back = swap_in_plane(reply(far_ids, others, "reply_far"))

    obs_out = pl.pallas_call(
        decode_blocks,
        out_shape=jax.ShapeDtypeStruct((feat_width, obs_count), jnp.bfloat16),
        in_specs=[smem(), vmem()] + [vmem()] * 2,
        out_specs=pl.BlockSpec(memory_space=pltpu.HBM),
        scratch_shapes=[
            pltpu.VMEM((devices * pairs * feat_width, LANES), jnp.bfloat16),
            pltpu.VMEM((feat_width, obs_count), jnp.bfloat16),
            pltpu.SemaphoreType.DMA((steps,)),
        ],
        compiler_params=params(12),
        name="decode_blocks",
    )(slots, obs_offset, near_back, far_back)
    return (latent, obs_out)


def solution(mesh):
    lat, lon = mesh.devices.shape
    width = lat // 2 if lat % 2 == 0 and lon % (lat // 2) == 0 else 1
    split = Mesh(mesh.devices.reshape(lat, lon // width, width), ("lat", "z", "x"))
    every = ("lat", "z", "x")
    placed = (
        P(None, every),
        P(None, every),
        P(every, None),
        P(every),
        P(),
        P("lat", ("z", "x"), None),
        P(),
        P(),
        P(),
        P(),
        P(),
        P(),
        P(),
    )
    return jax.shard_map(
        local,
        mesh=split,
        in_specs=placed,
        out_specs=(P("lat", ("z", "x"), None), P(None, every)),
        check_vma=False,
    )
```

```python
import math

import jax
import jax.numpy as jnp
from jax import lax
from jax.experimental import pallas as pl
from jax.experimental.pallas import tpu as pltpu
from jax.sharding import Mesh
from jax.sharding import PartitionSpec as P

HEAD_DIM = 32
WIN = 8
PATCH = 8
BLK = 128
CELLS = PATCH * PATCH
LANES = 2 * CELLS

epsilon = 1e-05
spread_coef = 0.5

NT = (((1,), (1,)), ((), ()))
TN = (((0,), (0,)), ((), ()))


def params(mib):
    return pltpu.CompilerParams(vmem_limit_bytes=mib * 1024 * 1024)


def vmem():
    return pl.BlockSpec(memory_space=pltpu.VMEM)


def smem():
    return pl.BlockSpec(memory_space=pltpu.SMEM)


def normalize(values, gain_row):
    center = jnp.mean(values, axis=-1, keepdims=True)
    centered = values - center
    variance = jnp.mean(centered * centered, axis=-1, keepdims=True)
    return centered * lax.rsqrt(variance + epsilon) * gain_row


def block_weights(offsets):
    axis_id = lax.broadcasted_iota(jnp.int32, (PATCH, BLK), 0).astype(jnp.float32) + 0.5
    row_gap = axis_id - offsets[0:1]
    col_gap = axis_id - offsets[1:2]
    row_gap = row_gap * row_gap
    col_gap = col_gap * col_gap
    total = row_gap[:, None, :] + col_gap[None, :, :]
    return jnp.exp(-spread_coef * total).reshape(CELLS, BLK).astype(jnp.bfloat16)


def meta_rows(pairs):
    return -(-3 * pairs // 16) * 16


def encode_blocks(
    capacity, shape, tile_hbm, patch_hbm, feat_hbm, offset_hbm, near_ref, far_ref,
    slot_ref, send_ref, tile_ref, patch_ref, feat_ref, offset_ref, count_ref, sems,
):
    lat, depth, width = shape
    devices = lat * depth * width
    plane_id = lax.axis_index("z")
    feat_width = feat_ref.shape[0]
    blocks = feat_ref.shape[1] // BLK
    step = sems.shape[0] - 3
    size = blocks // step
    pairs = capacity // 2
    meta = meta_rows(pairs)
    chunk = pairs * feat_width + meta
    small = [
        pltpu.make_async_copy(tile_hbm, tile_ref, sems.at[step]),
        pltpu.make_async_copy(patch_hbm, patch_ref, sems.at[step + 1]),
        pltpu.make_async_copy(offset_hbm, offset_ref, sems.at[step + 2]),
    ]
    large = []
    for i in range(step):
        span = pl.ds(i * size * BLK, size * BLK)
        large.append(pltpu.make_async_copy(feat_hbm.at[:, span], feat_ref.at[:, span], sems.at[i]))
    for copy in small + large:
        copy.start()
    send_ref[...] = jnp.zeros_like(send_ref)

    def clear(t, _):
        count_ref[t] = 0
        return 0

    lax.fori_loop(0, devices, clear, 0)
    lane_half = lax.broadcasted_iota(jnp.int32, (feat_width, LANES), 1) // CELLS
    meta_half = lax.broadcasted_iota(jnp.int32, (meta, LANES), 1) // CELLS
    meta_row = lax.broadcasted_iota(jnp.int32, (meta, LANES), 0)
    ones = jnp.ones((16, BLK), jnp.bfloat16)

    def one(b):
        tile = tile_ref[b]
        rank = count_ref[tile]
        count_ref[tile] = rank + 1
        lon = lax.rem(tile, depth * width)
        partner = lax.div(tile, depth * width) * width + lax.rem(lon, width)
        hop = lax.div(lon, width) ^ plane_id
        piece = jnp.where(hop == 0, partner, lat * width + partner * (depth - 1) + hop - 1)
        slot_ref[b] = piece * capacity + rank
        pair = lax.div(rank, 2)
        half = lax.rem(rank, 2)
        col = pl.multiple_of(b * BLK, BLK)
        feat = jnp.concatenate([feat_ref[:, pl.ds(col, BLK)], ones], axis=0)
        weights = block_weights(offset_ref[:, pl.ds(col, BLK)].astype(jnp.float32))
        twice = jnp.concatenate([weights, weights], axis=0)
        sums = lax.dot_general(feat, twice, NT, preferred_element_type=jnp.float32)
        row = pl.multiple_of(piece * chunk + pair * feat_width, 16)
        old = send_ref[pl.ds(row, feat_width), :].astype(jnp.float32)
        send_ref[pl.ds(row, feat_width), :] = jnp.where(
            lane_half == half, sums[:feat_width], old
        ).astype(jnp.bfloat16)
        mass = sums[feat_width : feat_width + 1]
        high = mass.astype(jnp.bfloat16).astype(jnp.float32)
        low = mass - high
        tag = (patch_ref[b] + 1).astype(jnp.float32)
        row = pl.multiple_of(piece * chunk + pairs * feat_width, 16)
        old = send_ref[pl.ds(row, meta), :].astype(jnp.float32)
        new = jnp.where(
            meta_row == pair,
            high,
            jnp.where(
                meta_row == pairs + pair, low, jnp.where(meta_row == 2 * pairs + pair, tag, old)
            ),
        )
        send_ref[pl.ds(row, meta), :] = jnp.where(meta_half == half, new, old).astype(jnp.bfloat16)

    for copy in small:
        copy.wait()
    for i in range(step):
        large[i].wait()
        for b in range(i * size, (i + 1) * size):
            one(b)
    near_ref[...] = send_ref[: near_ref.shape[0]]
    far_ref[...] = send_ref[near_ref.shape[0] :]


def dense_rows(pairs, feat_width):
    return pairs * feat_width + -(-2 * pairs // 16) * 16


def add_chunk(capacity, feat_width, id_ref, slot, recv_ref, base, low_ref, high_ref):
    pairs = capacity // 2
    tags = recv_ref[base + pairs * feat_width : base + pairs * feat_width + meta_rows(pairs), :]
    tags = tags.astype(jnp.float32)
    for k in range(pairs):
        at = base + k * feat_width
        sums = recv_ref[at : at + feat_width, :].astype(jnp.float32)
        mass = tags[k : k + 1] + tags[pairs + k : pairs + k + 1]
        both = jnp.concatenate([sums, jnp.broadcast_to(mass, (8, LANES))], axis=0)
        low_ref[id_ref[slot + 2 * k]] += both
        high_ref[id_ref[slot + 2 * k + 1]] += both


def paired(low_ref, high_ref, j):
    first = lax.broadcasted_iota(jnp.int32, low_ref.shape[1:], 1) < CELLS
    even = low_ref[2 * j] + pltpu.roll(high_ref[2 * j], CELLS, 1)
    odd = high_ref[2 * j + 1] + pltpu.roll(low_ref[2 * j + 1], CELLS, 1)
    return jnp.where(first, even, odd)


def gather_planes(capacity, plane, hops, feat_width, id_ref, recv_ref, *refs):
    outs, lows, highs = refs[:hops], refs[hops : 2 * hops], refs[2 * hops :]
    pairs = capacity // 2
    chunk = pairs * feat_width + meta_rows(pairs)
    patch_pairs = lows[0].shape[0] // 2
    for ref in lows + highs:
        ref[...] = jnp.zeros_like(ref)
    for r in range(plane):
        for hop in range(hops):
            n = r * hops + hop
            add_chunk(
                capacity, feat_width, id_ref, n * capacity, recv_ref, n * chunk, lows[hop], highs[hop]
            )
    for hop in range(hops):
        masses = []
        for j in range(patch_pairs):
            pair = paired(lows[hop], highs[hop], j)
            outs[hop][j * feat_width : (j + 1) * feat_width, :] = pair[:feat_width].astype(
                jnp.bfloat16
            )
            masses.append(pair[feat_width : feat_width + 1])
        masses = jnp.concatenate(masses, axis=0)
        high = masses.astype(jnp.bfloat16).astype(jnp.float32)
        spare = outs[hop].shape[0] - patch_pairs * (feat_width + 2)
        rows = [high, masses - high] + ([jnp.zeros((spare, LANES), jnp.float32)] if spare else [])
        outs[hop][patch_pairs * feat_width :, :] = jnp.concatenate(rows, axis=0).astype(jnp.bfloat16)


def gather_own(capacity, plane, feat_width, id_ref, recv_ref, *refs):
    own_ref, low_ref, high_ref = refs[-3:]
    chunk = recv_ref.shape[0] // plane
    low_ref[...] = jnp.zeros_like(low_ref)
    high_ref[...] = jnp.zeros_like(high_ref)
    for r in range(plane):
        add_chunk(
            capacity, feat_width, id_ref, r * capacity, recv_ref, r * chunk, low_ref, high_ref
        )
    for j in range(own_ref.shape[0]):
        own_ref[j] = paired(low_ref, high_ref, j)


def start_tile(hops, own_ref, *refs):
    parts = refs[:hops]
    embed_ref, base_ref, start_ref = refs[hops:]
    feat_width, channels = embed_ref.shape
    tile_rows, tile_cols, _ = base_ref.shape
    patch_rows, patch_cols = tile_rows // PATCH, tile_cols // PATCH
    patch_pairs = patch_rows * patch_cols // 2
    embed = embed_ref[...]
    mass_rows = [part[patch_pairs * feat_width :, :].astype(jnp.float32) for part in parts]
    for pr in range(patch_rows):
        lifted = []
        for pc in range(patch_cols // 2):
            j = pr * (patch_cols // 2) + pc
            pair = own_ref[j]
            sums, mass = pair[:feat_width], pair[feat_width : feat_width + 1]
            for part, rows in zip(parts, mass_rows):
                sums = sums + part[j * feat_width : (j + 1) * feat_width, :].astype(jnp.float32)
                mass = mass + (rows[j : j + 1] + rows[patch_pairs + j : patch_pairs + j + 1])
            encoded = (sums * (1.0 / (1.0 + mass))).astype(jnp.bfloat16)
            lifted.append(lax.dot_general(encoded, embed, TN, preferred_element_type=jnp.float32))
        lifted = jnp.concatenate(lifted, axis=0).reshape(patch_cols, PATCH, PATCH, channels)
        lifted = lifted.transpose(1, 0, 2, 3).reshape(PATCH, tile_cols, channels)
        rows = slice(pr * PATCH, (pr + 1) * PATCH)
        start_ref[rows] = (base_ref[rows].astype(jnp.float32) + lifted).astype(jnp.bfloat16)


def turn_weights(qkv_ref, turned_ref):
    channels = qkv_ref.shape[0]
    turned_ref[:channels] = qkv_ref[:, :channels].T
    turned_ref[channels:] = qkv_ref[:, 2 * channels :].T


def attend(
    cells_ref, windows, sides, norm_gain, qkv_ref, out_ref, turned_ref, key_ref, pack_ref, att_ref,
    score_ref, prob_ref,
):
    channels = qkv_ref.shape[0]
    tokens = WIN * WIN
    group = 128
    heads = group // HEAD_DIM
    count = -(-len(windows) // 2)
    size = count * LANES
    scale = HEAD_DIM ** (-0.5) / math.log(2.0)
    shape = (tokens, heads * LANES)
    own = lax.broadcasted_iota(jnp.int32, shape, 1) % LANES < tokens
    nothing = jnp.zeros(shape, jnp.bfloat16)
    empty = jnp.zeros((HEAD_DIM, LANES), jnp.bfloat16)
    cells = jnp.concatenate(
        [
            cells_ref[row : row + WIN, col : col + WIN, :].reshape(tokens, channels)
            for row, col in windows
        ],
        axis=0,
    )
    normed = normalize(cells, norm_gain).astype(jnp.bfloat16)
    if len(windows) % 2:
        normed = jnp.concatenate([normed, jnp.zeros((tokens, channels), jnp.bfloat16)], axis=0)
    key_ref[:size] = jnp.dot(
        normed, qkv_ref[:, channels : 2 * channels], preferred_element_type=jnp.float32
    ).astype(jnp.bfloat16)
    pack_ref[:, :size] = lax.dot_general(
        turned_ref[...], normed, NT, preferred_element_type=jnp.float32
    ).astype(jnp.bfloat16)
    key_row = lax.broadcasted_iota(jnp.int32, (tokens, LANES), 0) // WIN
    query_row = lax.broadcasted_iota(jnp.int32, (tokens, LANES), 1) % tokens // WIN
    bias = [None] * count
    for p, side in enumerate(sides):
        if side is not None:
            apart = jnp.where(side(key_row) == side(query_row), 0.0, -1e30)
            bias[p] = jnp.concatenate([apart] * heads, axis=1)
    parts = [(p, g) for p in range(count) for g in range(channels // group)]
    for n, (p, g) in enumerate(parts):
        span = slice(p * LANES, (p + 1) * LANES)
        at = slice(g * group, (g + 1) * group)
        query = pack_ref[at, span]
        stack = jnp.concatenate(
            [
                jnp.concatenate(
                    [
                        query[h * HEAD_DIM : (h + 1) * HEAD_DIM] if i == h else empty
                        for i in range(heads)
                    ],
                    axis=0,
                )
                for h in range(heads)
            ],
            axis=1,
        )
        scores = jnp.dot(key_ref[span, at], stack, preferred_element_type=jnp.float32)
        scores = jnp.where(own, scores[:tokens], scores[tokens:])
        score_ref[n] = scores if bias[p] is None else scores + bias[p]
    for n in range(len(parts)):
        scores = score_ref[n]
        peak = jnp.max(scores, axis=0, keepdims=True)
        raised = jnp.exp2((scores - peak) * scale)
        total = jnp.sum(raised, axis=0, keepdims=True)
        probs = (raised * (1.0 / total)).astype(jnp.bfloat16)
        prob_ref[n, :tokens] = jnp.where(own, probs, nothing)
        prob_ref[n, tokens:] = jnp.where(own, nothing, probs)
    for n, (p, g) in enumerate(parts):
        span = slice(p * LANES, (p + 1) * LANES)
        for h in range(0, heads, 2):
            at = g * group + h * HEAD_DIM
            both = jnp.dot(
                pack_ref[channels + at : channels + at + 2 * HEAD_DIM, span],
                prob_ref[n, :, h * LANES : (h + 2) * LANES],
                preferred_element_type=jnp.float32,
            ).astype(jnp.bfloat16)
            att_ref[at : at + HEAD_DIM, span] = both[:HEAD_DIM, :LANES]
            att_ref[at + HEAD_DIM : at + 2 * HEAD_DIM, span] = both[HEAD_DIM:, LANES:]
    mixed = lax.dot_general(
        att_ref[:, :size], out_ref[...], TN, preferred_element_type=jnp.float32
    )
    return [
        mixed[w * tokens : (w + 1) * tokens].reshape(WIN, WIN, channels)
        for w in range(len(windows))
    ]


def finish(begun, mixed, mlp_gain, up_ref, down_ref, decode_ref):
    residual = jnp.concatenate([a.reshape(CELLS, -1) + b.reshape(CELLS, -1) for a, b in zip(begun, mixed)])
    normed = normalize(residual, mlp_gain).astype(jnp.bfloat16)
    latent = residual
    units = up_ref.shape[1]
    step = min(units, 256)
    for at in range(0, units, step):
        span = slice(at, at + step)
        hidden = jax.nn.gelu(jnp.dot(normed, up_ref[:, span], preferred_element_type=jnp.float32))
        latent = latent + jnp.dot(
            hidden.astype(jnp.bfloat16), down_ref[span, :], preferred_element_type=jnp.float32
        )
    rounded = latent.astype(jnp.bfloat16)
    turned = [
        lax.dot_general(
            decode_ref[...],
            rounded[i * CELLS : i * CELLS + LANES],
            NT,
            preferred_element_type=jnp.float32,
        ).astype(jnp.bfloat16)
        for i in range(0, len(begun), 2)
    ]
    return latent, turned


def patch_order(patch_rows, patch_cols):
    every = [(r, c) for r in range(patch_rows) for c in range(patch_cols)]
    middle = [(r, c) for r, c in every if 0 < c < patch_cols - 1]
    first = [(r, c) for r, c in middle if 0 < r < patch_rows - 1]
    ends = [at for at in middle if at not in first]
    return first, ends, [at for at in every if at not in middle]


def edge_side(top, row, lat_cells):
    return lambda r: (top + row + r >= 0).astype(jnp.int32) + (
        top + row + r >= lat_cells
    ).astype(jnp.int32)


def inner_block(
    start_ref, norm_ref, qkv_ref, out_ref, mlp_ref, up_ref, down_ref, decode_ref, latent_ref,
    proj_ref, mixed_ref, cells_ref, turned_ref, key_ref, pack_ref, att_ref, score_ref, prob_ref,
):
    tile_rows, tile_cols, channels = cells_ref.shape
    margin = WIN // 2
    feat_width = decode_ref.shape[0]
    cells_ref[...] = start_ref[...].astype(jnp.float32)
    turn_weights(qkv_ref, turned_ref)
    for row in range(0, tile_rows - WIN, WIN):
        cols = range(0, tile_cols - WIN, WIN)
        mixed = attend(
            cells_ref, [(row + margin, col + margin) for col in cols], [], norm_ref[...],
            qkv_ref, out_ref, turned_ref, key_ref, pack_ref, att_ref, score_ref, prob_ref,
        )
        for col, block in zip(cols, mixed):
            mixed_ref[row : row + WIN, col : col + WIN, :] = block
    first, _, _ = patch_order(tile_rows // PATCH, tile_cols // PATCH)
    done = 0
    for pr in sorted(set(r for r, _ in first)):
        here = [c for r, c in first if r == pr]
        row = pr * PATCH
        latent, turned = finish(
            [cells_ref[row : row + PATCH, c * PATCH : (c + 1) * PATCH, :] for c in here],
            [
                mixed_ref[
                    row - margin : row - margin + PATCH,
                    c * PATCH - margin : c * PATCH - margin + PATCH,
                    :,
                ]
                for c in here
            ],
            mlp_ref[...], up_ref, down_ref, decode_ref,
        )
        placed = latent.reshape(len(here), PATCH, PATCH, channels).transpose(1, 0, 2, 3)
        latent_ref[row - PATCH : row] = placed.reshape(PATCH, len(here) * PATCH, channels).astype(
            jnp.bfloat16
        )
        for pair in turned:
            proj_ref[done : done + feat_width, :] = pair
            done += feat_width


def tall_block(
    lat_cells, tall_ref, inner_mixed_ref, norm_ref, qkv_ref, out_ref, mlp_ref, up_ref, down_ref,
    decode_ref, latent_ref, proj_ref, mixed_ref, cells_ref, turned_ref, key_ref, pack_ref,
    att_ref, score_ref, prob_ref,
):
    rows, tile_cols, channels = tall_ref.shape
    margin = WIN // 2
    tile_rows = rows - 2 * margin
    feat_width = decode_ref.shape[0]
    last = rows - WIN
    top = lax.axis_index("lat") * tile_rows - margin
    turn_weights(qkv_ref, turned_ref)
    for part in (slice(0, 2 * WIN), slice(rows - 2 * WIN, rows)):
        cells_ref[part] = tall_ref[part].astype(jnp.float32)
    cols = range(0, tile_cols - WIN, WIN)
    for i, row in enumerate((0, last)):
        mixed = attend(
            cells_ref, [(row, col + margin) for col in cols],
            [edge_side(top, row, lat_cells)] * -(-len(cols) // 2), norm_ref[...], qkv_ref,
            out_ref, turned_ref, key_ref, pack_ref, att_ref, score_ref, prob_ref,
        )
        for col, block in zip(cols, mixed):
            mixed_ref[i * WIN : (i + 1) * WIN, col : col + WIN, :] = block
    here = range(1, tile_cols // PATCH - 1)
    done = 0
    for i, row in enumerate((margin, last - margin)):
        begun, mixed = [], []
        for c in here:
            span = slice(c * PATCH - margin, (c + 1) * PATCH - margin)
            begun.append(cells_ref[row : row + PATCH, c * PATCH : (c + 1) * PATCH, :])
            if i == 0:
                halves = [mixed_ref[margin:WIN, span, :], inner_mixed_ref[:margin, span, :]]
            else:
                halves = [
                    inner_mixed_ref[tile_rows - WIN - margin :, span, :],
                    mixed_ref[WIN : WIN + margin, span, :],
                ]
            mixed.append(jnp.concatenate(halves, axis=0))
        latent, turned = finish(begun, mixed, mlp_ref[...], up_ref, down_ref, decode_ref)
        placed = latent.reshape(len(here), PATCH, PATCH, channels).transpose(1, 0, 2, 3)
        latent_ref[i * PATCH : (i + 1) * PATCH] = placed.reshape(
            PATCH, len(here) * PATCH, channels
        ).astype(jnp.bfloat16)
        for pair in turned:
            proj_ref[done : done + feat_width, :] = pair
            done += feat_width


def outer_block(
    lat_cells, ext_ref, inner_latent_ref, inner_proj_ref, inner_mixed_ref, tall_latent_ref,
    tall_proj_ref, tall_mixed_ref, norm_ref, qkv_ref, out_ref, mlp_ref, up_ref, down_ref,
    decode_ref, latent_ref, proj_ref, mixed_ref, turned_ref, key_ref, pack_ref, att_ref,
    score_ref, prob_ref,
):
    ext_rows, ext_cols, channels = ext_ref.shape
    tile_rows, tile_cols, _ = latent_ref.shape
    margin = WIN // 2
    feat_width = decode_ref.shape[0]
    last_row, last_col = ext_rows - WIN, ext_cols - WIN
    top = lax.axis_index("lat") * tile_rows - margin
    turn_weights(qkv_ref, turned_ref)
    mixed_ref[WIN:last_row, WIN:last_col, :] = inner_mixed_ref[...]
    mixed_ref[:WIN, WIN:last_col, :] = tall_mixed_ref[:WIN]
    mixed_ref[last_row:, WIN:last_col, :] = tall_mixed_ref[WIN:]
    windows = [(row, col) for row in range(0, ext_rows, WIN) for col in (0, last_col)]
    sides = [
        edge_side(top, row, lat_cells) if row in (0, last_row) else None
        for row in range(0, ext_rows, WIN)
    ]
    mixed = attend(
        ext_ref, windows, sides, norm_ref[...], qkv_ref, out_ref, turned_ref, key_ref, pack_ref,
        att_ref, score_ref, prob_ref,
    )
    for (row, col), block in zip(windows, mixed):
        mixed_ref[row : row + WIN, col : col + WIN, :] = block
    done = inner_proj_ref.shape[0]
    proj_ref[:done, :] = inner_proj_ref[...]
    proj_ref[done : done + tall_proj_ref.shape[0], :] = tall_proj_ref[...]
    done += tall_proj_ref.shape[0]
    patch_rows = tile_rows // PATCH
    _, _, here = patch_order(patch_rows, tile_cols // PATCH)
    at = [
        (
            slice(r * PATCH + margin, (r + 1) * PATCH + margin),
            slice(c * PATCH + margin, (c + 1) * PATCH + margin),
        )
        for r, c in here
    ]
    latent, turned = finish(
        [ext_ref[r, c, :] for r, c in at],
        [mixed_ref[r, c, :] for r, c in at],
        mlp_ref[...], up_ref, down_ref, decode_ref,
    )
    for pair in turned:
        proj_ref[done : done + feat_width, :] = pair
        done += feat_width
    latent = latent.reshape(len(here), PATCH, PATCH, channels)
    for pr in range(patch_rows):
        left, right = [latent[i] for i, (r, _) in enumerate(here) if r == pr]
        if 0 < pr < patch_rows - 1:
            middle = inner_latent_ref[(pr - 1) * PATCH : pr * PATCH]
        else:
            middle = tall_latent_ref[:PATCH] if pr == 0 else tall_latent_ref[PATCH:]
        whole = jnp.concatenate([left, middle.astype(jnp.float32), right], axis=1)
        latent_ref[pr * PATCH : (pr + 1) * PATCH] = whole.astype(jnp.bfloat16)


def reply_patches(capacity, plane, tiles, order, feat_width, id_ref, *refs):
    tile_refs, out_ref, both_ref = refs[:tiles], refs[tiles], refs[tiles + 1]
    pairs = capacity // 2
    first = lax.broadcasted_iota(jnp.int32, (feat_width, LANES), 1) < CELLS
    for t in range(tiles):
        for i in range(0, len(order), 2):
            at = i // 2 * feat_width
            pair = tile_refs[t][at : at + feat_width, :].astype(jnp.float32)
            swapped = pltpu.roll(pair, CELLS, 1)
            both_ref[t, order[i]] = jnp.where(first, pair, swapped)
            both_ref[t, order[i + 1]] = jnp.where(first, swapped, pair)
    for r in range(plane):
        for t in range(tiles):
            for k in range(pairs):
                slot = (r * tiles + t) * capacity + 2 * k
                pair = jnp.where(
                    first, both_ref[t, id_ref[slot]], both_ref[t, id_ref[slot + 1]]
                )
                at = ((r * tiles + t) * pairs + k) * feat_width
                out_ref[at : at + feat_width, :] = pair.astype(jnp.bfloat16)


def decode_blocks(slot_ref, offset_ref, near_ref, far_ref, out_hbm, back_ref, out_ref, sems):
    feat_width, count = out_ref.shape
    blocks = count // BLK
    step = sems.shape[0]
    size = blocks // step
    back_ref[: near_ref.shape[0], :] = near_ref[...]
    back_ref[near_ref.shape[0] :, :] = far_ref[...]

    def one(b):
        slot = slot_ref[b]
        span = slice(b * BLK, (b + 1) * BLK)
        weights = block_weights(offset_ref[:, span].astype(jnp.float32))
        total = jnp.sum(weights.astype(jnp.float32), axis=0, keepdims=True)
        nothing = jnp.zeros_like(weights)
        low = lax.rem(slot, 2) == 0
        both = jnp.concatenate(
            [jnp.where(low, weights, nothing), jnp.where(low, nothing, weights)], axis=0
        )
        row = pl.multiple_of(lax.div(slot, 2) * feat_width, 16)
        values = back_ref[pl.ds(row, feat_width), :]
        mean = jnp.dot(values, both, preferred_element_type=jnp.float32) * (1.0 / total)
        out_ref[:, span] = mean.astype(jnp.bfloat16)

    copies = []
    for i in range(step):
        for b in range(i * size, (i + 1) * size):
            one(b)
        span = pl.ds(i * size * BLK, size * BLK)
        copies.append(pltpu.make_async_copy(out_ref.at[:, span], out_hbm.at[:, span], sems.at[i]))
        copies[i].start()
    for copy in copies:
        copy.wait()


def with_halo(array, axis, dim, width):
    size, length = (axis_count(axis), array.shape[dim])
    up = [(i, (i + 1) % size) for i in range(size)]
    down = [(j, i) for i, j in up]
    last = lax.slice_in_dim(array, length - width, length, axis=dim)
    initial = lax.slice_in_dim(array, 0, width, axis=dim)
    before = lax.ppermute(last, axis, up)
    after = lax.ppermute(initial, axis, down)
    return jnp.concatenate([before, array, after], axis=dim)


def axis_count(axes):
    axes = axes if isinstance(axes, tuple) else (axes,)
    return math.prod([lax.axis_size(axis) for axis in axes])


def swap_in_plane(array):
    plane = axis_count(("lat", "x"))
    parts = array.reshape(plane, -1, LANES)
    parts = lax.all_to_all(parts, ("lat", "x"), split_axis=0, concat_axis=0, tiled=True)
    return parts.reshape(array.shape)


def swap_at_once(gains, array):
    def apart(array):
        lat, width = lax.axis_size("lat"), lax.axis_size("x")
        parts = array.reshape(lat, width, -1, LANES)
        for dim, axis in enumerate(("lat", "x")):
            parts = lax.all_to_all(parts, axis, split_axis=dim, concat_axis=dim, tiled=True)
        return parts.reshape(array.shape)

    return lax.cond(gains[0] > 0.0, swap_in_plane, apart, array)


def swap_planes(array, hop):
    depth = lax.axis_size("z")
    return lax.ppermute(array, "z", [(i, i ^ hop) for i in range(depth)])


def local(
    obs_feat,
    obs_offset,
    block_tile,
    block_patch,
    embed_weight,
    grid_base,
    norm_gain,
    qkv_weight,
    out_weight,
    mlp_gain,
    up_weight,
    down_weight,
    decode_weight,
):
    lat, depth, width = (lax.axis_size(axis) for axis in ("lat", "z", "x"))
    plane, hops = lat * width, depth - 1
    devices = plane * depth
    feat_width, obs_count = obs_feat.shape
    blocks = obs_count // BLK
    capacity = max(2, 2 * blocks // devices)
    capacity += capacity % 2
    pairs = capacity // 2
    tile_rows, tile_cols, channels = grid_base.shape
    patch_total = (tile_rows // PATCH) * (tile_cols // PATCH)
    chunk = pairs * feat_width + meta_rows(pairs)
    dense = dense_rows(patch_total // 2, feat_width)
    steps = 3 if blocks % 3 == 0 else 1
    send_near, send_far, slots = pl.pallas_call(
        lambda *refs: encode_blocks(capacity, (lat, depth, width), *refs),
        out_shape=(
            jax.ShapeDtypeStruct((plane * chunk, LANES), jnp.bfloat16),
            jax.ShapeDtypeStruct((plane * hops * chunk, LANES), jnp.bfloat16),
            jax.ShapeDtypeStruct((blocks,), jnp.int32),
        ),
        in_specs=[pl.BlockSpec(memory_space=pltpu.HBM)] * 4,
        out_specs=(vmem(), vmem(), smem()),
        scratch_shapes=[
            pltpu.VMEM((devices * chunk, LANES), jnp.bfloat16),
            pltpu.SMEM((blocks,), jnp.int32),
            pltpu.SMEM((blocks,), jnp.int32),
            pltpu.VMEM(obs_feat.shape, jnp.bfloat16),
            pltpu.VMEM(obs_offset.shape, jnp.bfloat16),
            pltpu.SMEM((devices,), jnp.int32),
            pltpu.SemaphoreType.DMA((steps + 3,)),
        ],
        compiler_params=params(61),
        name="encode_blocks",
    )(block_tile.reshape(blocks), block_patch, obs_feat, obs_offset)

    def ids_of(recv, tiles):
        at = pairs * feat_width + 2 * pairs
        tags = recv.reshape(plane * tiles, chunk, LANES)[:, at : at + pairs, 0::CELLS]
        ids = tags.astype(jnp.float32).astype(jnp.int32) - 1
        return jnp.clip(ids, 0, patch_total - 1).reshape(-1)

    far = swap_in_plane(send_far)
    far_ids = ids_of(far, hops)
    sums = pl.pallas_call(
        lambda *refs: gather_planes(capacity, plane, hops, feat_width, *refs),
        out_shape=[jax.ShapeDtypeStruct((dense, LANES), jnp.bfloat16)] * hops,
        in_specs=[smem(), vmem()],
        out_specs=[vmem()] * hops,
        scratch_shapes=[pltpu.VMEM((patch_total, feat_width + 8, LANES), jnp.float32)] * (2 * hops),
        compiler_params=params(14),
        name="gather_planes",
    )(far_ids, far)
    parts = [swap_planes(sums[hop - 1], hop) for hop in range(1, depth)]
    send_near, _ = lax.optimization_barrier((send_near, sums))
    near = swap_at_once(norm_gain, send_near)
    near_ids = ids_of(near, 1)
    own = pl.pallas_call(
        lambda *refs: gather_own(capacity, plane, feat_width, *refs),
        out_shape=jax.ShapeDtypeStruct((patch_total // 2, feat_width + 8, LANES), jnp.float32),
        in_specs=[smem()] + [vmem()] * 3,
        out_specs=vmem(),
        scratch_shapes=[pltpu.VMEM((patch_total, feat_width + 8, LANES), jnp.float32)] * 2,
        compiler_params=params(10),
        cost_estimate=pl.CostEstimate(flops=10**9, bytes_accessed=10**7, transcendentals=0),
        name="gather_own",
    )(near_ids, near, qkv_weight, out_weight)

    start = pl.pallas_call(
        lambda *refs: start_tile(hops, *refs),
        out_shape=jax.ShapeDtypeStruct(grid_base.shape, jnp.bfloat16),
        in_specs=[vmem()] * (hops + 3),
        out_specs=vmem(),
        compiler_params=params(10),
        name="start_tile",
    )(own, *parts, embed_weight, grid_base)

    margin = WIN // 2
    ext_rows, ext_cols = tile_rows + 2 * margin, tile_cols + 2 * margin
    tall = with_halo(start, "lat", 0, margin)
    group = 128
    gains = (norm_gain.reshape(1, channels), mlp_gain.reshape(1, channels))
    weights = (gains[0], qkv_weight, out_weight, gains[1], up_weight, down_weight, decode_weight.T)
    patch_rows, patch_cols = tile_rows // PATCH, tile_cols // PATCH
    inner, ends, sides = patch_order(patch_rows, patch_cols)
    order = [r * patch_cols + c for r, c in inner + ends + sides]
    inner_cells = (tile_rows - 2 * PATCH, tile_cols - 2 * PATCH, channels)
    inner_mixed = (tile_rows - WIN, tile_cols - WIN, channels)

    def scratch(windows):
        count = -(-windows // 2)
        parts = count * channels // group
        lanes = group // HEAD_DIM * LANES
        return [
            pltpu.VMEM((2 * channels, channels), jnp.bfloat16),
            pltpu.VMEM((count * LANES, channels), jnp.bfloat16),
            pltpu.VMEM((2 * channels, count * LANES), jnp.bfloat16),
            pltpu.VMEM((channels, count * LANES), jnp.bfloat16),
            pltpu.VMEM((parts, WIN * WIN, lanes), jnp.float32),
            pltpu.VMEM((parts, LANES, lanes), jnp.bfloat16),
        ]

    latent_inner, proj_inner, mixed_inner = pl.pallas_call(
        inner_block,
        out_shape=(
            jax.ShapeDtypeStruct(inner_cells, jnp.bfloat16),
            jax.ShapeDtypeStruct((len(inner) // 2 * feat_width, LANES), jnp.bfloat16),
            jax.ShapeDtypeStruct(inner_mixed, jnp.float32),
        ),
        in_specs=[vmem()] * 8,
        out_specs=(vmem(), vmem(), vmem()),
        scratch_shapes=[pltpu.VMEM(grid_base.shape, jnp.float32)]
        + scratch(tile_cols // WIN - 1),
        compiler_params=params(16),
        cost_estimate=pl.CostEstimate(flops=6 * 10**9, bytes_accessed=10**7, transcendentals=0),
        name="inner_block",
    )(start, *weights)

    tall, proj_inner = lax.optimization_barrier((tall, proj_inner))
    ext = with_halo(tall, ("z", "x"), 1, margin).astype(jnp.float32)

    latent_tall, proj_tall, mixed_tall = pl.pallas_call(
        lambda *refs: tall_block(tile_rows * lat, *refs),
        out_shape=(
            jax.ShapeDtypeStruct((2 * PATCH,) + inner_cells[1:], jnp.bfloat16),
            jax.ShapeDtypeStruct((len(ends) // 2 * feat_width, LANES), jnp.bfloat16),
            jax.ShapeDtypeStruct((2 * WIN,) + inner_mixed[1:], jnp.float32),
        ),
        in_specs=[vmem()] * 9,
        out_specs=(vmem(), vmem(), vmem()),
        scratch_shapes=[pltpu.VMEM(tall.shape, jnp.float32)] + scratch(tile_cols // WIN - 1),
        compiler_params=params(16),
        cost_estimate=pl.CostEstimate(flops=5 * 10**9, bytes_accessed=10**7, transcendentals=0),
        name="tall_block",
    )(tall, mixed_inner, *weights)

    latent, projected = pl.pallas_call(
        lambda *refs: outer_block(tile_rows * lat, *refs),
        out_shape=(
            jax.ShapeDtypeStruct(grid_base.shape, jnp.bfloat16),
            jax.ShapeDtypeStruct((patch_total // 2 * feat_width, LANES), jnp.bfloat16),
        ),
        in_specs=[vmem()] * 14,
        out_specs=(vmem(), vmem()),
        scratch_shapes=[pltpu.VMEM((ext_rows, ext_cols, channels), jnp.float32)]
        + scratch(2 * (ext_rows // WIN)),
        compiler_params=params(20),
        cost_estimate=pl.CostEstimate(flops=5 * 10**9, bytes_accessed=10**7, transcendentals=0),
        name="outer_block",
    )(
        ext, latent_inner, proj_inner, mixed_inner, latent_tall, proj_tall, mixed_tall, *weights
    )

    def reply(ids, tiles, name):
        count = len(tiles)
        return pl.pallas_call(
            lambda *refs: reply_patches(capacity, plane, count, order, feat_width, *refs),
            out_shape=jax.ShapeDtypeStruct(
                (plane * count * pairs * feat_width, LANES), jnp.bfloat16
            ),
            in_specs=[smem()] + [vmem()] * count,
            out_specs=vmem(),
            scratch_shapes=[pltpu.VMEM((count, patch_total, feat_width, LANES), jnp.float32)],
            compiler_params=params(12),
            cost_estimate=pl.CostEstimate(flops=10**9, bytes_accessed=10**7, transcendentals=0),
            name=name,
        )(ids, *tiles)

    others = [swap_planes(projected, hop) for hop in range(1, depth)]
    near_reply = reply(near_ids, [projected], "reply_near")
    near_back = swap_at_once(norm_gain, near_reply)
    far_back = swap_in_plane(reply(far_ids, others, "reply_far"))

    obs_out = pl.pallas_call(
        decode_blocks,
        out_shape=jax.ShapeDtypeStruct((feat_width, obs_count), jnp.bfloat16),
        in_specs=[smem(), vmem()] + [vmem()] * 2,
        out_specs=pl.BlockSpec(memory_space=pltpu.HBM),
        scratch_shapes=[
            pltpu.VMEM((devices * pairs * feat_width, LANES), jnp.bfloat16),
            pltpu.VMEM((feat_width, obs_count), jnp.bfloat16),
            pltpu.SemaphoreType.DMA((steps,)),
        ],
        compiler_params=params(12),
        name="decode_blocks",
    )(slots, obs_offset, near_back, far_back)
    return (latent, obs_out)


def solution(mesh):
    lat, lon = mesh.devices.shape
    width = lat // 2 if lat % 2 == 0 and lon % (lat // 2) == 0 else 1
    split = Mesh(mesh.devices.reshape(lat, lon // width, width), ("lat", "z", "x"))
    every = ("lat", "z", "x")
    placed = (
        P(None, every),
        P(None, every),
        P(every, None),
        P(every),
        P(),
        P("lat", ("z", "x"), None),
        P(),
        P(),
        P(),
        P(),
        P(),
        P(),
        P(),
    )
    return jax.shard_map(
        local,
        mesh=split,
        in_specs=placed,
        out_specs=(P("lat", ("z", "x"), None), P(None, every)),
        check_vma=False,
    )
```

```python
import math

import jax
import jax.numpy as jnp
from jax import lax
from jax.experimental import pallas as pl
from jax.experimental.pallas import tpu as pltpu
from jax.sharding import Mesh
from jax.sharding import PartitionSpec as P

HEAD_DIM = 32
WIN = 8
PATCH = 8
BLK = 128
CELLS = PATCH * PATCH
LANES = 2 * CELLS

epsilon = 1e-05
spread_coef = 0.5

NT = (((1,), (1,)), ((), ()))
TN = (((0,), (0,)), ((), ()))


def params(mib):
    return pltpu.CompilerParams(vmem_limit_bytes=mib * 1024 * 1024)


def vmem():
    return pl.BlockSpec(memory_space=pltpu.VMEM)


def smem():
    return pl.BlockSpec(memory_space=pltpu.SMEM)


def normalize(values, gain_row):
    center = jnp.mean(values, axis=-1, keepdims=True)
    centered = values - center
    variance = jnp.mean(centered * centered, axis=-1, keepdims=True)
    return centered * lax.rsqrt(variance + epsilon) * gain_row


def block_weights(offsets):
    axis_id = lax.broadcasted_iota(jnp.int32, (PATCH, BLK), 0).astype(jnp.float32) + 0.5
    row_gap = axis_id - offsets[0:1]
    col_gap = axis_id - offsets[1:2]
    row_gap = row_gap * row_gap
    col_gap = col_gap * col_gap
    total = row_gap[:, None, :] + col_gap[None, :, :]
    return jnp.exp(-spread_coef * total).reshape(CELLS, BLK).astype(jnp.bfloat16)


def meta_rows(pairs):
    return -(-3 * pairs // 16) * 16


def encode_blocks(
    capacity, shape, tile_hbm, patch_hbm, feat_hbm, offset_hbm, near_ref, far_ref,
    slot_ref, send_ref, tile_ref, patch_ref, feat_ref, offset_ref, count_ref, sems,
):
    lat, depth, width = shape
    devices = lat * depth * width
    plane_id = lax.axis_index("z")
    feat_width = feat_ref.shape[0]
    blocks = feat_ref.shape[1] // BLK
    step = sems.shape[0] - 3
    size = blocks // step
    pairs = capacity // 2
    meta = meta_rows(pairs)
    chunk = pairs * feat_width + meta
    small = [
        pltpu.make_async_copy(tile_hbm, tile_ref, sems.at[step]),
        pltpu.make_async_copy(patch_hbm, patch_ref, sems.at[step + 1]),
        pltpu.make_async_copy(offset_hbm, offset_ref, sems.at[step + 2]),
    ]
    large = []
    for i in range(step):
        span = pl.ds(i * size * BLK, size * BLK)
        large.append(pltpu.make_async_copy(feat_hbm.at[:, span], feat_ref.at[:, span], sems.at[i]))
    for copy in small + large:
        copy.start()
    send_ref[...] = jnp.zeros_like(send_ref)

    def clear(t, _):
        count_ref[t] = 0
        return 0

    lax.fori_loop(0, devices, clear, 0)
    lane_half = lax.broadcasted_iota(jnp.int32, (feat_width, LANES), 1) // CELLS
    meta_half = lax.broadcasted_iota(jnp.int32, (meta, LANES), 1) // CELLS
    meta_row = lax.broadcasted_iota(jnp.int32, (meta, LANES), 0)
    ones = jnp.ones((16, BLK), jnp.bfloat16)

    def one(b):
        tile = tile_ref[b]
        rank = count_ref[tile]
        count_ref[tile] = rank + 1
        lon = lax.rem(tile, depth * width)
        partner = lax.div(tile, depth * width) * width + lax.rem(lon, width)
        hop = lax.div(lon, width) ^ plane_id
        piece = jnp.where(hop == 0, partner, lat * width + partner * (depth - 1) + hop - 1)
        slot_ref[b] = piece * capacity + rank
        pair = lax.div(rank, 2)
        half = lax.rem(rank, 2)
        col = pl.multiple_of(b * BLK, BLK)
        feat = jnp.concatenate([feat_ref[:, pl.ds(col, BLK)], ones], axis=0)
        weights = block_weights(offset_ref[:, pl.ds(col, BLK)].astype(jnp.float32))
        twice = jnp.concatenate([weights, weights], axis=0)
        sums = lax.dot_general(feat, twice, NT, preferred_element_type=jnp.float32)
        row = pl.multiple_of(piece * chunk + pair * feat_width, 16)
        old = send_ref[pl.ds(row, feat_width), :].astype(jnp.float32)
        send_ref[pl.ds(row, feat_width), :] = jnp.where(
            lane_half == half, sums[:feat_width], old
        ).astype(jnp.bfloat16)
        mass = sums[feat_width : feat_width + 1]
        high = mass.astype(jnp.bfloat16).astype(jnp.float32)
        low = mass - high
        tag = (patch_ref[b] + 1).astype(jnp.float32)
        row = pl.multiple_of(piece * chunk + pairs * feat_width, 16)
        old = send_ref[pl.ds(row, meta), :].astype(jnp.float32)
        new = jnp.where(
            meta_row == pair,
            high,
            jnp.where(
                meta_row == pairs + pair, low, jnp.where(meta_row == 2 * pairs + pair, tag, old)
            ),
        )
        send_ref[pl.ds(row, meta), :] = jnp.where(meta_half == half, new, old).astype(jnp.bfloat16)

    for copy in small:
        copy.wait()
    for i in range(step):
        large[i].wait()
        for b in range(i * size, (i + 1) * size):
            one(b)
    near_ref[...] = send_ref[: near_ref.shape[0]]
    far_ref[...] = send_ref[near_ref.shape[0] :]


def dense_rows(pairs, feat_width):
    return pairs * feat_width + -(-2 * pairs // 16) * 16


def add_chunk(capacity, feat_width, id_ref, slot, recv_ref, base, low_ref, high_ref):
    pairs = capacity // 2
    tags = recv_ref[base + pairs * feat_width : base + pairs * feat_width + meta_rows(pairs), :]
    tags = tags.astype(jnp.float32)
    for k in range(pairs):
        at = base + k * feat_width
        sums = recv_ref[at : at + feat_width, :].astype(jnp.float32)
        mass = tags[k : k + 1] + tags[pairs + k : pairs + k + 1]
        both = jnp.concatenate([sums, jnp.broadcast_to(mass, (8, LANES))], axis=0)
        low_ref[id_ref[slot + 2 * k]] += both
        high_ref[id_ref[slot + 2 * k + 1]] += both


def paired(low_ref, high_ref, j):
    first = lax.broadcasted_iota(jnp.int32, low_ref.shape[1:], 1) < CELLS
    even = low_ref[2 * j] + pltpu.roll(high_ref[2 * j], CELLS, 1)
    odd = high_ref[2 * j + 1] + pltpu.roll(low_ref[2 * j + 1], CELLS, 1)
    return jnp.where(first, even, odd)


def gather_planes(capacity, plane, hops, feat_width, id_ref, recv_ref, *refs):
    outs, lows, highs = refs[:hops], refs[hops : 2 * hops], refs[2 * hops :]
    pairs = capacity // 2
    chunk = pairs * feat_width + meta_rows(pairs)
    patch_pairs = lows[0].shape[0] // 2
    for ref in lows + highs:
        ref[...] = jnp.zeros_like(ref)
    for r in range(plane):
        for hop in range(hops):
            n = r * hops + hop
            add_chunk(
                capacity, feat_width, id_ref, n * capacity, recv_ref, n * chunk, lows[hop], highs[hop]
            )
    for hop in range(hops):
        masses = []
        for j in range(patch_pairs):
            pair = paired(lows[hop], highs[hop], j)
            outs[hop][j * feat_width : (j + 1) * feat_width, :] = pair[:feat_width].astype(
                jnp.bfloat16
            )
            masses.append(pair[feat_width : feat_width + 1])
        masses = jnp.concatenate(masses, axis=0)
        high = masses.astype(jnp.bfloat16).astype(jnp.float32)
        spare = outs[hop].shape[0] - patch_pairs * (feat_width + 2)
        rows = [high, masses - high] + ([jnp.zeros((spare, LANES), jnp.float32)] if spare else [])
        outs[hop][patch_pairs * feat_width :, :] = jnp.concatenate(rows, axis=0).astype(jnp.bfloat16)


def gather_own(capacity, plane, feat_width, id_ref, recv_ref, *refs):
    own_ref, low_ref, high_ref = refs[-3:]
    chunk = recv_ref.shape[0] // plane
    low_ref[...] = jnp.zeros_like(low_ref)
    high_ref[...] = jnp.zeros_like(high_ref)
    for r in range(plane):
        add_chunk(
            capacity, feat_width, id_ref, r * capacity, recv_ref, r * chunk, low_ref, high_ref
        )
    for j in range(own_ref.shape[0]):
        own_ref[j] = paired(low_ref, high_ref, j)


def start_tile(hops, own_ref, *refs):
    parts = refs[:hops]
    embed_ref, base_ref, start_ref = refs[hops:]
    feat_width, channels = embed_ref.shape
    tile_rows, tile_cols, _ = base_ref.shape
    patch_rows, patch_cols = tile_rows // PATCH, tile_cols // PATCH
    patch_pairs = patch_rows * patch_cols // 2
    embed = embed_ref[...]
    mass_rows = [part[patch_pairs * feat_width :, :].astype(jnp.float32) for part in parts]
    for pr in range(patch_rows):
        lifted = []
        for pc in range(patch_cols // 2):
            j = pr * (patch_cols // 2) + pc
            pair = own_ref[j]
            sums, mass = pair[:feat_width], pair[feat_width : feat_width + 1]
            for part, rows in zip(parts, mass_rows):
                sums = sums + part[j * feat_width : (j + 1) * feat_width, :].astype(jnp.float32)
                mass = mass + (rows[j : j + 1] + rows[patch_pairs + j : patch_pairs + j + 1])
            encoded = (sums * (1.0 / (1.0 + mass))).astype(jnp.bfloat16)
            lifted.append(lax.dot_general(encoded, embed, TN, preferred_element_type=jnp.float32))
        lifted = jnp.concatenate(lifted, axis=0).reshape(patch_cols, PATCH, PATCH, channels)
        lifted = lifted.transpose(1, 0, 2, 3).reshape(PATCH, tile_cols, channels)
        rows = slice(pr * PATCH, (pr + 1) * PATCH)
        start_ref[rows] = (base_ref[rows].astype(jnp.float32) + lifted).astype(jnp.bfloat16)


def turn_weights(qkv_ref, turned_ref):
    channels = qkv_ref.shape[0]
    turned_ref[:channels] = qkv_ref[:, :channels].T
    turned_ref[channels:] = qkv_ref[:, 2 * channels :].T


def attend(
    cells_ref, windows, sides, norm_gain, qkv_ref, out_ref, turned_ref, key_ref, pack_ref, att_ref,
    score_ref, prob_ref,
):
    channels = qkv_ref.shape[0]
    tokens = WIN * WIN
    group = 128
    heads = group // HEAD_DIM
    count = -(-len(windows) // 2)
    size = count * LANES
    scale = HEAD_DIM ** (-0.5) / math.log(2.0)
    shape = (tokens, heads * LANES)
    own = lax.broadcasted_iota(jnp.int32, shape, 1) % LANES < tokens
    nothing = jnp.zeros(shape, jnp.bfloat16)
    empty = jnp.zeros((HEAD_DIM, LANES), jnp.bfloat16)
    cells = jnp.concatenate(
        [
            cells_ref[row : row + WIN, col : col + WIN, :].reshape(tokens, channels)
            for row, col in windows
        ],
        axis=0,
    )
    normed = normalize(cells, norm_gain).astype(jnp.bfloat16)
    if len(windows) % 2:
        normed = jnp.concatenate([normed, jnp.zeros((tokens, channels), jnp.bfloat16)], axis=0)
    key_ref[:size] = jnp.dot(
        normed, qkv_ref[:, channels : 2 * channels], preferred_element_type=jnp.float32
    ).astype(jnp.bfloat16)
    pack_ref[:, :size] = lax.dot_general(
        turned_ref[...], normed, NT, preferred_element_type=jnp.float32
    ).astype(jnp.bfloat16)
    key_row = lax.broadcasted_iota(jnp.int32, (tokens, LANES), 0) // WIN
    query_row = lax.broadcasted_iota(jnp.int32, (tokens, LANES), 1) % tokens // WIN
    bias = [None] * count
    for p, side in enumerate(sides):
        if side is not None:
            apart = jnp.where(side(key_row) == side(query_row), 0.0, -1e30)
            bias[p] = jnp.concatenate([apart] * heads, axis=1)
    parts = [(p, g) for p in range(count) for g in range(channels // group)]
    for n, (p, g) in enumerate(parts):
        span = slice(p * LANES, (p + 1) * LANES)
        at = slice(g * group, (g + 1) * group)
        query = pack_ref[at, span]
        stack = jnp.concatenate(
            [
                jnp.concatenate(
                    [
                        query[h * HEAD_DIM : (h + 1) * HEAD_DIM] if i == h else empty
                        for i in range(heads)
                    ],
                    axis=0,
                )
                for h in range(heads)
            ],
            axis=1,
        )
        scores = jnp.dot(key_ref[span, at], stack, preferred_element_type=jnp.float32)
        scores = jnp.where(own, scores[:tokens], scores[tokens:])
        score_ref[n] = scores if bias[p] is None else scores + bias[p]
    for n in range(len(parts)):
        scores = score_ref[n]
        peak = jnp.max(scores, axis=0, keepdims=True)
        raised = jnp.exp2((scores - peak) * scale)
        total = jnp.sum(raised, axis=0, keepdims=True)
        probs = (raised * (1.0 / total)).astype(jnp.bfloat16)
        prob_ref[n, :tokens] = jnp.where(own, probs, nothing)
        prob_ref[n, tokens:] = jnp.where(own, nothing, probs)
    for n, (p, g) in enumerate(parts):
        span = slice(p * LANES, (p + 1) * LANES)
        for h in range(0, heads, 2):
            at = g * group + h * HEAD_DIM
            both = jnp.dot(
                pack_ref[channels + at : channels + at + 2 * HEAD_DIM, span],
                prob_ref[n, :, h * LANES : (h + 2) * LANES],
                preferred_element_type=jnp.float32,
            ).astype(jnp.bfloat16)
            att_ref[at : at + HEAD_DIM, span] = both[:HEAD_DIM, :LANES]
            att_ref[at + HEAD_DIM : at + 2 * HEAD_DIM, span] = both[HEAD_DIM:, LANES:]
    mixed = lax.dot_general(
        att_ref[:, :size], out_ref[...], TN, preferred_element_type=jnp.float32
    )
    return [
        mixed[w * tokens : (w + 1) * tokens].reshape(WIN, WIN, channels)
        for w in range(len(windows))
    ]


def finish(begun, mixed, mlp_gain, up_ref, down_ref, decode_ref):
    residual = jnp.concatenate([a.reshape(CELLS, -1) + b.reshape(CELLS, -1) for a, b in zip(begun, mixed)])
    normed = normalize(residual, mlp_gain).astype(jnp.bfloat16)
    latent = residual
    units = up_ref.shape[1]
    step = min(units, 256)
    for at in range(0, units, step):
        span = slice(at, at + step)
        hidden = jax.nn.gelu(jnp.dot(normed, up_ref[:, span], preferred_element_type=jnp.float32))
        latent = latent + jnp.dot(
            hidden.astype(jnp.bfloat16), down_ref[span, :], preferred_element_type=jnp.float32
        )
    rounded = latent.astype(jnp.bfloat16)
    turned = [
        lax.dot_general(
            decode_ref[...],
            rounded[i * CELLS : i * CELLS + LANES],
            NT,
            preferred_element_type=jnp.float32,
        ).astype(jnp.bfloat16)
        for i in range(0, len(begun), 2)
    ]
    return latent, turned


def patch_order(patch_rows, patch_cols):
    every = [(r, c) for r in range(patch_rows) for c in range(patch_cols)]
    middle = [(r, c) for r, c in every if 0 < c < patch_cols - 1]
    return middle, [at for at in every if at not in middle]


def edge_side(top, row, lat_cells):
    return lambda r: (top + row + r >= 0).astype(jnp.int32) + (
        top + row + r >= lat_cells
    ).astype(jnp.int32)


def inner_block(
    start_ref, norm_ref, qkv_ref, out_ref, mixed_ref, cells_ref, turned_ref, key_ref, pack_ref,
    att_ref, score_ref, prob_ref,
):
    tile_rows, tile_cols, _ = cells_ref.shape
    margin = WIN // 2
    cells_ref[...] = start_ref[...].astype(jnp.float32)
    turn_weights(qkv_ref, turned_ref)
    for row in range(0, tile_rows - WIN, WIN):
        cols = range(0, tile_cols - WIN, WIN)
        mixed = attend(
            cells_ref, [(row + margin, col + margin) for col in cols], [], norm_ref[...],
            qkv_ref, out_ref, turned_ref, key_ref, pack_ref, att_ref, score_ref, prob_ref,
        )
        for col, block in zip(cols, mixed):
            mixed_ref[row : row + WIN, col : col + WIN, :] = block


def tall_block(
    lat_cells, tall_ref, inner_mixed_ref, norm_ref, qkv_ref, out_ref, mlp_ref, up_ref, down_ref,
    decode_ref, latent_ref, proj_ref, mixed_ref, cells_ref, turned_ref, key_ref, pack_ref,
    att_ref, score_ref, prob_ref,
):
    rows, tile_cols, channels = tall_ref.shape
    margin = WIN // 2
    tile_rows = rows - 2 * margin
    feat_width = decode_ref.shape[0]
    last = rows - WIN
    top = lax.axis_index("lat") * tile_rows - margin
    turn_weights(qkv_ref, turned_ref)
    cells_ref[...] = tall_ref[...].astype(jnp.float32)
    cols = range(0, tile_cols - WIN, WIN)
    for i, row in enumerate((0, last)):
        mixed = attend(
            cells_ref, [(row, col + margin) for col in cols],
            [edge_side(top, row, lat_cells)] * -(-len(cols) // 2), norm_ref[...], qkv_ref,
            out_ref, turned_ref, key_ref, pack_ref, att_ref, score_ref, prob_ref,
        )
        for col, block in zip(cols, mixed):
            mixed_ref[i * WIN : (i + 1) * WIN, col : col + WIN, :] = block
    here = range(1, tile_cols // PATCH - 1)
    done = 0
    for pr in range(tile_rows // PATCH):
        row = pr * PATCH + margin
        begun, mixed = [], []
        for c in here:
            span = slice(c * PATCH - margin, (c + 1) * PATCH - margin)
            begun.append(cells_ref[row : row + PATCH, c * PATCH : (c + 1) * PATCH, :])
            if pr == 0:
                halves = [mixed_ref[margin:WIN, span, :], inner_mixed_ref[:margin, span, :]]
            elif row == last - margin:
                halves = [
                    inner_mixed_ref[tile_rows - WIN - margin :, span, :],
                    mixed_ref[WIN : WIN + margin, span, :],
                ]
            else:
                halves = [inner_mixed_ref[row - WIN : row - WIN + PATCH, span, :]]
            mixed.append(jnp.concatenate(halves, axis=0))
        latent, turned = finish(begun, mixed, mlp_ref[...], up_ref, down_ref, decode_ref)
        placed = latent.reshape(len(here), PATCH, PATCH, channels).transpose(1, 0, 2, 3)
        latent_ref[pr * PATCH : (pr + 1) * PATCH] = placed.reshape(
            PATCH, len(here) * PATCH, channels
        ).astype(jnp.bfloat16)
        for pair in turned:
            proj_ref[done : done + feat_width, :] = pair
            done += feat_width


def outer_block(
    lat_cells, ext_ref, inner_mixed_ref, tall_latent_ref, tall_proj_ref, tall_mixed_ref, norm_ref, qkv_ref, out_ref, mlp_ref, up_ref, down_ref,
    decode_ref, latent_ref, proj_ref, mixed_ref, turned_ref, key_ref, pack_ref, att_ref,
    score_ref, prob_ref,
):
    ext_rows, ext_cols, channels = ext_ref.shape
    tile_rows, tile_cols, _ = latent_ref.shape
    margin = WIN // 2
    feat_width = decode_ref.shape[0]
    last_row, last_col = ext_rows - WIN, ext_cols - WIN
    top = lax.axis_index("lat") * tile_rows - margin
    turn_weights(qkv_ref, turned_ref)
    mixed_ref[WIN:last_row, WIN:last_col, :] = inner_mixed_ref[...]
    mixed_ref[:WIN, WIN:last_col, :] = tall_mixed_ref[:WIN]
    mixed_ref[last_row:, WIN:last_col, :] = tall_mixed_ref[WIN:]
    windows = [(row, col) for row in range(0, ext_rows, WIN) for col in (0, last_col)]
    sides = [
        edge_side(top, row, lat_cells) if row in (0, last_row) else None
        for row in range(0, ext_rows, WIN)
    ]
    mixed = attend(
        ext_ref, windows, sides, norm_ref[...], qkv_ref, out_ref, turned_ref, key_ref, pack_ref,
        att_ref, score_ref, prob_ref,
    )
    for (row, col), block in zip(windows, mixed):
        mixed_ref[row : row + WIN, col : col + WIN, :] = block
    done = tall_proj_ref.shape[0]
    proj_ref[:done, :] = tall_proj_ref[...]
    patch_rows = tile_rows // PATCH
    _, here = patch_order(patch_rows, tile_cols // PATCH)
    at = [
        (
            slice(r * PATCH + margin, (r + 1) * PATCH + margin),
            slice(c * PATCH + margin, (c + 1) * PATCH + margin),
        )
        for r, c in here
    ]
    latent, turned = finish(
        [ext_ref[r, c, :] for r, c in at],
        [mixed_ref[r, c, :] for r, c in at],
        mlp_ref[...], up_ref, down_ref, decode_ref,
    )
    for pair in turned:
        proj_ref[done : done + feat_width, :] = pair
        done += feat_width
    latent = latent.reshape(len(here), PATCH, PATCH, channels)
    for pr in range(patch_rows):
        left, right = [latent[i] for i, (r, _) in enumerate(here) if r == pr]
        middle = tall_latent_ref[pr * PATCH : (pr + 1) * PATCH]
        whole = jnp.concatenate([left, middle.astype(jnp.float32), right], axis=1)
        latent_ref[pr * PATCH : (pr + 1) * PATCH] = whole.astype(jnp.bfloat16)


def reply_patches(capacity, plane, tiles, order, feat_width, id_ref, *refs):
    tile_refs, out_ref, both_ref = refs[:tiles], refs[tiles], refs[tiles + 1]
    pairs = capacity // 2
    first = lax.broadcasted_iota(jnp.int32, (feat_width, LANES), 1) < CELLS
    for t in range(tiles):
        for i in range(0, len(order), 2):
            at = i // 2 * feat_width
            pair = tile_refs[t][at : at + feat_width, :].astype(jnp.float32)
            swapped = pltpu.roll(pair, CELLS, 1)
            both_ref[t, order[i]] = jnp.where(first, pair, swapped)
            both_ref[t, order[i + 1]] = jnp.where(first, swapped, pair)
    for r in range(plane):
        for t in range(tiles):
            for k in range(pairs):
                slot = (r * tiles + t) * capacity + 2 * k
                pair = jnp.where(
                    first, both_ref[t, id_ref[slot]], both_ref[t, id_ref[slot + 1]]
                )
                at = ((r * tiles + t) * pairs + k) * feat_width
                out_ref[at : at + feat_width, :] = pair.astype(jnp.bfloat16)


def decode_blocks(slot_ref, offset_ref, near_ref, far_ref, out_hbm, back_ref, out_ref, sems):
    feat_width, count = out_ref.shape
    blocks = count // BLK
    step = sems.shape[0]
    size = blocks // step
    back_ref[: near_ref.shape[0], :] = near_ref[...]
    back_ref[near_ref.shape[0] :, :] = far_ref[...]

    def one(b):
        slot = slot_ref[b]
        span = slice(b * BLK, (b + 1) * BLK)
        weights = block_weights(offset_ref[:, span].astype(jnp.float32))
        total = jnp.sum(weights.astype(jnp.float32), axis=0, keepdims=True)
        nothing = jnp.zeros_like(weights)
        low = lax.rem(slot, 2) == 0
        both = jnp.concatenate(
            [jnp.where(low, weights, nothing), jnp.where(low, nothing, weights)], axis=0
        )
        row = pl.multiple_of(lax.div(slot, 2) * feat_width, 16)
        values = back_ref[pl.ds(row, feat_width), :]
        mean = jnp.dot(values, both, preferred_element_type=jnp.float32) * (1.0 / total)
        out_ref[:, span] = mean.astype(jnp.bfloat16)

    copies = []
    for i in range(step):
        for b in range(i * size, (i + 1) * size):
            one(b)
        span = pl.ds(i * size * BLK, size * BLK)
        copies.append(pltpu.make_async_copy(out_ref.at[:, span], out_hbm.at[:, span], sems.at[i]))
        copies[i].start()
    for copy in copies:
        copy.wait()


def with_halo(array, axis, dim, width):
    size, length = (axis_count(axis), array.shape[dim])
    up = [(i, (i + 1) % size) for i in range(size)]
    down = [(j, i) for i, j in up]
    last = lax.slice_in_dim(array, length - width, length, axis=dim)
    initial = lax.slice_in_dim(array, 0, width, axis=dim)
    before = lax.ppermute(last, axis, up)
    after = lax.ppermute(initial, axis, down)
    return jnp.concatenate([before, array, after], axis=dim)


def axis_count(axes):
    axes = axes if isinstance(axes, tuple) else (axes,)
    return math.prod([lax.axis_size(axis) for axis in axes])


def swap_in_plane(array):
    plane = axis_count(("lat", "x"))
    parts = array.reshape(plane, -1, LANES)
    parts = lax.all_to_all(parts, ("lat", "x"), split_axis=0, concat_axis=0, tiled=True)
    return parts.reshape(array.shape)


def swap_at_once(gains, array):
    def apart(array):
        lat, width = lax.axis_size("lat"), lax.axis_size("x")
        parts = array.reshape(lat, width, -1, LANES)
        for dim, axis in enumerate(("lat", "x")):
            parts = lax.all_to_all(parts, axis, split_axis=dim, concat_axis=dim, tiled=True)
        return parts.reshape(array.shape)

    return lax.cond(gains[0] > 0.0, swap_in_plane, apart, array)


def swap_planes(array, hop):
    depth = lax.axis_size("z")
    return lax.ppermute(array, "z", [(i, i ^ hop) for i in range(depth)])


def local(
    obs_feat,
    obs_offset,
    block_tile,
    block_patch,
    embed_weight,
    grid_base,
    norm_gain,
    qkv_weight,
    out_weight,
    mlp_gain,
    up_weight,
    down_weight,
    decode_weight,
):
    lat, depth, width = (lax.axis_size(axis) for axis in ("lat", "z", "x"))
    plane, hops = lat * width, depth - 1
    devices = plane * depth
    feat_width, obs_count = obs_feat.shape
    blocks = obs_count // BLK
    capacity = max(2, 2 * blocks // devices)
    capacity += capacity % 2
    pairs = capacity // 2
    tile_rows, tile_cols, channels = grid_base.shape
    patch_total = (tile_rows // PATCH) * (tile_cols // PATCH)
    chunk = pairs * feat_width + meta_rows(pairs)
    dense = dense_rows(patch_total // 2, feat_width)
    steps = 3 if blocks % 3 == 0 else 1
    send_near, send_far, slots = pl.pallas_call(
        lambda *refs: encode_blocks(capacity, (lat, depth, width), *refs),
        out_shape=(
            jax.ShapeDtypeStruct((plane * chunk, LANES), jnp.bfloat16),
            jax.ShapeDtypeStruct((plane * hops * chunk, LANES), jnp.bfloat16),
            jax.ShapeDtypeStruct((blocks,), jnp.int32),
        ),
        in_specs=[pl.BlockSpec(memory_space=pltpu.HBM)] * 4,
        out_specs=(vmem(), vmem(), smem()),
        scratch_shapes=[
            pltpu.VMEM((devices * chunk, LANES), jnp.bfloat16),
            pltpu.SMEM((blocks,), jnp.int32),
            pltpu.SMEM((blocks,), jnp.int32),
            pltpu.VMEM(obs_feat.shape, jnp.bfloat16),
            pltpu.VMEM(obs_offset.shape, jnp.bfloat16),
            pltpu.SMEM((devices,), jnp.int32),
            pltpu.SemaphoreType.DMA((steps + 3,)),
        ],
        compiler_params=params(61),
        name="encode_blocks",
    )(block_tile.reshape(blocks), block_patch, obs_feat, obs_offset)

    def ids_of(recv, tiles):
        at = pairs * feat_width + 2 * pairs
        tags = recv.reshape(plane * tiles, chunk, LANES)[:, at : at + pairs, 0::CELLS]
        ids = tags.astype(jnp.float32).astype(jnp.int32) - 1
        return jnp.clip(ids, 0, patch_total - 1).reshape(-1)

    far = swap_in_plane(send_far)
    far_ids = ids_of(far, hops)
    sums = pl.pallas_call(
        lambda *refs: gather_planes(capacity, plane, hops, feat_width, *refs),
        out_shape=[jax.ShapeDtypeStruct((dense, LANES), jnp.bfloat16)] * hops,
        in_specs=[smem(), vmem()],
        out_specs=[vmem()] * hops,
        scratch_shapes=[pltpu.VMEM((patch_total, feat_width + 8, LANES), jnp.float32)] * (2 * hops),
        compiler_params=params(14),
        name="gather_planes",
    )(far_ids, far)
    parts = [swap_planes(sums[hop - 1], hop) for hop in range(1, depth)]
    send_near, _ = lax.optimization_barrier((send_near, sums))
    near = swap_at_once(norm_gain, send_near)
    near_ids = ids_of(near, 1)
    own = pl.pallas_call(
        lambda *refs: gather_own(capacity, plane, feat_width, *refs),
        out_shape=jax.ShapeDtypeStruct((patch_total // 2, feat_width + 8, LANES), jnp.float32),
        in_specs=[smem()] + [vmem()] * 3,
        out_specs=vmem(),
        scratch_shapes=[pltpu.VMEM((patch_total, feat_width + 8, LANES), jnp.float32)] * 2,
        compiler_params=params(10),
        cost_estimate=pl.CostEstimate(flops=10**9, bytes_accessed=10**7, transcendentals=0),
        name="gather_own",
    )(near_ids, near, qkv_weight, out_weight)

    start = pl.pallas_call(
        lambda *refs: start_tile(hops, *refs),
        out_shape=jax.ShapeDtypeStruct(grid_base.shape, jnp.bfloat16),
        in_specs=[vmem()] * (hops + 3),
        out_specs=vmem(),
        compiler_params=params(10),
        name="start_tile",
    )(own, *parts, embed_weight, grid_base)

    margin = WIN // 2
    ext_rows, ext_cols = tile_rows + 2 * margin, tile_cols + 2 * margin
    tall = with_halo(start, "lat", 0, margin)
    group = 128
    gains = (norm_gain.reshape(1, channels), mlp_gain.reshape(1, channels))
    weights = (gains[0], qkv_weight, out_weight, gains[1], up_weight, down_weight, decode_weight.T)
    patch_rows, patch_cols = tile_rows // PATCH, tile_cols // PATCH
    middle, sides = patch_order(patch_rows, patch_cols)
    order = [r * patch_cols + c for r, c in middle + sides]
    inner_mixed = (tile_rows - WIN, tile_cols - WIN, channels)

    def scratch(windows):
        count = -(-windows // 2)
        parts = count * channels // group
        lanes = group // HEAD_DIM * LANES
        return [
            pltpu.VMEM((2 * channels, channels), jnp.bfloat16),
            pltpu.VMEM((count * LANES, channels), jnp.bfloat16),
            pltpu.VMEM((2 * channels, count * LANES), jnp.bfloat16),
            pltpu.VMEM((channels, count * LANES), jnp.bfloat16),
            pltpu.VMEM((parts, WIN * WIN, lanes), jnp.float32),
            pltpu.VMEM((parts, LANES, lanes), jnp.bfloat16),
        ]

    mixed_inner = pl.pallas_call(
        inner_block,
        out_shape=jax.ShapeDtypeStruct(inner_mixed, jnp.float32),
        in_specs=[vmem()] * 4,
        out_specs=vmem(),
        scratch_shapes=[pltpu.VMEM(grid_base.shape, jnp.float32)]
        + scratch(tile_cols // WIN - 1),
        compiler_params=params(16),
        cost_estimate=pl.CostEstimate(flops=5 * 10**9, bytes_accessed=10**7, transcendentals=0),
        name="inner_block",
    )(start, *weights[:3])
    tall, mixed_inner = lax.optimization_barrier((tall, mixed_inner))
    ext = with_halo(tall, ("z", "x"), 1, margin).astype(jnp.float32)

    latent_tall, proj_tall, mixed_tall = pl.pallas_call(
        lambda *refs: tall_block(tile_rows * lat, *refs),
        out_shape=(
            jax.ShapeDtypeStruct((tile_rows, tile_cols - 2 * PATCH, channels), jnp.bfloat16),
            jax.ShapeDtypeStruct((len(middle) // 2 * feat_width, LANES), jnp.bfloat16),
            jax.ShapeDtypeStruct((2 * WIN,) + inner_mixed[1:], jnp.float32),
        ),
        in_specs=[vmem()] * 9,
        out_specs=(vmem(), vmem(), vmem()),
        scratch_shapes=[pltpu.VMEM(tall.shape, jnp.float32)] + scratch(tile_cols // WIN - 1),
        compiler_params=params(16),
        cost_estimate=pl.CostEstimate(flops=5 * 10**9, bytes_accessed=10**7, transcendentals=0),
        name="tall_block",
    )(tall, mixed_inner, *weights)

    latent, projected = pl.pallas_call(
        lambda *refs: outer_block(tile_rows * lat, *refs),
        out_shape=(
            jax.ShapeDtypeStruct(grid_base.shape, jnp.bfloat16),
            jax.ShapeDtypeStruct((patch_total // 2 * feat_width, LANES), jnp.bfloat16),
        ),
        in_specs=[vmem()] * 12,
        out_specs=(vmem(), vmem()),
        scratch_shapes=[pltpu.VMEM((ext_rows, ext_cols, channels), jnp.float32)]
        + scratch(2 * (ext_rows // WIN)),
        compiler_params=params(20),
        cost_estimate=pl.CostEstimate(flops=5 * 10**9, bytes_accessed=10**7, transcendentals=0),
        name="outer_block",
    )(
        ext, mixed_inner, latent_tall, proj_tall, mixed_tall, *weights
    )

    def reply(ids, tiles, name):
        count = len(tiles)
        return pl.pallas_call(
            lambda *refs: reply_patches(capacity, plane, count, order, feat_width, *refs),
            out_shape=jax.ShapeDtypeStruct(
                (plane * count * pairs * feat_width, LANES), jnp.bfloat16
            ),
            in_specs=[smem()] + [vmem()] * count,
            out_specs=vmem(),
            scratch_shapes=[pltpu.VMEM((count, patch_total, feat_width, LANES), jnp.float32)],
            compiler_params=params(12),
            cost_estimate=pl.CostEstimate(flops=10**9, bytes_accessed=10**7, transcendentals=0),
            name=name,
        )(ids, *tiles)

    others = [swap_planes(projected, hop) for hop in range(1, depth)]
    near_reply = reply(near_ids, [projected], "reply_near")
    near_back = swap_at_once(norm_gain, near_reply)
    far_back = swap_in_plane(reply(far_ids, others, "reply_far"))

    obs_out = pl.pallas_call(
        decode_blocks,
        out_shape=jax.ShapeDtypeStruct((feat_width, obs_count), jnp.bfloat16),
        in_specs=[smem(), vmem()] + [vmem()] * 2,
        out_specs=pl.BlockSpec(memory_space=pltpu.HBM),
        scratch_shapes=[
            pltpu.VMEM((devices * pairs * feat_width, LANES), jnp.bfloat16),
            pltpu.VMEM((feat_width, obs_count), jnp.bfloat16),
            pltpu.SemaphoreType.DMA((steps,)),
        ],
        compiler_params=params(12),
        name="decode_blocks",
    )(slots, obs_offset, near_back, far_back)
    return (latent, obs_out)


def solution(mesh):
    lat, lon = mesh.devices.shape
    width = lat // 2 if lat % 2 == 0 and lon % (lat // 2) == 0 else 1
    split = Mesh(mesh.devices.reshape(lat, lon // width, width), ("lat", "z", "x"))
    every = ("lat", "z", "x")
    placed = (
        P(None, every),
        P(None, every),
        P(every, None),
        P(every),
        P(),
        P("lat", ("z", "x"), None),
        P(),
        P(),
        P(),
        P(),
        P(),
        P(),
        P(),
    )
    return jax.shard_map(
        local,
        mesh=split,
        in_specs=placed,
        out_specs=(P("lat", ("z", "x"), None), P(None, every)),
        check_vma=False,
    )
```

```python
import math

import jax
import jax.numpy as jnp
from jax import lax
from jax.experimental import pallas as pl
from jax.experimental.pallas import tpu as pltpu
from jax.sharding import Mesh
from jax.sharding import PartitionSpec as P

HEAD_DIM = 32
WIN = 8
PATCH = 8
BLK = 128
CELLS = PATCH * PATCH
LANES = 2 * CELLS

epsilon = 1e-05
spread_coef = 0.5

NT = (((1,), (1,)), ((), ()))
TN = (((0,), (0,)), ((), ()))


def params(mib):
    return pltpu.CompilerParams(vmem_limit_bytes=mib * 1024 * 1024)


def vmem():
    return pl.BlockSpec(memory_space=pltpu.VMEM)


def smem():
    return pl.BlockSpec(memory_space=pltpu.SMEM)


def normalize(values, gain_row):
    center = jnp.mean(values, axis=-1, keepdims=True)
    centered = values - center
    variance = jnp.mean(centered * centered, axis=-1, keepdims=True)
    return centered * lax.rsqrt(variance + epsilon) * gain_row


def block_weights(offsets):
    axis_id = lax.broadcasted_iota(jnp.int32, (PATCH, BLK), 0).astype(jnp.float32) + 0.5
    row_gap = axis_id - offsets[0:1]
    col_gap = axis_id - offsets[1:2]
    row_gap = row_gap * row_gap
    col_gap = col_gap * col_gap
    total = row_gap[:, None, :] + col_gap[None, :, :]
    return jnp.exp(-spread_coef * total).reshape(CELLS, BLK).astype(jnp.bfloat16)


def meta_rows(pairs):
    return -(-3 * pairs // 16) * 16


def encode_blocks(
    capacity, shape, tile_hbm, patch_hbm, feat_hbm, offset_hbm, near_ref, far_ref,
    slot_ref, send_ref, tile_ref, patch_ref, feat_ref, offset_ref, count_ref, sems,
):
    lat, depth, width = shape
    devices = lat * depth * width
    plane_id = lax.axis_index("z")
    feat_width = feat_ref.shape[0]
    blocks = feat_ref.shape[1] // BLK
    step = sems.shape[0] - 3
    size = blocks // step
    pairs = capacity // 2
    meta = meta_rows(pairs)
    chunk = pairs * feat_width + meta
    small = [
        pltpu.make_async_copy(tile_hbm, tile_ref, sems.at[step]),
        pltpu.make_async_copy(patch_hbm, patch_ref, sems.at[step + 1]),
        pltpu.make_async_copy(offset_hbm, offset_ref, sems.at[step + 2]),
    ]
    large = []
    for i in range(step):
        span = pl.ds(i * size * BLK, size * BLK)
        large.append(pltpu.make_async_copy(feat_hbm.at[:, span], feat_ref.at[:, span], sems.at[i]))
    for copy in small + large:
        copy.start()
    send_ref[...] = jnp.zeros_like(send_ref)

    def clear(t, _):
        count_ref[t] = 0
        return 0

    lax.fori_loop(0, devices, clear, 0)
    lane_half = lax.broadcasted_iota(jnp.int32, (feat_width, LANES), 1) // CELLS
    meta_half = lax.broadcasted_iota(jnp.int32, (meta, LANES), 1) // CELLS
    meta_row = lax.broadcasted_iota(jnp.int32, (meta, LANES), 0)
    ones = jnp.ones((16, BLK), jnp.bfloat16)

    def one(b):
        tile = tile_ref[b]
        rank = count_ref[tile]
        count_ref[tile] = rank + 1
        lon = lax.rem(tile, depth * width)
        partner = lax.div(tile, depth * width) * width + lax.rem(lon, width)
        hop = lax.div(lon, width) ^ plane_id
        piece = jnp.where(hop == 0, partner, lat * width + partner * (depth - 1) + hop - 1)
        slot_ref[b] = piece * capacity + rank
        pair = lax.div(rank, 2)
        half = lax.rem(rank, 2)
        col = pl.multiple_of(b * BLK, BLK)
        feat = jnp.concatenate([feat_ref[:, pl.ds(col, BLK)], ones], axis=0)
        weights = block_weights(offset_ref[:, pl.ds(col, BLK)].astype(jnp.float32))
        twice = jnp.concatenate([weights, weights], axis=0)
        sums = lax.dot_general(feat, twice, NT, preferred_element_type=jnp.float32)
        row = pl.multiple_of(piece * chunk + pair * feat_width, 16)
        old = send_ref[pl.ds(row, feat_width), :].astype(jnp.float32)
        send_ref[pl.ds(row, feat_width), :] = jnp.where(
            lane_half == half, sums[:feat_width], old
        ).astype(jnp.bfloat16)
        mass = sums[feat_width : feat_width + 1]
        high = mass.astype(jnp.bfloat16).astype(jnp.float32)
        low = mass - high
        tag = (patch_ref[b] + 1).astype(jnp.float32)
        row = pl.multiple_of(piece * chunk + pairs * feat_width, 16)
        old = send_ref[pl.ds(row, meta), :].astype(jnp.float32)
        new = jnp.where(
            meta_row == pair,
            high,
            jnp.where(
                meta_row == pairs + pair, low, jnp.where(meta_row == 2 * pairs + pair, tag, old)
            ),
        )
        send_ref[pl.ds(row, meta), :] = jnp.where(meta_half == half, new, old).astype(jnp.bfloat16)

    for copy in small:
        copy.wait()
    for i in range(step):
        large[i].wait()
        for b in range(i * size, (i + 1) * size):
            one(b)
    near_ref[...] = send_ref[: near_ref.shape[0]]
    far_ref[...] = send_ref[near_ref.shape[0] :]


def dense_rows(pairs, feat_width):
    return pairs * feat_width + -(-pairs // 16) * 16


def add_chunk(capacity, feat_width, id_ref, slot, recv_ref, base, low_ref, high_ref):
    pairs = capacity // 2
    tags = recv_ref[base + pairs * feat_width : base + pairs * feat_width + meta_rows(pairs), :]
    tags = tags.astype(jnp.float32)
    for k in range(pairs):
        at = base + k * feat_width
        sums = recv_ref[at : at + feat_width, :].astype(jnp.float32)
        mass = tags[k : k + 1] + tags[pairs + k : pairs + k + 1]
        both = jnp.concatenate([sums, jnp.broadcast_to(mass, (8, LANES))], axis=0)
        low_ref[id_ref[slot + 2 * k]] += both
        high_ref[id_ref[slot + 2 * k + 1]] += both


def paired(low_ref, high_ref, j):
    first = lax.broadcasted_iota(jnp.int32, low_ref.shape[1:], 1) < CELLS
    even = low_ref[2 * j] + pltpu.roll(high_ref[2 * j], CELLS, 1)
    odd = high_ref[2 * j + 1] + pltpu.roll(low_ref[2 * j + 1], CELLS, 1)
    return jnp.where(first, even, odd)


def gather_planes(capacity, plane, hops, feat_width, id_ref, recv_ref, *refs):
    outs, lows, highs = refs[:hops], refs[hops : 2 * hops], refs[2 * hops :]
    pairs = capacity // 2
    chunk = pairs * feat_width + meta_rows(pairs)
    patch_pairs = lows[0].shape[0] // 2
    for ref in lows + highs:
        ref[...] = jnp.zeros_like(ref)
    for r in range(plane):
        for hop in range(hops):
            n = r * hops + hop
            add_chunk(
                capacity, feat_width, id_ref, n * capacity, recv_ref, n * chunk, lows[hop], highs[hop]
            )
    for hop in range(hops):
        masses = []
        for j in range(patch_pairs):
            pair = paired(lows[hop], highs[hop], j)
            outs[hop][j * feat_width : (j + 1) * feat_width, :] = pair[:feat_width].astype(
                jnp.bfloat16
            )
            masses.append(pair[feat_width : feat_width + 1])
        masses = jnp.concatenate(masses, axis=0)
        spare = outs[hop].shape[0] - patch_pairs * (feat_width + 1)
        rows = [masses] + ([jnp.zeros((spare, LANES), jnp.float32)] if spare else [])
        outs[hop][patch_pairs * feat_width :, :] = jnp.concatenate(rows, axis=0).astype(jnp.bfloat16)


def gather_own(capacity, plane, feat_width, id_ref, recv_ref, *refs):
    own_ref, low_ref, high_ref = refs[-3:]
    chunk = recv_ref.shape[0] // plane
    low_ref[...] = jnp.zeros_like(low_ref)
    high_ref[...] = jnp.zeros_like(high_ref)
    for r in range(plane):
        add_chunk(
            capacity, feat_width, id_ref, r * capacity, recv_ref, r * chunk, low_ref, high_ref
        )
    for j in range(own_ref.shape[0]):
        own_ref[j] = paired(low_ref, high_ref, j)


def start_tile(hops, own_ref, *refs):
    parts = refs[:hops]
    embed_ref, base_ref, start_ref = refs[hops:]
    feat_width, channels = embed_ref.shape
    tile_rows, tile_cols, _ = base_ref.shape
    patch_rows, patch_cols = tile_rows // PATCH, tile_cols // PATCH
    patch_pairs = patch_rows * patch_cols // 2
    embed = embed_ref[...]
    mass_rows = [part[patch_pairs * feat_width :, :].astype(jnp.float32) for part in parts]
    for pr in range(patch_rows):
        lifted = []
        for pc in range(patch_cols // 2):
            j = pr * (patch_cols // 2) + pc
            pair = own_ref[j]
            sums, mass = pair[:feat_width], pair[feat_width : feat_width + 1]
            for part, rows in zip(parts, mass_rows):
                sums = sums + part[j * feat_width : (j + 1) * feat_width, :].astype(jnp.float32)
                mass = mass + rows[j : j + 1]
            encoded = (sums * (1.0 / (1.0 + mass))).astype(jnp.bfloat16)
            lifted.append(lax.dot_general(encoded, embed, TN, preferred_element_type=jnp.float32))
        lifted = jnp.concatenate(lifted, axis=0).reshape(patch_cols, PATCH, PATCH, channels)
        lifted = lifted.transpose(1, 0, 2, 3).reshape(PATCH, tile_cols, channels)
        rows = slice(pr * PATCH, (pr + 1) * PATCH)
        start_ref[rows] = (base_ref[rows].astype(jnp.float32) + lifted).astype(jnp.bfloat16)


def turn_weights(qkv_ref, turned_ref):
    channels = qkv_ref.shape[0]
    turned_ref[:channels] = qkv_ref[:, :channels].T
    turned_ref[channels:] = qkv_ref[:, 2 * channels :].T


def attend(
    cells_ref, windows, sides, norm_gain, qkv_ref, out_ref, turned_ref, key_ref, pack_ref, att_ref,
    score_ref, prob_ref,
):
    channels = qkv_ref.shape[0]
    tokens = WIN * WIN
    group = 128
    heads = group // HEAD_DIM
    count = -(-len(windows) // 2)
    size = count * LANES
    scale = HEAD_DIM ** (-0.5) / math.log(2.0)
    shape = (tokens, heads * LANES)
    own = lax.broadcasted_iota(jnp.int32, shape, 1) % LANES < tokens
    nothing = jnp.zeros(shape, jnp.bfloat16)
    empty = jnp.zeros((HEAD_DIM, LANES), jnp.bfloat16)
    cells = jnp.concatenate(
        [
            cells_ref[row : row + WIN, col : col + WIN, :].reshape(tokens, channels)
            for row, col in windows
        ],
        axis=0,
    )
    normed = normalize(cells, norm_gain).astype(jnp.bfloat16)
    if len(windows) % 2:
        normed = jnp.concatenate([normed, jnp.zeros((tokens, channels), jnp.bfloat16)], axis=0)
    key_ref[:size] = jnp.dot(
        normed, qkv_ref[:, channels : 2 * channels], preferred_element_type=jnp.float32
    ).astype(jnp.bfloat16)
    pack_ref[:, :size] = lax.dot_general(
        turned_ref[...], normed, NT, preferred_element_type=jnp.float32
    ).astype(jnp.bfloat16)
    key_row = lax.broadcasted_iota(jnp.int32, (tokens, LANES), 0) // WIN
    query_row = lax.broadcasted_iota(jnp.int32, (tokens, LANES), 1) % tokens // WIN
    bias = [None] * count
    for p, side in enumerate(sides):
        if side is not None:
            apart = jnp.where(side(key_row) == side(query_row), 0.0, -1e30)
            bias[p] = jnp.concatenate([apart] * heads, axis=1)
    parts = [(p, g) for p in range(count) for g in range(channels // group)]
    for n, (p, g) in enumerate(parts):
        span = slice(p * LANES, (p + 1) * LANES)
        at = slice(g * group, (g + 1) * group)
        query = pack_ref[at, span]
        stack = jnp.concatenate(
            [
                jnp.concatenate(
                    [
                        query[h * HEAD_DIM : (h + 1) * HEAD_DIM] if i == h else empty
                        for i in range(heads)
                    ],
                    axis=0,
                )
                for h in range(heads)
            ],
            axis=1,
        )
        scores = jnp.dot(key_ref[span, at], stack, preferred_element_type=jnp.float32)
        scores = jnp.where(own, scores[:tokens], scores[tokens:])
        score_ref[n] = scores if bias[p] is None else scores + bias[p]
    for n in range(len(parts)):
        scores = score_ref[n]
        peak = jnp.max(scores, axis=0, keepdims=True)
        raised = jnp.exp2((scores - peak) * scale)
        total = jnp.sum(raised, axis=0, keepdims=True)
        probs = (raised * (1.0 / total)).astype(jnp.bfloat16)
        prob_ref[n, :tokens] = jnp.where(own, probs, nothing)
        prob_ref[n, tokens:] = jnp.where(own, nothing, probs)
    for n, (p, g) in enumerate(parts):
        span = slice(p * LANES, (p + 1) * LANES)
        for h in range(0, heads, 2):
            at = g * group + h * HEAD_DIM
            both = jnp.dot(
                pack_ref[channels + at : channels + at + 2 * HEAD_DIM, span],
                prob_ref[n, :, h * LANES : (h + 2) * LANES],
                preferred_element_type=jnp.float32,
            ).astype(jnp.bfloat16)
            att_ref[at : at + HEAD_DIM, span] = both[:HEAD_DIM, :LANES]
            att_ref[at + HEAD_DIM : at + 2 * HEAD_DIM, span] = both[HEAD_DIM:, LANES:]
    mixed = lax.dot_general(
        att_ref[:, :size], out_ref[...], TN, preferred_element_type=jnp.float32
    )
    return [
        mixed[w * tokens : (w + 1) * tokens].reshape(WIN, WIN, channels)
        for w in range(len(windows))
    ]


def finish(begun, mixed, mlp_gain, up_ref, down_ref, decode_ref):
    residual = jnp.concatenate([a.reshape(CELLS, -1) + b.reshape(CELLS, -1) for a, b in zip(begun, mixed)])
    normed = normalize(residual, mlp_gain).astype(jnp.bfloat16)
    latent = residual
    units = up_ref.shape[1]
    step = min(units, 256)
    for at in range(0, units, step):
        span = slice(at, at + step)
        hidden = jax.nn.gelu(jnp.dot(normed, up_ref[:, span], preferred_element_type=jnp.float32))
        latent = latent + jnp.dot(
            hidden.astype(jnp.bfloat16), down_ref[span, :], preferred_element_type=jnp.float32
        )
    rounded = latent.astype(jnp.bfloat16)
    turned = [
        lax.dot_general(
            decode_ref[...],
            rounded[i * CELLS : i * CELLS + LANES],
            NT,
            preferred_element_type=jnp.float32,
        ).astype(jnp.bfloat16)
        for i in range(0, len(begun), 2)
    ]
    return latent, turned


def patch_order(patch_rows, patch_cols):
    every = [(r, c) for r in range(patch_rows) for c in range(patch_cols)]
    middle = [(r, c) for r, c in every if 0 < c < patch_cols - 1]
    return middle, [at for at in every if at not in middle]


def edge_side(top, row, lat_cells):
    return lambda r: (top + row + r >= 0).astype(jnp.int32) + (
        top + row + r >= lat_cells
    ).astype(jnp.int32)


def inner_block(
    start_ref, norm_ref, qkv_ref, out_ref, mixed_ref, cells_ref, turned_ref, key_ref, pack_ref,
    att_ref, score_ref, prob_ref,
):
    tile_rows, tile_cols, _ = cells_ref.shape
    margin = WIN // 2
    cells_ref[...] = start_ref[...].astype(jnp.float32)
    turn_weights(qkv_ref, turned_ref)
    for row in range(0, tile_rows - WIN, WIN):
        cols = range(0, tile_cols - WIN, WIN)
        mixed = attend(
            cells_ref, [(row + margin, col + margin) for col in cols], [], norm_ref[...],
            qkv_ref, out_ref, turned_ref, key_ref, pack_ref, att_ref, score_ref, prob_ref,
        )
        for col, block in zip(cols, mixed):
            mixed_ref[row : row + WIN, col : col + WIN, :] = block


def tall_block(
    lat_cells, tall_ref, inner_mixed_ref, norm_ref, qkv_ref, out_ref, mlp_ref, up_ref, down_ref,
    decode_ref, latent_ref, proj_ref, mixed_ref, cells_ref, turned_ref, key_ref, pack_ref,
    att_ref, score_ref, prob_ref,
):
    rows, tile_cols, channels = tall_ref.shape
    margin = WIN // 2
    tile_rows = rows - 2 * margin
    feat_width = decode_ref.shape[0]
    last = rows - WIN
    top = lax.axis_index("lat") * tile_rows - margin
    turn_weights(qkv_ref, turned_ref)
    cells_ref[...] = tall_ref[...].astype(jnp.float32)
    cols = range(0, tile_cols - WIN, WIN)
    for i, row in enumerate((0, last)):
        mixed = attend(
            cells_ref, [(row, col + margin) for col in cols],
            [edge_side(top, row, lat_cells)] * -(-len(cols) // 2), norm_ref[...], qkv_ref,
            out_ref, turned_ref, key_ref, pack_ref, att_ref, score_ref, prob_ref,
        )
        for col, block in zip(cols, mixed):
            mixed_ref[i * WIN : (i + 1) * WIN, col : col + WIN, :] = block
    here = range(1, tile_cols // PATCH - 1)
    done = 0
    for pr in range(tile_rows // PATCH):
        row = pr * PATCH + margin
        begun, mixed = [], []
        for c in here:
            span = slice(c * PATCH - margin, (c + 1) * PATCH - margin)
            begun.append(cells_ref[row : row + PATCH, c * PATCH : (c + 1) * PATCH, :])
            if pr == 0:
                halves = [mixed_ref[margin:WIN, span, :], inner_mixed_ref[:margin, span, :]]
            elif row == last - margin:
                halves = [
                    inner_mixed_ref[tile_rows - WIN - margin :, span, :],
                    mixed_ref[WIN : WIN + margin, span, :],
                ]
            else:
                halves = [inner_mixed_ref[row - WIN : row - WIN + PATCH, span, :]]
            mixed.append(jnp.concatenate(halves, axis=0))
        latent, turned = finish(begun, mixed, mlp_ref[...], up_ref, down_ref, decode_ref)
        placed = latent.reshape(len(here), PATCH, PATCH, channels).transpose(1, 0, 2, 3)
        latent_ref[pr * PATCH : (pr + 1) * PATCH] = placed.reshape(
            PATCH, len(here) * PATCH, channels
        ).astype(jnp.bfloat16)
        for pair in turned:
            proj_ref[done : done + feat_width, :] = pair
            done += feat_width


def outer_block(
    lat_cells, ext_ref, inner_mixed_ref, tall_latent_ref, tall_proj_ref, tall_mixed_ref, norm_ref, qkv_ref, out_ref, mlp_ref, up_ref, down_ref,
    decode_ref, latent_ref, proj_ref, mixed_ref, turned_ref, key_ref, pack_ref, att_ref,
    score_ref, prob_ref,
):
    ext_rows, ext_cols, channels = ext_ref.shape
    tile_rows, tile_cols, _ = latent_ref.shape
    margin = WIN // 2
    feat_width = decode_ref.shape[0]
    last_row, last_col = ext_rows - WIN, ext_cols - WIN
    top = lax.axis_index("lat") * tile_rows - margin
    turn_weights(qkv_ref, turned_ref)
    mixed_ref[WIN:last_row, WIN:last_col, :] = inner_mixed_ref[...]
    mixed_ref[:WIN, WIN:last_col, :] = tall_mixed_ref[:WIN]
    mixed_ref[last_row:, WIN:last_col, :] = tall_mixed_ref[WIN:]
    windows = [(row, col) for row in range(0, ext_rows, WIN) for col in (0, last_col)]
    sides = [
        edge_side(top, row, lat_cells) if row in (0, last_row) else None
        for row in range(0, ext_rows, WIN)
    ]
    mixed = attend(
        ext_ref, windows, sides, norm_ref[...], qkv_ref, out_ref, turned_ref, key_ref, pack_ref,
        att_ref, score_ref, prob_ref,
    )
    for (row, col), block in zip(windows, mixed):
        mixed_ref[row : row + WIN, col : col + WIN, :] = block
    done = tall_proj_ref.shape[0]
    proj_ref[:done, :] = tall_proj_ref[...]
    patch_rows = tile_rows // PATCH
    _, here = patch_order(patch_rows, tile_cols // PATCH)
    at = [
        (
            slice(r * PATCH + margin, (r + 1) * PATCH + margin),
            slice(c * PATCH + margin, (c + 1) * PATCH + margin),
        )
        for r, c in here
    ]
    latent, turned = finish(
        [ext_ref[r, c, :] for r, c in at],
        [mixed_ref[r, c, :] for r, c in at],
        mlp_ref[...], up_ref, down_ref, decode_ref,
    )
    for pair in turned:
        proj_ref[done : done + feat_width, :] = pair
        done += feat_width
    latent = latent.reshape(len(here), PATCH, PATCH, channels)
    for pr in range(patch_rows):
        left, right = [latent[i] for i, (r, _) in enumerate(here) if r == pr]
        middle = tall_latent_ref[pr * PATCH : (pr + 1) * PATCH]
        whole = jnp.concatenate([left, middle.astype(jnp.float32), right], axis=1)
        latent_ref[pr * PATCH : (pr + 1) * PATCH] = whole.astype(jnp.bfloat16)


def reply_patches(capacity, plane, tiles, order, feat_width, id_ref, *refs):
    tile_refs, out_ref, both_ref = refs[:tiles], refs[tiles], refs[tiles + 1]
    pairs = capacity // 2
    first = lax.broadcasted_iota(jnp.int32, (feat_width, LANES), 1) < CELLS
    for t in range(tiles):
        for i in range(0, len(order), 2):
            at = i // 2 * feat_width
            pair = tile_refs[t][at : at + feat_width, :].astype(jnp.float32)
            swapped = pltpu.roll(pair, CELLS, 1)
            both_ref[t, order[i]] = jnp.where(first, pair, swapped)
            both_ref[t, order[i + 1]] = jnp.where(first, swapped, pair)
    for r in range(plane):
        for t in range(tiles):
            for k in range(pairs):
                slot = (r * tiles + t) * capacity + 2 * k
                pair = jnp.where(
                    first, both_ref[t, id_ref[slot]], both_ref[t, id_ref[slot + 1]]
                )
                at = ((r * tiles + t) * pairs + k) * feat_width
                out_ref[at : at + feat_width, :] = pair.astype(jnp.bfloat16)


def decode_blocks(slot_ref, offset_ref, near_ref, far_ref, out_hbm, back_ref, out_ref, sems):
    feat_width, count = out_ref.shape
    blocks = count // BLK
    step = sems.shape[0]
    size = blocks // step
    back_ref[: near_ref.shape[0], :] = near_ref[...]
    back_ref[near_ref.shape[0] :, :] = far_ref[...]

    def one(b):
        slot = slot_ref[b]
        span = slice(b * BLK, (b + 1) * BLK)
        weights = block_weights(offset_ref[:, span].astype(jnp.float32))
        total = jnp.sum(weights.astype(jnp.float32), axis=0, keepdims=True)
        nothing = jnp.zeros_like(weights)
        low = lax.rem(slot, 2) == 0
        both = jnp.concatenate(
            [jnp.where(low, weights, nothing), jnp.where(low, nothing, weights)], axis=0
        )
        row = pl.multiple_of(lax.div(slot, 2) * feat_width, 16)
        values = back_ref[pl.ds(row, feat_width), :]
        mean = jnp.dot(values, both, preferred_element_type=jnp.float32) * (1.0 / total)
        out_ref[:, span] = mean.astype(jnp.bfloat16)

    copies = []
    for i in range(step):
        for b in range(i * size, (i + 1) * size):
            one(b)
        span = pl.ds(i * size * BLK, size * BLK)
        copies.append(pltpu.make_async_copy(out_ref.at[:, span], out_hbm.at[:, span], sems.at[i]))
        copies[i].start()
    for copy in copies:
        copy.wait()


def with_halo(array, axis, dim, width):
    size, length = (axis_count(axis), array.shape[dim])
    up = [(i, (i + 1) % size) for i in range(size)]
    down = [(j, i) for i, j in up]
    last = lax.slice_in_dim(array, length - width, length, axis=dim)
    initial = lax.slice_in_dim(array, 0, width, axis=dim)
    before = lax.ppermute(last, axis, up)
    after = lax.ppermute(initial, axis, down)
    return jnp.concatenate([before, array, after], axis=dim)


def axis_count(axes):
    axes = axes if isinstance(axes, tuple) else (axes,)
    return math.prod([lax.axis_size(axis) for axis in axes])


def swap_in_plane(array):
    plane = axis_count(("lat", "x"))
    parts = array.reshape(plane, -1, LANES)
    parts = lax.all_to_all(parts, ("lat", "x"), split_axis=0, concat_axis=0, tiled=True)
    return parts.reshape(array.shape)


def swap_at_once(gains, array):
    def apart(array):
        lat, width = lax.axis_size("lat"), lax.axis_size("x")
        parts = array.reshape(lat, width, -1, LANES)
        for dim, axis in enumerate(("lat", "x")):
            parts = lax.all_to_all(parts, axis, split_axis=dim, concat_axis=dim, tiled=True)
        return parts.reshape(array.shape)

    return lax.cond(gains[0] > 0.0, swap_in_plane, apart, array)


def swap_planes(array, hop):
    depth = lax.axis_size("z")
    return lax.ppermute(array, "z", [(i, i ^ hop) for i in range(depth)])


def local(
    obs_feat,
    obs_offset,
    block_tile,
    block_patch,
    embed_weight,
    grid_base,
    norm_gain,
    qkv_weight,
    out_weight,
    mlp_gain,
    up_weight,
    down_weight,
    decode_weight,
):
    lat, depth, width = (lax.axis_size(axis) for axis in ("lat", "z", "x"))
    plane, hops = lat * width, depth - 1
    devices = plane * depth
    feat_width, obs_count = obs_feat.shape
    blocks = obs_count // BLK
    capacity = max(2, 2 * blocks // devices)
    capacity += capacity % 2
    pairs = capacity // 2
    tile_rows, tile_cols, channels = grid_base.shape
    patch_total = (tile_rows // PATCH) * (tile_cols // PATCH)
    chunk = pairs * feat_width + meta_rows(pairs)
    dense = dense_rows(patch_total // 2, feat_width)
    steps = 3 if blocks % 3 == 0 else 1
    send_near, send_far, slots = pl.pallas_call(
        lambda *refs: encode_blocks(capacity, (lat, depth, width), *refs),
        out_shape=(
            jax.ShapeDtypeStruct((plane * chunk, LANES), jnp.bfloat16),
            jax.ShapeDtypeStruct((plane * hops * chunk, LANES), jnp.bfloat16),
            jax.ShapeDtypeStruct((blocks,), jnp.int32),
        ),
        in_specs=[pl.BlockSpec(memory_space=pltpu.HBM)] * 4,
        out_specs=(vmem(), vmem(), smem()),
        scratch_shapes=[
            pltpu.VMEM((devices * chunk, LANES), jnp.bfloat16),
            pltpu.SMEM((blocks,), jnp.int32),
            pltpu.SMEM((blocks,), jnp.int32),
            pltpu.VMEM(obs_feat.shape, jnp.bfloat16),
            pltpu.VMEM(obs_offset.shape, jnp.bfloat16),
            pltpu.SMEM((devices,), jnp.int32),
            pltpu.SemaphoreType.DMA((steps + 3,)),
        ],
        compiler_params=params(61),
        name="encode_blocks",
    )(block_tile.reshape(blocks), block_patch, obs_feat, obs_offset)

    def ids_of(recv, tiles):
        at = pairs * feat_width + 2 * pairs
        tags = recv.reshape(plane * tiles, chunk, LANES)[:, at : at + pairs, 0::CELLS]
        ids = tags.astype(jnp.float32).astype(jnp.int32) - 1
        return jnp.clip(ids, 0, patch_total - 1).reshape(-1)

    far = swap_in_plane(send_far)
    far_ids = ids_of(far, hops)
    sums = pl.pallas_call(
        lambda *refs: gather_planes(capacity, plane, hops, feat_width, *refs),
        out_shape=[jax.ShapeDtypeStruct((dense, LANES), jnp.bfloat16)] * hops,
        in_specs=[smem(), vmem()],
        out_specs=[vmem()] * hops,
        scratch_shapes=[pltpu.VMEM((patch_total, feat_width + 8, LANES), jnp.float32)] * (2 * hops),
        compiler_params=params(14),
        name="gather_planes",
    )(far_ids, far)
    parts = [swap_planes(sums[hop - 1], hop) for hop in range(1, depth)]
    send_near, _ = lax.optimization_barrier((send_near, sums))
    near = swap_at_once(norm_gain, send_near)
    near_ids = ids_of(near, 1)
    own = pl.pallas_call(
        lambda *refs: gather_own(capacity, plane, feat_width, *refs),
        out_shape=jax.ShapeDtypeStruct((patch_total // 2, feat_width + 8, LANES), jnp.float32),
        in_specs=[smem()] + [vmem()] * 3,
        out_specs=vmem(),
        scratch_shapes=[pltpu.VMEM((patch_total, feat_width + 8, LANES), jnp.float32)] * 2,
        compiler_params=params(10),
        cost_estimate=pl.CostEstimate(flops=10**9, bytes_accessed=10**7, transcendentals=0),
        name="gather_own",
    )(near_ids, near, qkv_weight, out_weight)

    start = pl.pallas_call(
        lambda *refs: start_tile(hops, *refs),
        out_shape=jax.ShapeDtypeStruct(grid_base.shape, jnp.bfloat16),
        in_specs=[vmem()] * (hops + 3),
        out_specs=vmem(),
        compiler_params=params(10),
        name="start_tile",
    )(own, *parts, embed_weight, grid_base)

    margin = WIN // 2
    ext_rows, ext_cols = tile_rows + 2 * margin, tile_cols + 2 * margin
    tall = with_halo(start, "lat", 0, margin)
    group = 128
    gains = (norm_gain.reshape(1, channels), mlp_gain.reshape(1, channels))
    weights = (gains[0], qkv_weight, out_weight, gains[1], up_weight, down_weight, decode_weight.T)
    patch_rows, patch_cols = tile_rows // PATCH, tile_cols // PATCH
    middle, sides = patch_order(patch_rows, patch_cols)
    order = [r * patch_cols + c for r, c in middle + sides]
    inner_mixed = (tile_rows - WIN, tile_cols - WIN, channels)

    def scratch(windows):
        count = -(-windows // 2)
        parts = count * channels // group
        lanes = group // HEAD_DIM * LANES
        return [
            pltpu.VMEM((2 * channels, channels), jnp.bfloat16),
            pltpu.VMEM((count * LANES, channels), jnp.bfloat16),
            pltpu.VMEM((2 * channels, count * LANES), jnp.bfloat16),
            pltpu.VMEM((channels, count * LANES), jnp.bfloat16),
            pltpu.VMEM((parts, WIN * WIN, lanes), jnp.float32),
            pltpu.VMEM((parts, LANES, lanes), jnp.bfloat16),
        ]

    mixed_inner = pl.pallas_call(
        inner_block,
        out_shape=jax.ShapeDtypeStruct(inner_mixed, jnp.float32),
        in_specs=[vmem()] * 4,
        out_specs=vmem(),
        scratch_shapes=[pltpu.VMEM(grid_base.shape, jnp.float32)]
        + scratch(tile_cols // WIN - 1),
        compiler_params=params(16),
        cost_estimate=pl.CostEstimate(flops=5 * 10**9, bytes_accessed=10**7, transcendentals=0),
        name="inner_block",
    )(start, *weights[:3])
    tall, mixed_inner = lax.optimization_barrier((tall, mixed_inner))
    ext = with_halo(tall, ("z", "x"), 1, margin).astype(jnp.float32)

    latent_tall, proj_tall, mixed_tall = pl.pallas_call(
        lambda *refs: tall_block(tile_rows * lat, *refs),
        out_shape=(
            jax.ShapeDtypeStruct((tile_rows, tile_cols - 2 * PATCH, channels), jnp.bfloat16),
            jax.ShapeDtypeStruct((len(middle) // 2 * feat_width, LANES), jnp.bfloat16),
            jax.ShapeDtypeStruct((2 * WIN,) + inner_mixed[1:], jnp.float32),
        ),
        in_specs=[vmem()] * 9,
        out_specs=(vmem(), vmem(), vmem()),
        scratch_shapes=[pltpu.VMEM(tall.shape, jnp.float32)] + scratch(tile_cols // WIN - 1),
        compiler_params=params(16),
        cost_estimate=pl.CostEstimate(flops=5 * 10**9, bytes_accessed=10**7, transcendentals=0),
        name="tall_block",
    )(tall, mixed_inner, *weights)

    latent, projected = pl.pallas_call(
        lambda *refs: outer_block(tile_rows * lat, *refs),
        out_shape=(
            jax.ShapeDtypeStruct(grid_base.shape, jnp.bfloat16),
            jax.ShapeDtypeStruct((patch_total // 2 * feat_width, LANES), jnp.bfloat16),
        ),
        in_specs=[vmem()] * 12,
        out_specs=(vmem(), vmem()),
        scratch_shapes=[pltpu.VMEM((ext_rows, ext_cols, channels), jnp.float32)]
        + scratch(2 * (ext_rows // WIN)),
        compiler_params=params(20),
        cost_estimate=pl.CostEstimate(flops=5 * 10**9, bytes_accessed=10**7, transcendentals=0),
        name="outer_block",
    )(
        ext, mixed_inner, latent_tall, proj_tall, mixed_tall, *weights
    )

    def reply(ids, tiles, name):
        count = len(tiles)
        return pl.pallas_call(
            lambda *refs: reply_patches(capacity, plane, count, order, feat_width, *refs),
            out_shape=jax.ShapeDtypeStruct(
                (plane * count * pairs * feat_width, LANES), jnp.bfloat16
            ),
            in_specs=[smem()] + [vmem()] * count,
            out_specs=vmem(),
            scratch_shapes=[pltpu.VMEM((count, patch_total, feat_width, LANES), jnp.float32)],
            compiler_params=params(12),
            cost_estimate=pl.CostEstimate(flops=10**9, bytes_accessed=10**7, transcendentals=0),
            name=name,
        )(ids, *tiles)

    others = [swap_planes(projected, hop) for hop in range(1, depth)]
    near_reply = reply(near_ids, [projected], "reply_near")
    near_back = swap_at_once(norm_gain, near_reply)
    far_back = swap_in_plane(reply(far_ids, others, "reply_far"))

    obs_out = pl.pallas_call(
        decode_blocks,
        out_shape=jax.ShapeDtypeStruct((feat_width, obs_count), jnp.bfloat16),
        in_specs=[smem(), vmem()] + [vmem()] * 2,
        out_specs=pl.BlockSpec(memory_space=pltpu.HBM),
        scratch_shapes=[
            pltpu.VMEM((devices * pairs * feat_width, LANES), jnp.bfloat16),
            pltpu.VMEM((feat_width, obs_count), jnp.bfloat16),
            pltpu.SemaphoreType.DMA((steps,)),
        ],
        compiler_params=params(12),
        name="decode_blocks",
    )(slots, obs_offset, near_back, far_back)
    return (latent, obs_out)


def solution(mesh):
    lat, lon = mesh.devices.shape
    width = lat // 2 if lat % 2 == 0 and lon % (lat // 2) == 0 else 1
    split = Mesh(mesh.devices.reshape(lat, lon // width, width), ("lat", "z", "x"))
    every = ("lat", "z", "x")
    placed = (
        P(None, every),
        P(None, every),
        P(every, None),
        P(every),
        P(),
        P("lat", ("z", "x"), None),
        P(),
        P(),
        P(),
        P(),
        P(),
        P(),
        P(),
    )
    return jax.shard_map(
        local,
        mesh=split,
        in_specs=placed,
        out_specs=(P("lat", ("z", "x"), None), P(None, every)),
        check_vma=False,
    )
```
